32 devices in a mesh: rep: 2 (over x), seq: 16 (over z, y, core).
Axes of the slice: x: 2, y: 2, z: 4, core: 2. Of those that a mesh axis runs over, the one named last changes fastest.
Arguments:
- q_stream: bfloat16 [4096, 8192], P(('rep', 'seq')), parts along dimension 0, may hold values from -6 to 6
- k_stream: bfloat16 [4096, 8192], P(('rep', 'seq')), parts along dimension 0, may hold values from -6 to 6
- v_stream: bfloat16 [4096, 8192], P(('rep', 'seq')), parts along dimension 0, may hold values from -6 to 6
- feat_filter: float32 [3, 3, 8192], replicated, may hold values from -3.5 to 3.5
- long_filter: bfloat16 [512, 128], replicated, may hold values from -0.5 to 0.5
- skip_gain: float32 [8192], replicated, may hold values from -3 to 3
Outputs:
- mixed: bfloat16 [4096, 8192], P(('rep', 'seq')), parts along dimension 0
The draws below stay inside these ranges and needn't reach their ends.
There are 2 independent parts, one for each index of `rep`. The reference program is written for one: setup_inputs(seed, part) draws one part's arguments, and reference() takes and returns one part's arrays. A program takes and returns all parts, laid end to end along the dimension named above; an argument that names none is the same for every part. Nothing has to cross between parts.
All inputs are finite; a program needn't handle non-finite values.
Results may differ from the reference program's by a relative error of at most 0.005.
Values may be sent and summed in bfloat16 or wider, within the bound.
No kernel may reach another device: no remote copies, remote signals or barrier semaphores. Data moves between devices by JAX's collectives and lax.ppermute only.
A program may use at most 128 MiB of HBM per device.

```python
import math
import jax
import jax.numpy as jnp
from jax import lax

D = 8192
GROUP_CH = 16
FILT = 128
FEAT = 3
GROUPS = 512
SEQ_LEN = 2048


def shard_levels(own_key, extent, cuts, least, high):
    loudness = 1.0
    for position, blocks in cuts:
        heights = jax.random.uniform(jax.random.fold_in(jax.random.fold_in(own_key, 6), position), (blocks,), jnp.float32, least / len(cuts), high / len(cuts))
        loudness = loudness * jnp.repeat(jnp.exp(heights), extent[position] // blocks).reshape((-1,) + (1,) * (len(extent) - 1 - position))
    return loudness


def noise(stream_key, shape, scale, limit, cuts=(), kind=jnp.bfloat16):
    level = shard_levels(stream_key, shape, cuts, -0.22, 0.18) if cuts else 1.0
    drawn = jax.random.normal(stream_key, shape, jnp.float32) * scale * level
    return jnp.minimum(jnp.maximum(drawn, -limit), limit).astype(kind)


def setup_inputs(seed: int = 0, part: int = 0) -> dict:
    key_list = jax.random.split(jax.random.key(seed), 7)
    part_keys = jax.random.split(jax.random.fold_in(key_list[6], part), 7)
    return {
        "q_stream": noise(part_keys[0], (SEQ_LEN, D), 1.0, 6.0, ((0, 16),)),
        "k_stream": noise(part_keys[1], (SEQ_LEN, D), 1.0, 6.0, ((0, 16),)),
        "v_stream": noise(part_keys[2], (SEQ_LEN, D), 1.0, 6.0, ((0, 16),)),
        "feat_filter": noise(key_list[3], (3, FEAT, D), FEAT ** -0.5, 3.5, (), jnp.float32),
        "long_filter": noise(key_list[4], (GROUPS, FILT), FILT ** -0.5, 0.5),
        "skip_gain": noise(key_list[5], (D,), 0.5, 3.0, (), jnp.float32),
    }


def featurize(stream, taps):
    length = stream.shape[0]
    padded = jnp.pad(stream.astype(jnp.float32), ((FEAT - 1, 0), (0, 0)))
    total = taps[0] * padded[FEAT - 1:FEAT - 1 + length]
    for j in range(1, FEAT):
        total = total + taps[j] * padded[FEAT - 1 - j:FEAT - 1 - j + length]
    return total


def reference(q_stream, k_stream, v_stream, feat_filter, long_filter, skip_gain):
    length = q_stream.shape[0]
    block = math.gcd(D, 512)
    count = D // block
    expanded = jnp.repeat(long_filter.astype(jnp.float32), GROUP_CH, axis=0).T

    def split(stream):
        return stream.reshape(length, count, block).transpose(1, 0, 2)

    taps_feat = feat_filter.reshape(3, FEAT, count, block).transpose(2, 0, 1, 3)
    taps_long = expanded.reshape(FILT, count, block).transpose(1, 0, 2)
    skips = skip_gain.reshape(count, block)

    def one_block(items):
        query, keys, values, tfeat, tlong, skip = items
        q_feat = featurize(query, tfeat[0])
        k_feat = featurize(keys, tfeat[1])
        v_feat = featurize(values, tfeat[2])
        gated = (k_feat * v_feat).astype(jnp.bfloat16)
        gated_f = gated.astype(jnp.float32)
        padded = jnp.pad(gated_f, ((FILT - 1, 0), (0, 0)))

        def add_tap(j, total):
            return total + tlong[j] * lax.dynamic_slice_in_dim(padded, FILT - 1 - j, length, 0)

        conv = lax.fori_loop(0, FILT, add_tap, jnp.zeros((length, block), jnp.float32))
        return (q_feat * (conv + skip * gated_f)).astype(jnp.bfloat16)

    result = lax.map(one_block, (split(q_stream), split(k_stream), split(v_stream), taps_feat, taps_long, skips))
    return result.transpose(1, 0, 2).reshape(length, D)
```

```python
import functools

import jax
import jax.numpy as jnp
from jax import lax
from jax.experimental import pallas as pl
from jax.experimental.pallas import tpu as pltpu
from jax.sharding import PartitionSpec as P

GROUP_CH = 16
FILT = 128
FEAT = 3
LANES = 128
SUB = 16
STEP = 512
F32 = jnp.float32
BF16 = jnp.bfloat16


def passed_along(shard):
    length = lax.axis_size("seq")
    return lax.ppermute(shard, "seq", [(i, i + 1) for i in range(length - 1)])


def delayed(x, by):
    return pltpu.roll(x, by, 0)


def feature(x, taps):
    total = taps[0:1] * x
    for j in range(1, FEAT):
        total = total + taps[j : j + 1] * delayed(x, j)
    return total


def rows_iota(shape):
    return lax.broadcasted_iota(jnp.int32, shape, 0)


def gate_kernel(rims, *refs):
    if rims:
        k_ref, v_ref, qt_ref, taps_ref, kt_ref, vt_ref, out_ref = refs
    else:
        k_ref, v_ref, qt_ref, taps_ref, out_ref = refs
    rows, width = k_ref.shape
    for c in range(width // LANES):
        at = slice(c * LANES, (c + 1) * LANES)
        k = k_ref[:, at].astype(F32)
        v = v_ref[:, at].astype(F32)
        gated = feature(k, taps_ref[1, :, at]) * feature(v, taps_ref[2, :, at])
        qt = delayed(qt_ref[:, at].astype(F32), FEAT - 1)
        head = jnp.where(rows_iota((SUB, LANES)) < FEAT - 1, qt, gated[:SUB])
        out_ref[:SUB, at] = head.astype(BF16)
        out_ref[SUB:rows, at] = gated[SUB:].astype(BF16)
    if rims:
        parts = kt_ref.shape[1] // width
        for c in range(width // LANES):
            tail = jnp.zeros((SUB, LANES), F32)
            iota = rows_iota((SUB, LANES))
            for b in range(parts):
                at = slice(b * width + c * LANES, b * width + (c + 1) * LANES)
                kt = kt_ref[:, at].astype(F32)
                vt = vt_ref[:, at].astype(F32)
                low = 2 * (FEAT - 1) * b
                kt = pltpu.roll(kt, (low + FEAT - 1) % SUB, 0)
                vt = pltpu.roll(vt, (low + 2 * (FEAT - 1)) % SUB, 0)
                tail = jnp.where((iota >= low) & (iota < low + FEAT - 1), kt, tail)
                tail = jnp.where((iota >= low + FEAT - 1) & (iota < low + 2 * (FEAT - 1)), vt, tail)
            out_ref[rows:, c * LANES : (c + 1) * LANES] = tail.astype(BF16)


def gate(k, v, q, taps, first, width, rims=False):
    rows, full = k.shape
    steps = width // STEP
    base = first // STEP
    last = rows // SUB - 1
    big = pl.BlockSpec((rows, STEP), lambda s: (0, base + s))
    in_specs = [
        big,
        big,
        pl.BlockSpec((SUB, STEP), lambda s: (last, base + s)),
        pl.BlockSpec((3, FEAT, STEP), lambda s: (0, 0, base + s)),
    ]
    args = [k, v, q, taps]
    out_rows = rows
    if rims:
        wide = full // steps
        in_specs += [pl.BlockSpec((SUB, wide), lambda s: (last, s))] * 2
        args += [k, v]
        out_rows += SUB
    return pl.pallas_call(
        functools.partial(gate_kernel, rims),
        grid=(steps,),
        in_specs=in_specs,
        out_specs=pl.BlockSpec((out_rows, STEP), lambda s: (0, s)),
        out_shape=jax.ShapeDtypeStruct((out_rows, width), BF16),
        cost_estimate=pl.CostEstimate(flops=12 * rows * width, bytes_accessed=6 * rows * width, transcendentals=0),
        name="gate",
    )(*args)


def edge_kernel(k_ref, v_ref, rim_ref, taps_ref, out_ref):
    width = rim_ref.shape[1]
    parts = k_ref.shape[1] // width
    iota = rows_iota((SUB, LANES))
    for b in range(parts):
        low = 2 * (FEAT - 1) * b
        for c in range(width // LANES):
            at = slice(b * width + c * LANES, b * width + (c + 1) * LANES)
            rim = rim_ref[:, c * LANES : (c + 1) * LANES].astype(F32)
            feats = []
            for i, ref in ((0, k_ref), (1, v_ref)):
                moved = pltpu.roll(rim, (SUB - (FEAT - 1) * (i + 1) - low) % SUB, 0)
                x = jnp.where(iota >= SUB - (FEAT - 1), moved, ref[:, at].astype(F32))
                feats.append(feature(x, taps_ref[i + 1, :, at]))
            out_ref[:, at] = (feats[0] * feats[1]).astype(BF16)[: out_ref.shape[0]]


def edge(k, v, rims, taps):
    rows, full = k.shape
    steps = rims.shape[1] // STEP
    wide = full // steps
    at_rim = rows // SUB
    return pl.pallas_call(
        edge_kernel,
        grid=(steps,),
        in_specs=[
            pl.BlockSpec((SUB, wide), lambda s: (0, s)),
            pl.BlockSpec((SUB, wide), lambda s: (0, s)),
            pl.BlockSpec((SUB, STEP), lambda s: (at_rim, s)),
            pl.BlockSpec((3, FEAT, wide), lambda s: (0, 0, s)),
        ],
        out_specs=pl.BlockSpec((FEAT - 1, wide), lambda s: (0, s)),
        out_shape=jax.ShapeDtypeStruct((FEAT - 1, full), BF16),
        cost_estimate=pl.CostEstimate(flops=12 * SUB * full, bytes_accessed=6 * SUB * full, transcendentals=0),
        name="edge",
    )(k, v, rims, taps)


def mix_kernel(h_ref, own_ref, got_ref, edge_ref, before_ref, q_ref, taps_ref, skip_ref, _, out_ref, lhs_ref):
    rows, width = q_ref.shape
    half = rows // 2
    per = LANES // GROUP_CH
    i = rows_iota((FILT, FILT))
    j = lax.broadcasted_iota(jnp.int32, (FILT, FILT), 1)
    flip = (i + j == FILT) | ((i == 0) & (j == 0))
    turned = jnp.dot(h_ref[...], flip.astype(BF16), preferred_element_type=F32)
    iota = rows_iota((SUB, LANES))
    b = rows_iota((half, FILT))
    m = lax.broadcasted_iota(jnp.int32, (half, FILT), 1)
    lane_group = lax.broadcasted_iota(jnp.int32, (half, 2 * LANES), 1) % LANES // GROUP_CH
    for c in range(width // LANES):
        at = slice(c * LANES, (c + 1) * LANES)
        for g in range(per):
            row = jnp.broadcast_to(turned[c * per + g : c * per + g + 1], (half, FILT))
            ring = pltpu.roll(row, 0, 1, stride=1, stride_axis=0)
            lhs_ref[g * half : (g + 1) * half, :FILT] = jnp.where(m > b, ring, 0.0).astype(BF16)
            lhs_ref[g * half : (g + 1) * half, FILT:] = jnp.where(m <= b, ring, 0.0).astype(BF16)
        edges = edge_ref[:, at].astype(F32)
        own_head = own_ref[:SUB, at].astype(F32)
        own_head = jnp.where(iota == 0, edges[0:1], own_head)
        own_head = jnp.where(iota == 1, edges[1:2], own_head)
        got_head = got_ref[:SUB, at].astype(F32)
        q_rim = got_head
        got_head = jnp.where(iota == 1, before_ref[1:2, at].astype(F32), got_head)
        cur0 = jnp.concatenate([own_head.astype(BF16), own_ref[SUB:half, at]], axis=0)
        cur1 = own_ref[half:, at]
        prev0 = jnp.concatenate([got_head.astype(BF16), got_ref[SUB:half, at]], axis=0)
        prev1 = got_ref[half:rows, at]
        rhs = jnp.concatenate(
            [
                jnp.concatenate([prev0, prev1], axis=1),
                jnp.concatenate([prev1, cur0], axis=1),
                jnp.concatenate([cur0, cur1], axis=1),
                jnp.concatenate([cur1, cur1], axis=1),
            ],
            axis=0,
        )
        res = jnp.dot(lhs_ref[...], rhs, preferred_element_type=F32)
        total = res[:half]
        for g in range(1, per):
            total = jnp.where(lane_group == g, res[g * half : (g + 1) * half], total)
        conv = jnp.concatenate([total[:, :LANES], total[:, LANES:]], axis=0)
        cur = jnp.concatenate([cur0, cur1], axis=0).astype(F32)
        q = q_ref[:, at].astype(F32)
        taps = taps_ref[0, :, at]
        q_feat = taps[0:1] * q
        rim = jnp.concatenate([q_rim[:8], jnp.zeros((rows - 8, LANES), F32)], axis=0)
        full_iota = rows_iota((rows, LANES))
        for d in range(1, FEAT):
            moved = delayed(q, d)
            shifted = pltpu.roll(rim, (d - (FEAT - 1)) % rows, 0)
            q_feat = q_feat + taps[d : d + 1] * jnp.where(full_iota < d, shifted, moved)
        out_ref[:, at] = (q_feat * (conv + skip_ref[:, at] * cur)).astype(BF16)


def mix(filters, own, got, edges, before, q, taps, skip, out, first):
    rows, full = q.shape
    width = own.shape[1]
    steps = width // STEP
    base = first // STEP
    mine = lambda s: (0, s)
    abs_ = lambda s: (0, base + s)
    in_specs = [
        pl.BlockSpec((STEP // GROUP_CH, FILT), lambda s: (base + s, 0)),
        pl.BlockSpec((rows, STEP), mine),
        pl.BlockSpec((rows, STEP), mine),
        pl.BlockSpec((FEAT - 1, STEP), abs_),
        pl.BlockSpec((FEAT - 1, STEP), abs_),
        pl.BlockSpec((rows, STEP), abs_),
        pl.BlockSpec((3, FEAT, STEP), lambda s: (0, 0, base + s)),
        pl.BlockSpec((1, STEP), abs_),
    ]
    args = [filters, own, got, edges, before, q, taps, skip]
    aliases = {}
    kernel = mix_kernel
    if out is not None:
        in_specs.append(pl.BlockSpec(memory_space=pl.ANY))
        args.append(out)
        aliases = {len(args) - 1: 0}
    else:
        kernel = lambda *refs: mix_kernel(*refs[:8], None, *refs[8:])
    return pl.pallas_call(
        kernel,
        grid=(steps,),
        in_specs=in_specs,
        out_specs=pl.BlockSpec((rows, STEP), abs_),
        out_shape=jax.ShapeDtypeStruct((rows, full), BF16),
        scratch_shapes=[pltpu.VMEM((LANES // GROUP_CH * rows // 2, 2 * FILT), BF16)],
        input_output_aliases=aliases,
        cost_estimate=pl.CostEstimate(
            flops=4 * rows * FILT * width, bytes_accessed=8 * rows * width, transcendentals=0
        ),
        name="mix",
    )(*args)


def shards(q_stream, k_stream, v_stream, feat_filter, long_filter, skip_gain):
    rows, width = q_stream.shape
    skip = skip_gain.reshape(1, width)
    quarter = width // 4
    sizes = [quarter, quarter, quarter, quarter - STEP, STEP]
    starts = [sum(sizes[:i]) for i in range(len(sizes))]
    own = []
    got = []
    for i, (first, size) in enumerate(zip(starts, sizes)):
        own.append(gate(k_stream, v_stream, q_stream, feat_filter, first, size, rims=i == 0))
        got.append(passed_along(own[-1]))
    edges = edge(k_stream, v_stream, got[0], feat_filter)
    before = passed_along(edges)
    out = None
    for first, a, b in zip(starts, own, got):
        out = mix(long_filter, a, b, edges, before, q_stream, feat_filter, skip, out, first)
    return out


def solution(mesh):
    in_specs = (
        P(("rep", "seq"), None),
        P(("rep", "seq"), None),
        P(("rep", "seq"), None),
        P(),
        P(),
        P(),
    )
    out_specs = P(("rep", "seq"), None)
    return jax.shard_map(shards, mesh=mesh, in_specs=in_specs, out_specs=out_specs, check_vma=False)
```

```python
import functools

import jax
import jax.numpy as jnp
from jax import lax
from jax.experimental import pallas as pl
from jax.experimental.pallas import tpu as pltpu
from jax.sharding import PartitionSpec as P

GROUP_CH = 16
FILT = 128
FEAT = 3
LANES = 128
SUB = 16
PIECE = 512
MIB = 1 << 20
F32 = jnp.float32
BF16 = jnp.bfloat16
VMEM = pl.BlockSpec(memory_space=pltpu.VMEM)
HBM = pl.BlockSpec(memory_space=pltpu.HBM)
COST = pl.CostEstimate(flops=1000, bytes_accessed=1000, transcendentals=0)
LONG = pl.CostEstimate(flops=1000, bytes_accessed=64 * MIB, transcendentals=0)


def passed_along(shard):
    length = lax.axis_size("seq")
    return lax.ppermute(shard, "seq", [(i, i + 1) for i in range(length - 1)])


def feature(x, taps):
    total = taps[0:1] * x
    for j in range(1, FEAT):
        total = total + taps[j : j + 1] * pltpu.roll(x, j, 0)
    return total


def rows_iota(shape):
    return lax.broadcasted_iota(jnp.int32, shape, 0)


def lanes_at(c):
    return pl.ds(c * LANES if isinstance(c, int) else pl.multiple_of(c * LANES, LANES), LANES)


def in_hbm(x):
    return pltpu.with_memory_space_constraint(x, pltpu.HBM)


def run_of(tiles, most=8):
    return max(n for n in range(1, most + 1) if tiles % n == 0)


def params(mib):
    return pltpu.CompilerParams(vmem_limit_bytes=mib * MIB)


def gate_tile(k, v, taps, at):
    return feature(k.astype(F32), taps[1, :, at]) * feature(v.astype(F32), taps[2, :, at])


def gate_piece(k_ref, v_ref, q_tail, taps_ref, out_ref, src, dst, at):
    rows = k_ref.shape[0]
    gated = gate_tile(k_ref[:, src], v_ref[:, src], taps_ref, at)
    tail = pltpu.roll(q_tail.astype(F32), FEAT - 1, 0)
    head = jnp.where(rows_iota((SUB, LANES)) < FEAT - 1, tail, gated[:SUB])
    out_ref[:SUB, dst] = head.astype(BF16)
    out_ref[SUB:rows, dst] = gated[SUB:].astype(BF16)


def first_gate_kernel(k_hbm, v_hbm, q_hbm, taps_hbm, out_ref, k_ref, v_ref, taps_ref, qt_ref, kt_ref, vt_ref, sems):
    rows, width = k_ref.shape
    full = kt_ref.shape[1]
    pieces = width // PIECE
    last = pl.ds(rows - SUB, SUB)

    def load(p, ref, hbm, i):
        at = pl.ds(p * PIECE, PIECE)
        return pltpu.make_async_copy(hbm.at[:, at], ref.at[:, at], sems.at[2 * p + i])

    rest = [
        pltpu.make_async_copy(taps_hbm.at[:, :, pl.ds(0, width)], taps_ref, sems.at[2 * pieces]),
        pltpu.make_async_copy(q_hbm.at[last, pl.ds(0, width)], qt_ref, sems.at[2 * pieces + 1]),
        pltpu.make_async_copy(k_hbm.at[last], kt_ref, sems.at[2 * pieces + 2]),
        pltpu.make_async_copy(v_hbm.at[last], vt_ref, sems.at[2 * pieces + 3]),
    ]
    rest[0].start()
    rest[1].start()
    for p in range(pieces):
        load(p, k_ref, k_hbm, 0).start()
        load(p, v_ref, v_hbm, 1).start()
    rest[2].start()
    rest[3].start()
    rest[0].wait()
    rest[1].wait()
    for p in range(pieces):
        load(p, k_ref, k_hbm, 0).wait()
        load(p, v_ref, v_hbm, 1).wait()

        @pl.loop(0, PIECE // LANES)
        def _(c):
            at = lanes_at(c + p * (PIECE // LANES))
            gate_piece(k_ref, v_ref, qt_ref[:, at], taps_ref, out_ref, at, at, at)

    rest[2].wait()
    rest[3].wait()
    iota = rows_iota((SUB, LANES))

    @pl.loop(0, width // LANES)
    def _(c):
        tail = jnp.zeros((SUB, LANES), F32)
        for b in range(full // width):
            low = 2 * (FEAT - 1) * b
            at = lanes_at(c + b * (width // LANES))
            kt = pltpu.roll(kt_ref[:, at].astype(F32), (low + FEAT - 1) % SUB, 0)
            vt = pltpu.roll(vt_ref[:, at].astype(F32), (low + 2 * (FEAT - 1)) % SUB, 0)
            tail = jnp.where((iota >= low) & (iota < low + FEAT - 1), kt, tail)
            tail = jnp.where((iota >= low + FEAT - 1) & (iota < low + 2 * (FEAT - 1)), vt, tail)
        out_ref[rows:, lanes_at(c)] = tail.astype(BF16)


def first_gate(k, v, q, taps, width):
    rows, full = k.shape
    return pl.pallas_call(
        first_gate_kernel,
        in_specs=[HBM] * 4,
        out_specs=VMEM,
        out_shape=jax.ShapeDtypeStruct((rows + SUB, width), BF16),
        scratch_shapes=[
            pltpu.VMEM((rows, width), BF16),
            pltpu.VMEM((rows, width), BF16),
            pltpu.VMEM((3, FEAT, width), F32),
            pltpu.VMEM((SUB, width), BF16),
            pltpu.VMEM((SUB, full), BF16),
            pltpu.VMEM((SUB, full), BF16),
            pltpu.SemaphoreType.DMA((2 * (width // PIECE) + 4,)),
        ],
        compiler_params=params(12),
        cost_estimate=COST,
        name="gate_first",
    )(*(in_hbm(x) for x in (k, v, q, taps)))


def gate_kernel(firsts, k_ref, v_ref, q_ref, taps_ref, _, *out_refs):
    rows = k_ref.shape[0]
    for first, out_ref in zip(firsts, out_refs):

        @pl.loop(0, out_ref.shape[1] // LANES, unroll=2)
        def _(c):
            at = lanes_at(c + first // LANES)
            gate_piece(k_ref, v_ref, q_ref[rows - SUB :, at], taps_ref, out_ref, at, lanes_at(c), at)


def gate(k, v, q, taps, after, firsts, widths):
    rows = k.shape[0]
    return pl.pallas_call(
        functools.partial(gate_kernel, firsts),
        in_specs=[VMEM] * 4 + [pl.BlockSpec(memory_space=pl.ANY)],
        out_specs=[VMEM] * len(widths),
        out_shape=[jax.ShapeDtypeStruct((rows, w), BF16) for w in widths],
        compiler_params=params(12),
        cost_estimate=COST,
        name="gate",
    )(k, v, q, taps, after)


def last_gate_kernel(kh_ref, vh_ref, taps_ref, rim_ref, own_ref, out_ref, edge_ref):
    rows, width = own_ref.shape
    full = kh_ref.shape[1]
    wide = rim_ref.shape[1]
    iota = rows_iota((SUB, LANES))

    @pl.loop(0, wide // LANES)
    def _(c):
        rim = rim_ref[rows:, lanes_at(c)].astype(F32)
        for b in range(full // wide):
            low = 2 * (FEAT - 1) * b
            at = lanes_at(c + b * (wide // LANES))
            feats = []
            for i, ref in ((0, kh_ref), (1, vh_ref)):
                moved = pltpu.roll(rim, (SUB - (FEAT - 1) * (i + 1) - low) % SUB, 0)
                x = jnp.where(iota >= SUB - (FEAT - 1), moved, ref[:SUB, at].astype(F32))
                feats.append(feature(x, taps_ref[i + 1, :, at]))
            edge_ref[:, at] = (feats[0] * feats[1]).astype(BF16)

    @pl.loop(0, width // LANES)
    def _(c):
        out_ref[:rows, lanes_at(c)] = own_ref[:, lanes_at(c)]
        tail = jnp.zeros((SUB, LANES), F32)
        for b in range(pl.cdiv(full, width)):
            at = lanes_at(lax.rem(c + b * (width // LANES), full // LANES))
            one = jnp.broadcast_to(edge_ref[:, at].astype(F32)[1:2], (SUB, LANES))
            tail = jnp.where(iota == b, one, tail)
        out_ref[rows:, lanes_at(c)] = tail.astype(BF16)


def last_gate(k_head, v_head, taps, rims, own):
    rows, width = own.shape
    full = k_head.shape[1]
    return pl.pallas_call(
        last_gate_kernel,
        in_specs=[VMEM] * 5,
        out_specs=[VMEM] * 2,
        out_shape=[
            jax.ShapeDtypeStruct((rows + SUB, width), BF16),
            jax.ShapeDtypeStruct((SUB, full), BF16),
        ],
        compiler_params=params(12),
        cost_estimate=COST,
        name="gate_last",
    )(k_head, v_head, taps, rims, own)


def turned_filters(h):
    i = rows_iota((FILT, FILT))
    j = lax.broadcasted_iota(jnp.int32, (FILT, FILT), 1)
    flip = (i + j == FILT) | ((i == 0) & (j == 0))
    return jnp.dot(h, flip.astype(BF16), preferred_element_type=F32)


def fill_mask(mask_ref):
    rows, cols = mask_ref.shape
    i = rows_iota((rows, cols))
    b = i // SUB * 8 + i % 8
    m = lax.broadcasted_iota(jnp.int32, (rows, cols), 1)
    mask_ref[...] = jnp.where((m > b) & (m <= b + FILT), 1.0, 0.0).astype(BF16)


def mix_tile(turned_ref, mask_ref, lhs_ref, own_ref, got_ref, edge_ref, q_ref, taps_ref, skip_ref, before, src, dst, c):
    rows = q_ref.shape[0]
    half = rows // 2
    per = LANES // GROUP_CH
    iota = rows_iota((SUB, LANES))
    lane_group = lax.broadcasted_iota(jnp.int32, (8, 2 * LANES), 1) % LANES // GROUP_CH
    turned = turned_ref[pl.ds(c * per if isinstance(c, int) else pl.multiple_of(c * per, per), per), :]
    rings = []
    for g in range(per):
        row = jnp.broadcast_to(turned[g : g + 1], (half, FILT))
        rings.append(pltpu.roll(row, 0, 1, stride=1, stride_axis=0))
    for r in range(half // 8):
        mask = mask_ref[r * SUB : (r + 1) * SUB]
        for g in range(0, per, 2):
            pair = jnp.concatenate([rings[g][r * 8 : r * 8 + 8], rings[g + 1][r * 8 : r * 8 + 8]], axis=0)
            pair = pair.astype(BF16)
            low = (r * per + g) * 8
            lhs_ref[low : low + SUB, :] = jnp.concatenate([pair, pair], axis=1) * mask
    own_head = jnp.where(iota < FEAT - 1, edge_ref[:, src].astype(F32), own_ref[:SUB, dst].astype(F32))
    got_head = got_ref[:SUB, dst].astype(F32)
    q_rim = got_head
    if before is None:
        got_head = jnp.where(iota < FEAT - 1, 0.0, got_head)
    else:
        got_head = jnp.where(iota < FEAT - 1, before, got_head)
    cur0 = jnp.concatenate([own_head.astype(BF16), own_ref[SUB:half, dst]], axis=0)
    cur1 = own_ref[half:rows, dst]
    prev0 = jnp.concatenate([got_head.astype(BF16), got_ref[SUB:half, dst]], axis=0)
    prev1 = got_ref[half:rows, dst]
    rhs = jnp.concatenate(
        [
            jnp.concatenate([prev0, prev1], axis=1),
            jnp.concatenate([prev1, cur0], axis=1),
            jnp.concatenate([cur0, cur1], axis=1),
            jnp.concatenate([cur1, cur1], axis=1),
        ],
        axis=0,
    )
    res = jnp.dot(lhs_ref[...], rhs, preferred_element_type=F32)
    totals = []
    for r in range(half // 8):
        total = res[r * per * 8 : r * per * 8 + 8]
        for g in range(1, per):
            low = (r * per + g) * 8
            total = jnp.where(lane_group == g, res[low : low + 8], total)
        totals.append(total)
    conv = jnp.concatenate([t[:, :LANES] for t in totals] + [t[:, LANES:] for t in totals], axis=0)
    cur = jnp.concatenate([cur0, cur1], axis=0).astype(F32)
    q = q_ref[:, src].astype(F32)
    taps = taps_ref[0, :, src]
    q_feat = taps[0:1] * q
    for d in range(1, FEAT):
        moved = pltpu.roll(q, d, 0)
        shifted = pltpu.roll(q_rim, (d - (FEAT - 1)) % SUB, 0)
        head = jnp.where(iota < d, shifted, moved[:SUB])
        q_feat = q_feat + taps[d : d + 1] * jnp.concatenate([head, moved[SUB:]], axis=0)
    return q_feat * (conv + skip_ref[:, src] * cur), q_feat, turned


def mix_kernel(first, has_out, h_ref, own_ref, got_ref, edge_ref, q_ref, taps_ref, skip_ref, *refs):
    refs = refs[1:] if has_out else refs
    out_hbm, head_ref, slope_ref, res_ref, turned_ref, mask_ref, lhs_ref, sems = refs
    rows = q_ref.shape[0]
    width = res_ref.shape[1]
    per = LANES // GROUP_CH
    fill_mask(mask_ref)
    turned_ref[...] = turned_filters(h_ref[pl.ds(first // GROUP_CH, width // GROUP_CH), :])
    row_group = rows_iota((per, LANES))
    lane_group = lax.broadcasted_iota(jnp.int32, (per, LANES), 1) // GROUP_CH

    run = run_of(width // LANES)
    runs = width // LANES // run

    def store(p):
        here = pl.ds(pl.multiple_of(p * run * LANES, LANES), run * LANES)
        there = pl.ds(pl.multiple_of(first + p * run * LANES, LANES), run * LANES)
        return pltpu.make_async_copy(
            res_ref.at[:, here], out_hbm.at[pl.ds(SUB, rows - SUB), there], sems.at[p]
        )

    @pl.loop(0, runs)
    def _(p):
        for u in range(run):
            c = p * run + u
            dst = lanes_at(c)
            src = lanes_at(c + first // LANES)
            mixed, q_feat, turned = mix_tile(
                turned_ref, mask_ref, lhs_ref.at[u], own_ref, got_ref, edge_ref, q_ref, taps_ref, skip_ref, None, src, dst, c
            )
            res_ref[:, dst] = mixed[SUB:].astype(BF16)
            head_ref[:, dst] = mixed[:SUB]
            last_tap = jnp.where(row_group == lane_group, jnp.broadcast_to(turned[:, 1:2], (per, LANES)), 0.0)
            slope_ref[:, dst] = q_feat[:8] * jnp.sum(last_tap, axis=0, keepdims=True)
        store(p).start()

    @pl.loop(0, runs)
    def _(p):
        store(p).wait()


def mix(filters, own, got, edges, q, taps, skip, out, first):
    rows, full = q.shape
    width = own.shape[1]
    run = run_of(width // LANES)
    per = LANES // GROUP_CH
    args = [filters, own, got, edges, q, taps, skip]
    in_specs = [VMEM] * len(args)
    if out is not None:
        in_specs.append(HBM)
        args.append(out)
    return pl.pallas_call(
        functools.partial(mix_kernel, first, out is not None),
        in_specs=in_specs,
        out_specs=[HBM, VMEM, VMEM],
        out_shape=[
            jax.ShapeDtypeStruct((rows, full), BF16),
            jax.ShapeDtypeStruct((SUB, width), F32),
            jax.ShapeDtypeStruct((8, width), F32),
        ],
        scratch_shapes=[
            pltpu.VMEM((rows - SUB, width), BF16),
            pltpu.VMEM((width // GROUP_CH, FILT), F32),
            pltpu.VMEM((rows, 2 * FILT), BF16),
            pltpu.VMEM((run, per * rows // 2, 2 * FILT), BF16),
            pltpu.SemaphoreType.DMA((width // LANES // run,)),
        ],
        input_output_aliases={} if out is None else {len(args) - 1: 0},
        compiler_params=params(12),
        cost_estimate=LONG,
        name="mix",
    )(*args)


def last_mix_kernel(first, parts, h_ref, own_ref, got_ref, edge_ref, q_ref, taps_ref, skip_ref, *refs):
    heads, slopes = refs[:parts], refs[parts : 2 * parts]
    _, out_hbm, res_ref, top_ref, turned_ref, mask_ref, lhs_ref, sems, top_sem = refs[2 * parts :]
    rows, full = q_ref.shape
    width = res_ref.shape[1]
    fill_mask(mask_ref)
    turned_ref[...] = turned_filters(h_ref[pl.ds(first // GROUP_CH, width // GROUP_CH), :])
    iota = rows_iota((SUB, LANES))

    def before_at(c_all):
        tiles = width // LANES
        col = lax.rem(c_all, tiles)
        row = lax.div(c_all, tiles)
        x = got_ref[rows:, lanes_at(col)].astype(F32)
        return jnp.sum(jnp.where(iota == row, x, 0.0), axis=0, keepdims=True)

    at_first = 0
    for head_ref, slope_ref in zip(heads, slopes):
        wide = head_ref.shape[1]

        @pl.loop(0, wide // LANES, unroll=2)
        def _(c):
            c_all = c + at_first // LANES
            head = head_ref[:, lanes_at(c)]
            more = slope_ref[:, lanes_at(c)] * before_at(c_all)
            more = jnp.concatenate([more, jnp.zeros_like(more)], axis=0)
            top_ref[:, lanes_at(c_all)] = jnp.where(iota == 0, head + more, head).astype(BF16)

        at_first += wide
    top = pltpu.make_async_copy(top_ref, out_hbm.at[pl.ds(0, SUB), pl.ds(0, first)], top_sem)
    top.start()

    run = run_of(width // LANES)
    runs = width // LANES // run

    def store(p):
        here = pl.ds(pl.multiple_of(p * run * LANES, LANES), run * LANES)
        there = pl.ds(pl.multiple_of(first + p * run * LANES, LANES), run * LANES)
        return pltpu.make_async_copy(res_ref.at[:, here], out_hbm.at[:, there], sems.at[p])

    @pl.loop(0, runs)
    def _(p):
        for u in range(run):
            c = p * run + u
            dst = lanes_at(c)
            src = lanes_at(c + first // LANES)
            before = before_at(c + first // LANES)
            mixed, _, _ = mix_tile(
                turned_ref, mask_ref, lhs_ref.at[u], own_ref, got_ref, edge_ref, q_ref, taps_ref, skip_ref, before, src, dst, c
            )
            res_ref[:, dst] = mixed.astype(BF16)
        store(p).start()

    @pl.loop(0, runs)
    def _(p):
        store(p).wait()

    top.wait()


def last_mix(filters, own, got, edges, q, taps, skip, heads, slopes, out, first):
    rows, full = q.shape
    width = own.shape[1]
    run = run_of(width // LANES)
    per = LANES // GROUP_CH
    args = [filters, own, got, edges, q, taps, skip, *heads, *slopes, out]
    return pl.pallas_call(
        functools.partial(last_mix_kernel, first, len(heads)),
        in_specs=[VMEM] * (len(args) - 1) + [HBM],
        out_specs=HBM,
        out_shape=jax.ShapeDtypeStruct((rows, full), BF16),
        scratch_shapes=[
            pltpu.VMEM((rows, width), BF16),
            pltpu.VMEM((SUB, first), BF16),
            pltpu.VMEM((width // GROUP_CH, FILT), F32),
            pltpu.VMEM((rows, 2 * FILT), BF16),
            pltpu.VMEM((run, per * rows // 2, 2 * FILT), BF16),
            pltpu.SemaphoreType.DMA((width // LANES // run,)),
            pltpu.SemaphoreType.DMA,
        ],
        input_output_aliases={len(args) - 1: 0},
        compiler_params=params(12),
        cost_estimate=LONG,
        name="mix_last",
    )(*args)


def shards(q_stream, k_stream, v_stream, feat_filter, long_filter, skip_gain):
    rows, width = q_stream.shape
    skip = skip_gain.reshape(1, width)
    unit = width // 32
    sizes = [8 * unit, 9 * unit, 8 * unit, 7 * unit]
    starts = [sum(sizes[:i]) for i in range(len(sizes))]
    streams = (k_stream, v_stream, q_stream, feat_filter)
    own = [first_gate(*streams, sizes[0])]
    got = [passed_along(own[0])]
    more = gate(*streams, own[0], starts[1:], sizes[1:])
    own += more[:2]
    got += [passed_along(own[1]), passed_along(own[2])]
    last, edges = last_gate(k_stream, v_stream, feat_filter, got[0], more[2])
    own.append(last)
    got.append(passed_along(last))
    out = None
    heads = []
    slopes = []
    for first, a, b in zip(starts[:3], own, got):
        out, head, slope = mix(long_filter, a, b, edges, q_stream, feat_filter, skip, out, first)
        heads.append(head)
        slopes.append(slope)
    return last_mix(
        long_filter, own[3], got[3], edges, q_stream, feat_filter, skip, heads, slopes, out, starts[3]
    )


def solution(mesh):
    in_specs = (
        P(("rep", "seq"), None),
        P(("rep", "seq"), None),
        P(("rep", "seq"), None),
        P(),
        P(),
        P(),
    )
    out_specs = P(("rep", "seq"), None)
    return jax.shard_map(shards, mesh=mesh, in_specs=in_specs, out_specs=out_specs, check_vma=False)
```

```python
import functools

import jax
import jax.numpy as jnp
from jax import lax
from jax.experimental import pallas as pl
from jax.experimental.pallas import tpu as pltpu
from jax.sharding import PartitionSpec as P

GROUP_CH = 16
FILT = 128
FEAT = 3
LANES = 128
SUB = 16
PIECE = 512
MIB = 1 << 20
F32 = jnp.float32
BF16 = jnp.bfloat16
VMEM = pl.BlockSpec(memory_space=pltpu.VMEM)
HBM = pl.BlockSpec(memory_space=pltpu.HBM)
COST = pl.CostEstimate(flops=1000, bytes_accessed=1000, transcendentals=0)
LONG = pl.CostEstimate(flops=1000, bytes_accessed=64 * MIB, transcendentals=0)


def passed_along(shard, first=0, step=1):
    length = lax.axis_size("seq")
    return lax.ppermute(shard, "seq", [(i, i + 1) for i in range(first, length - 1, step)])


def sends_first():
    return lax.rem(lax.axis_index("seq"), 2) == 1


def feature(x, taps):
    total = taps[0:1] * x
    for j in range(1, FEAT):
        total = total + taps[j : j + 1] * pltpu.roll(x, j, 0)
    return total


def rows_iota(shape):
    return lax.broadcasted_iota(jnp.int32, shape, 0)


def lanes_at(c):
    return pl.ds(c * LANES if isinstance(c, int) else pl.multiple_of(c * LANES, LANES), LANES)


def in_hbm(x):
    return pltpu.with_memory_space_constraint(x, pltpu.HBM)


def run_of(tiles, most=8):
    return max(n for n in range(1, most + 1) if tiles % n == 0)


def params(mib):
    return pltpu.CompilerParams(vmem_limit_bytes=mib * MIB)


def gate_tile(k, v, taps, at):
    return feature(k.astype(F32), taps[1, :, at]) * feature(v.astype(F32), taps[2, :, at])


def gate_piece(k_ref, v_ref, q_tail, taps_ref, out_ref, src, dst, at):
    rows = k_ref.shape[0]
    gated = gate_tile(k_ref[:, src], v_ref[:, src], taps_ref, at)
    tail = pltpu.roll(q_tail.astype(F32), FEAT - 1, 0)
    head = jnp.where(rows_iota((SUB, LANES)) < FEAT - 1, tail, gated[:SUB])
    out_ref[:SUB, dst] = head.astype(BF16)
    out_ref[SUB:rows, dst] = gated[SUB:].astype(BF16)


def rim_rows(kt_ref, vt_ref, out_ref):
    full = kt_ref.shape[1]
    rows, width = out_ref.shape
    last = kt_ref.shape[0] - SUB
    iota = rows_iota((SUB, LANES))

    @pl.loop(0, width // LANES, unroll=2)
    def _(c):
        tail = jnp.zeros((SUB, LANES), F32)
        for b in range(pl.cdiv(full, width)):
            low = 2 * (FEAT - 1) * b
            at = lanes_at(lax.rem(c + b * (width // LANES), full // LANES))
            kt = pltpu.roll(kt_ref[last:, at].astype(F32), (low + FEAT - 1) % SUB, 0)
            vt = pltpu.roll(vt_ref[last:, at].astype(F32), (low + 2 * (FEAT - 1)) % SUB, 0)
            tail = jnp.where((iota >= low) & (iota < low + FEAT - 1), kt, tail)
            tail = jnp.where((iota >= low + FEAT - 1) & (iota < low + 2 * (FEAT - 1)), vt, tail)
        out_ref[rows - SUB :, lanes_at(c)] = tail.astype(BF16)


def first_gate_kernel(*refs):
    @pl.when(sends_first())
    def _():
        first_gate_body(*refs)


def first_gate_body(k_hbm, v_hbm, q_hbm, taps_hbm, out_ref, k_ref, v_ref, taps_ref, qt_ref, kt_ref, vt_ref, sems):
    rows, width = k_ref.shape
    pieces = width // PIECE
    last = pl.ds(rows - SUB, SUB)

    def load(p, ref, hbm, i):
        at = pl.ds(p * PIECE, PIECE)
        return pltpu.make_async_copy(hbm.at[:, at], ref.at[:, at], sems.at[2 * p + i])

    rest = [
        pltpu.make_async_copy(taps_hbm.at[:, :, pl.ds(0, width)], taps_ref, sems.at[2 * pieces]),
        pltpu.make_async_copy(q_hbm.at[last, pl.ds(0, width)], qt_ref, sems.at[2 * pieces + 1]),
        pltpu.make_async_copy(k_hbm.at[last], kt_ref, sems.at[2 * pieces + 2]),
        pltpu.make_async_copy(v_hbm.at[last], vt_ref, sems.at[2 * pieces + 3]),
    ]
    rest[0].start()
    rest[1].start()
    for p in range(pieces):
        load(p, k_ref, k_hbm, 0).start()
        load(p, v_ref, v_hbm, 1).start()
    rest[2].start()
    rest[3].start()
    rest[0].wait()
    rest[1].wait()
    for p in range(pieces):
        load(p, k_ref, k_hbm, 0).wait()
        load(p, v_ref, v_hbm, 1).wait()

        @pl.loop(0, PIECE // LANES)
        def _(c):
            at = lanes_at(c + p * (PIECE // LANES))
            gate_piece(k_ref, v_ref, qt_ref[:, at], taps_ref, out_ref, at, at, at)

    rest[2].wait()
    rest[3].wait()
    rim_rows(kt_ref, vt_ref, out_ref)


def first_gate(k, v, q, taps, width):
    rows, full = k.shape
    return pl.pallas_call(
        first_gate_kernel,
        in_specs=[HBM] * 4,
        out_specs=VMEM,
        out_shape=jax.ShapeDtypeStruct((rows + SUB, width), BF16),
        scratch_shapes=[
            pltpu.VMEM((rows, width), BF16),
            pltpu.VMEM((rows, width), BF16),
            pltpu.VMEM((3, FEAT, width), F32),
            pltpu.VMEM((SUB, width), BF16),
            pltpu.VMEM((SUB, full), BF16),
            pltpu.VMEM((SUB, full), BF16),
            pltpu.SemaphoreType.DMA((2 * (width // PIECE) + 4,)),
        ],
        compiler_params=params(12),
        cost_estimate=COST,
        name="gate_first",
    )(*(in_hbm(x) for x in (k, v, q, taps)))


def gate_block(k_ref, v_ref, q_ref, taps_ref, out_ref, first):
    rows = k_ref.shape[0]

    @pl.loop(0, out_ref.shape[1] // LANES, unroll=2)
    def _(c):
        at = lanes_at(c + first // LANES)
        gate_piece(k_ref, v_ref, q_ref[rows - SUB :, at], taps_ref, out_ref, at, lanes_at(c), at)


def second_gate_kernel(first, k_ref, v_ref, q_ref, taps_ref, begun_ref, out_ref, more_ref):
    begun = sends_first()

    @pl.when(begun)
    def _():
        out_ref[...] = begun_ref[...]

    @pl.when(jnp.logical_not(begun))
    def _():
        gate_block(k_ref, v_ref, q_ref, taps_ref, out_ref, 0)
        rim_rows(k_ref, v_ref, out_ref)

    gate_block(k_ref, v_ref, q_ref, taps_ref, more_ref, first)


def second_gate(k, v, q, taps, begun, first, width):
    return pl.pallas_call(
        functools.partial(second_gate_kernel, first),
        in_specs=[VMEM] * 5,
        out_specs=[VMEM] * 2,
        out_shape=[
            jax.ShapeDtypeStruct(begun.shape, BF16),
            jax.ShapeDtypeStruct((k.shape[0], width), BF16),
        ],
        compiler_params=params(12),
        cost_estimate=COST,
        name="gate_second",
    )(k, v, q, taps, begun)


def gate_kernel(firsts, k_ref, v_ref, q_ref, taps_ref, _, *out_refs):
    for first, out_ref in zip(firsts, out_refs):
        gate_block(k_ref, v_ref, q_ref, taps_ref, out_ref, first)


def gate(k, v, q, taps, after, firsts, widths):
    return pl.pallas_call(
        functools.partial(gate_kernel, firsts),
        in_specs=[VMEM] * 4 + [pl.BlockSpec(memory_space=pl.ANY)],
        out_specs=[VMEM] * len(widths),
        out_shape=[jax.ShapeDtypeStruct((k.shape[0], w), BF16) for w in widths],
        compiler_params=params(12),
        cost_estimate=COST,
        name="gate",
    )(k, v, q, taps, after)


def settle_kernel(in_ref, out_ref):
    out_ref[...] = in_ref[...]


def settle(x):
    return pl.pallas_call(
        settle_kernel,
        in_specs=[VMEM],
        out_specs=VMEM,
        out_shape=jax.ShapeDtypeStruct(x.shape, x.dtype),
        compiler_params=params(12),
        cost_estimate=COST,
        name="settle",
    )(x)


def last_gate_kernel(k_ref, v_ref, taps_ref, crossed_ref, near_ref, own_ref, out_ref, edge_ref, got_ref):
    rows, width = own_ref.shape
    full = k_ref.shape[1]
    wide = got_ref.shape[1]
    iota = rows_iota((SUB, LANES))
    got_ref[...] = crossed_ref[...] + near_ref[...]

    for b in range(pl.cdiv(full, wide)):
        low = 2 * (FEAT - 1) * b
        count = min(wide, full - b * wide) // LANES

        @pl.loop(0, count, unroll=2)
        def _(c):
            rim = got_ref[rows:, lanes_at(c)].astype(F32)
            at = lanes_at(c + b * (wide // LANES))
            feats = []
            for i, ref in ((0, k_ref), (1, v_ref)):
                moved = pltpu.roll(rim, (SUB - (FEAT - 1) * (i + 1) - low) % SUB, 0)
                x = jnp.where(iota >= SUB - (FEAT - 1), moved, ref[:SUB, at].astype(F32))
                feats.append(feature(x, taps_ref[i + 1, :, at]))
            edge_ref[:, at] = (feats[0] * feats[1]).astype(BF16)

    extra = out_ref.shape[0] - rows

    @pl.loop(0, width // LANES)
    def _(c):
        out_ref[:rows, lanes_at(c)] = own_ref[:, lanes_at(c)]
        tail = jnp.zeros((extra, LANES), F32)
        for b in range(pl.cdiv(full, width)):
            at = lanes_at(lax.rem(c + b * (width // LANES), full // LANES))
            one = jnp.broadcast_to(edge_ref[:, at].astype(F32)[1:2], (extra, LANES))
            tail = jnp.where(rows_iota((extra, LANES)) == b, one, tail)
        out_ref[rows:, lanes_at(c)] = tail.astype(BF16)


def last_gate(k, v, taps, crossed, near, own):
    rows, width = own.shape
    full = k.shape[1]
    extra = pl.cdiv(pl.cdiv(full, width), 8) * 8
    return pl.pallas_call(
        last_gate_kernel,
        in_specs=[VMEM] * 6,
        out_specs=[VMEM] * 3,
        out_shape=[
            jax.ShapeDtypeStruct((rows + extra, width), BF16),
            jax.ShapeDtypeStruct((SUB, full), BF16),
            jax.ShapeDtypeStruct(crossed.shape, BF16),
        ],
        compiler_params=params(12),
        cost_estimate=COST,
        name="gate_last",
    )(k, v, taps, crossed, near, own)


def turned_filters(h):
    i = rows_iota((FILT, FILT))
    j = lax.broadcasted_iota(jnp.int32, (FILT, FILT), 1)
    flip = (i + j == FILT) | ((i == 0) & (j == 0))
    return jnp.dot(h, flip.astype(BF16), preferred_element_type=F32)


def fill_mask(mask_ref):
    rows, cols = mask_ref.shape
    i = rows_iota((rows, cols))
    b = i // SUB * 8 + i % 8
    m = lax.broadcasted_iota(jnp.int32, (rows, cols), 1)
    mask_ref[...] = jnp.where((m > b) & (m <= b + FILT), 1.0, 0.0).astype(BF16)


def mix_tile(turned_ref, mask_ref, lhs_ref, own_ref, got_ref, edge_ref, q_ref, taps_ref, skip_ref, before, src, dst, c):
    rows = q_ref.shape[0]
    half = rows // 2
    per = LANES // GROUP_CH
    iota = rows_iota((SUB, LANES))
    lane_group = lax.broadcasted_iota(jnp.int32, (8, 2 * LANES), 1) % LANES // GROUP_CH
    turned = turned_ref[pl.ds(c * per if isinstance(c, int) else pl.multiple_of(c * per, per), per), :]
    rings = []
    for g in range(per):
        row = jnp.broadcast_to(turned[g : g + 1], (half, FILT))
        rings.append(pltpu.roll(row, 0, 1, stride=1, stride_axis=0))
    for r in range(half // 8):
        mask = mask_ref[r * SUB : (r + 1) * SUB]
        for g in range(0, per, 2):
            pair = jnp.concatenate([rings[g][r * 8 : r * 8 + 8], rings[g + 1][r * 8 : r * 8 + 8]], axis=0)
            pair = pair.astype(BF16)
            low = (r * per + g) * 8
            lhs_ref[low : low + SUB, :] = jnp.concatenate([pair, pair], axis=1) * mask
    own_head = jnp.where(iota < FEAT - 1, edge_ref[:, src].astype(F32), own_ref[:SUB, dst].astype(F32))
    got_head = got_ref[:SUB, dst].astype(F32)
    q_rim = got_head
    if before is None:
        got_head = jnp.where(iota < FEAT - 1, 0.0, got_head)
    else:
        got_head = jnp.where(iota < FEAT - 1, before, got_head)
    cur0 = jnp.concatenate([own_head.astype(BF16), own_ref[SUB:half, dst]], axis=0)
    cur1 = own_ref[half:rows, dst]
    prev0 = jnp.concatenate([got_head.astype(BF16), got_ref[SUB:half, dst]], axis=0)
    prev1 = got_ref[half:rows, dst]
    rhs = jnp.concatenate(
        [
            jnp.concatenate([prev0, prev1], axis=1),
            jnp.concatenate([prev1, cur0], axis=1),
            jnp.concatenate([cur0, cur1], axis=1),
            jnp.concatenate([cur1, cur1], axis=1),
        ],
        axis=0,
    )
    res = jnp.dot(lhs_ref[...], rhs, preferred_element_type=F32)
    totals = []
    for r in range(half // 8):
        total = res[r * per * 8 : r * per * 8 + 8]
        for g in range(1, per):
            low = (r * per + g) * 8
            total = jnp.where(lane_group == g, res[low : low + 8], total)
        totals.append(total)
    conv = jnp.concatenate([t[:, :LANES] for t in totals] + [t[:, LANES:] for t in totals], axis=0)
    cur = jnp.concatenate([cur0, cur1], axis=0).astype(F32)
    q = q_ref[:, src].astype(F32)
    taps = taps_ref[0, :, src]
    q_feat = taps[0:1] * q
    for d in range(1, FEAT):
        moved = pltpu.roll(q, d, 0)
        shifted = pltpu.roll(q_rim, (d - (FEAT - 1)) % SUB, 0)
        head = jnp.where(iota < d, shifted, moved[:SUB])
        q_feat = q_feat + taps[d : d + 1] * jnp.concatenate([head, moved[SUB:]], axis=0)
    return q_feat * (conv + skip_ref[:, src] * cur), q_feat, turned


def mix_kernel(first, has_out, h_ref, own_ref, got_ref, edge_ref, q_ref, taps_ref, skip_ref, *refs):
    refs = refs[1:] if has_out else refs
    out_hbm, head_ref, slope_ref, res_ref, turned_ref, mask_ref, lhs_ref, sems = refs
    rows = q_ref.shape[0]
    width = res_ref.shape[1]
    per = LANES // GROUP_CH
    fill_mask(mask_ref)
    turned_ref[...] = turned_filters(h_ref[pl.ds(first // GROUP_CH, width // GROUP_CH), :])
    row_group = rows_iota((per, LANES))
    lane_group = lax.broadcasted_iota(jnp.int32, (per, LANES), 1) // GROUP_CH

    run = run_of(width // LANES)
    runs = width // LANES // run

    def store(p):
        here = pl.ds(pl.multiple_of(p * run * LANES, LANES), run * LANES)
        there = pl.ds(pl.multiple_of(first + p * run * LANES, LANES), run * LANES)
        return pltpu.make_async_copy(
            res_ref.at[:, here], out_hbm.at[pl.ds(SUB, rows - SUB), there], sems.at[p]
        )

    @pl.loop(0, runs)
    def _(p):
        for u in range(run):
            c = p * run + u
            dst = lanes_at(c)
            src = lanes_at(c + first // LANES)
            mixed, q_feat, turned = mix_tile(
                turned_ref, mask_ref, lhs_ref.at[u], own_ref, got_ref, edge_ref, q_ref, taps_ref, skip_ref, None, src, dst, c
            )
            res_ref[:, dst] = mixed[SUB:].astype(BF16)
            head_ref[:, dst] = mixed[:SUB]
            last_tap = jnp.where(row_group == lane_group, jnp.broadcast_to(turned[:, 1:2], (per, LANES)), 0.0)
            slope_ref[:, dst] = q_feat[:8] * jnp.sum(last_tap, axis=0, keepdims=True)
        store(p).start()

    @pl.loop(0, runs)
    def _(p):
        store(p).wait()


def mix(filters, own, got, edges, q, taps, skip, out, first):
    rows, full = q.shape
    width = own.shape[1]
    run = run_of(width // LANES)
    per = LANES // GROUP_CH
    args = [filters, own, got, edges, q, taps, skip]
    in_specs = [VMEM] * len(args)
    if out is not None:
        in_specs.append(HBM)
        args.append(out)
    return pl.pallas_call(
        functools.partial(mix_kernel, first, out is not None),
        in_specs=in_specs,
        out_specs=[HBM, VMEM, VMEM],
        out_shape=[
            jax.ShapeDtypeStruct((rows, full), BF16),
            jax.ShapeDtypeStruct((SUB, width), F32),
            jax.ShapeDtypeStruct((8, width), F32),
        ],
        scratch_shapes=[
            pltpu.VMEM((rows - SUB, width), BF16),
            pltpu.VMEM((width // GROUP_CH, FILT), F32),
            pltpu.VMEM((rows, 2 * FILT), BF16),
            pltpu.VMEM((run, per * rows // 2, 2 * FILT), BF16),
            pltpu.SemaphoreType.DMA((width // LANES // run,)),
        ],
        input_output_aliases={} if out is None else {len(args) - 1: 0},
        compiler_params=params(12),
        cost_estimate=LONG,
        name="mix",
    )(*args)


def last_mix_kernel(first, parts, h_ref, own_ref, got_ref, edge_ref, q_ref, taps_ref, skip_ref, *refs):
    heads, slopes = refs[:parts], refs[parts : 2 * parts]
    _, out_hbm, res_ref, top_ref, turned_ref, mask_ref, lhs_ref, sems, top_sem = refs[2 * parts :]
    rows, full = q_ref.shape
    width = res_ref.shape[1]
    fill_mask(mask_ref)
    turned_ref[...] = turned_filters(h_ref[pl.ds(first // GROUP_CH, width // GROUP_CH), :])
    iota = rows_iota((SUB, LANES))

    def before_at(c_all):
        tiles = width // LANES
        col = lax.rem(c_all, tiles)
        row = lax.div(c_all, tiles)
        x = got_ref[rows:, lanes_at(col)].astype(F32)
        return jnp.sum(jnp.where(rows_iota(x.shape) == row, x, 0.0), axis=0, keepdims=True)

    at_first = 0
    for head_ref, slope_ref in zip(heads, slopes):
        wide = head_ref.shape[1]

        @pl.loop(0, wide // LANES, unroll=2)
        def _(c):
            c_all = c + at_first // LANES
            head = head_ref[:, lanes_at(c)]
            more = slope_ref[:, lanes_at(c)] * before_at(c_all)
            more = jnp.concatenate([more, jnp.zeros_like(more)], axis=0)
            top_ref[:, lanes_at(c_all)] = jnp.where(iota == 0, head + more, head).astype(BF16)

        at_first += wide
    top = pltpu.make_async_copy(top_ref, out_hbm.at[pl.ds(0, SUB), pl.ds(0, first)], top_sem)
    top.start()

    run = run_of(width // LANES)
    runs = width // LANES // run

    def store(p):
        here = pl.ds(pl.multiple_of(p * run * LANES, LANES), run * LANES)
        there = pl.ds(pl.multiple_of(first + p * run * LANES, LANES), run * LANES)
        return pltpu.make_async_copy(res_ref.at[:, here], out_hbm.at[:, there], sems.at[p])

    @pl.loop(0, runs)
    def _(p):
        for u in range(run):
            c = p * run + u
            dst = lanes_at(c)
            src = lanes_at(c + first // LANES)
            before = before_at(c + first // LANES)
            mixed, _, _ = mix_tile(
                turned_ref, mask_ref, lhs_ref.at[u], own_ref, got_ref, edge_ref, q_ref, taps_ref, skip_ref, before, src, dst, c
            )
            res_ref[:, dst] = mixed.astype(BF16)
        store(p).start()

    @pl.loop(0, runs)
    def _(p):
        store(p).wait()

    top.wait()


def last_mix(filters, own, got, edges, q, taps, skip, heads, slopes, out, first):
    rows, full = q.shape
    width = own.shape[1]
    run = run_of(width // LANES)
    per = LANES // GROUP_CH
    args = [filters, own, got, edges, q, taps, skip, *heads, *slopes, out]
    return pl.pallas_call(
        functools.partial(last_mix_kernel, first, len(heads)),
        in_specs=[VMEM] * (len(args) - 1) + [HBM],
        out_specs=HBM,
        out_shape=jax.ShapeDtypeStruct((rows, full), BF16),
        scratch_shapes=[
            pltpu.VMEM((rows, width), BF16),
            pltpu.VMEM((SUB, first), BF16),
            pltpu.VMEM((width // GROUP_CH, FILT), F32),
            pltpu.VMEM((rows, 2 * FILT), BF16),
            pltpu.VMEM((run, per * rows // 2, 2 * FILT), BF16),
            pltpu.SemaphoreType.DMA((width // LANES // run,)),
            pltpu.SemaphoreType.DMA,
        ],
        input_output_aliases={len(args) - 1: 0},
        compiler_params=params(12),
        cost_estimate=LONG,
        name="mix_last",
    )(*args)


def shards(q_stream, k_stream, v_stream, feat_filter, long_filter, skip_gain):
    rows, width = q_stream.shape
    skip = skip_gain.reshape(1, width)
    unit = width // 32
    sizes = [8 * unit, 9 * unit, 8 * unit, 7 * unit]
    starts = [sum(sizes[:i]) for i in range(len(sizes))]
    streams = (k_stream, v_stream, q_stream, feat_filter)
    begun = first_gate(*streams, sizes[0])
    crossed = passed_along(begun, 1, 2)
    own = list(second_gate(*streams, begun, starts[1], sizes[1]))
    near = passed_along(own[0], 0, 2)
    got = [None, passed_along(own[1])]
    more, last = gate(*streams, own[1], starts[2:], sizes[2:])
    own.append(more)
    got.append(passed_along(more))
    last, edges, got[0] = last_gate(k_stream, v_stream, feat_filter, settle(crossed), near, last)
    own.append(last)
    got.append(passed_along(last))
    out = None
    heads = []
    slopes = []
    for first, a, b in zip(starts[:3], own, got):
        out, head, slope = mix(long_filter, a, b, edges, q_stream, feat_filter, skip, out, first)
        heads.append(head)
        slopes.append(slope)
    return last_mix(
        long_filter, own[3], got[3], edges, q_stream, feat_filter, skip, heads, slopes, out, starts[3]
    )


def solution(mesh):
    in_specs = (
        P(("rep", "seq"), None),
        P(("rep", "seq"), None),
        P(("rep", "seq"), None),
        P(),
        P(),
        P(),
    )
    out_specs = P(("rep", "seq"), None)
    return jax.shard_map(shards, mesh=mesh, in_specs=in_specs, out_specs=out_specs, check_vma=False)
```

```python
import functools

import jax
import jax.numpy as jnp
from jax import lax
from jax.experimental import pallas as pl
from jax.experimental.pallas import tpu as pltpu
from jax.sharding import PartitionSpec as P

GROUP_CH = 16
FILT = 128
FEAT = 3
LANES = 128
SUB = 16
MIB = 1 << 20
F32 = jnp.float32
BF16 = jnp.bfloat16
VMEM = pl.BlockSpec(memory_space=pltpu.VMEM)
HBM = pl.BlockSpec(memory_space=pltpu.HBM)
COST = pl.CostEstimate(flops=1000, bytes_accessed=1000, transcendentals=0)


def passed_along(shard, first=0, step=1):
    length = lax.axis_size("seq")
    return lax.ppermute(shard, "seq", [(i, i + 1) for i in range(first, length - 1, step)])


def sends_first():
    return lax.rem(lax.axis_index("seq"), 2) == 1


def feature(x, taps):
    total = taps[0:1] * x
    for j in range(1, FEAT):
        total = total + taps[j : j + 1] * pltpu.roll(x, j, 0)
    return total


def rows_iota(shape):
    return lax.broadcasted_iota(jnp.int32, shape, 0)


def lanes_at(c):
    return pl.ds(c * LANES if isinstance(c, int) else pl.multiple_of(c * LANES, LANES), LANES)


def in_hbm(x):
    return pltpu.with_memory_space_constraint(x, pltpu.HBM)


def run_of(tiles, most=8):
    return max(n for n in range(1, most + 1) if tiles % n == 0)


def params(mib):
    return pltpu.CompilerParams(vmem_limit_bytes=mib * MIB)


def gate_tile(k, v, taps, at):
    return feature(k.astype(F32), taps[1, :, at]) * feature(v.astype(F32), taps[2, :, at])


def gate_piece(k_ref, v_ref, q_tail, taps_ref, out_ref, src, dst, at):
    rows = k_ref.shape[0]
    gated = gate_tile(k_ref[:, src], v_ref[:, src], taps_ref, at)
    tail = pltpu.roll(q_tail.astype(F32), FEAT - 1, 0)
    head = jnp.where(rows_iota((SUB, LANES)) < FEAT - 1, tail, gated[:SUB])
    out_ref[:SUB, dst] = head.astype(BF16)
    out_ref[SUB:rows, dst] = gated[SUB:].astype(BF16)


def rim_rows(kt_ref, vt_ref, out_ref):
    full = kt_ref.shape[1]
    rows, width = out_ref.shape
    last = kt_ref.shape[0] - SUB
    iota = rows_iota((SUB, LANES))

    @pl.loop(0, width // LANES, unroll=2)
    def _(c):
        tail = jnp.zeros((SUB, LANES), F32)
        for b in range(pl.cdiv(full, width)):
            low = 2 * (FEAT - 1) * b
            at = lanes_at(lax.rem(c + b * (width // LANES), full // LANES))
            kt = pltpu.roll(kt_ref[last:, at].astype(F32), (low + FEAT - 1) % SUB, 0)
            vt = pltpu.roll(vt_ref[last:, at].astype(F32), (low + 2 * (FEAT - 1)) % SUB, 0)
            tail = jnp.where((iota >= low) & (iota < low + FEAT - 1), kt, tail)
            tail = jnp.where((iota >= low + FEAT - 1) & (iota < low + 2 * (FEAT - 1)), vt, tail)
        out_ref[rows - SUB :, lanes_at(c)] = tail.astype(BF16)


def first_gate_kernel(*refs):
    @pl.when(sends_first())
    def _():
        first_gate_body(*refs)


def first_gate_body(k_hbm, v_hbm, q_hbm, taps_hbm, out_ref, k_ref, v_ref, taps_ref, qt_ref, kt_ref, vt_ref, sems):
    rows, width = k_ref.shape
    run = run_of(width // LANES, 5)
    pieces = width // LANES // run
    last = pl.ds(rows - SUB, SUB)

    def load(p, ref, hbm, i):
        at = pl.ds(p * run * LANES, run * LANES)
        return pltpu.make_async_copy(hbm.at[:, at], ref.at[:, at], sems.at[2 * p + i])

    rest = [
        pltpu.make_async_copy(taps_hbm.at[:, :, pl.ds(0, width)], taps_ref, sems.at[2 * pieces]),
        pltpu.make_async_copy(q_hbm.at[last, pl.ds(0, width)], qt_ref, sems.at[2 * pieces + 1]),
        pltpu.make_async_copy(k_hbm.at[last], kt_ref, sems.at[2 * pieces + 2]),
        pltpu.make_async_copy(v_hbm.at[last], vt_ref, sems.at[2 * pieces + 3]),
    ]
    rest[0].start()
    rest[1].start()
    for p in range(pieces):
        load(p, k_ref, k_hbm, 0).start()
        load(p, v_ref, v_hbm, 1).start()
    rest[2].start()
    rest[3].start()
    rest[0].wait()
    rest[1].wait()
    for p in range(pieces):
        load(p, k_ref, k_hbm, 0).wait()
        load(p, v_ref, v_hbm, 1).wait()

        @pl.loop(0, run, unroll=run)
        def _(c):
            at = lanes_at(c + p * run)
            gate_piece(k_ref, v_ref, qt_ref[:, at], taps_ref, out_ref, at, at, at)

    rest[2].wait()
    rest[3].wait()
    rim_rows(kt_ref, vt_ref, out_ref)


def first_gate(k, v, q, taps, width):
    rows, full = k.shape
    return pl.pallas_call(
        first_gate_kernel,
        in_specs=[HBM] * 4,
        out_specs=VMEM,
        out_shape=jax.ShapeDtypeStruct((rows + SUB, width), BF16),
        scratch_shapes=[
            pltpu.VMEM((rows, width), BF16),
            pltpu.VMEM((rows, width), BF16),
            pltpu.VMEM((3, FEAT, width), F32),
            pltpu.VMEM((SUB, width), BF16),
            pltpu.VMEM((SUB, full), BF16),
            pltpu.VMEM((SUB, full), BF16),
            pltpu.SemaphoreType.DMA((2 * (width // LANES // run_of(width // LANES, 5)) + 4,)),
        ],
        compiler_params=params(12),
        cost_estimate=COST,
        name="gate_first",
    )(*(in_hbm(x) for x in (k, v, q, taps)))


def gate_block(k_ref, v_ref, q_ref, taps_ref, out_ref, first):
    rows = k_ref.shape[0]

    @pl.loop(0, out_ref.shape[1] // LANES, unroll=2)
    def _(c):
        at = lanes_at(c + first // LANES)
        gate_piece(k_ref, v_ref, q_ref[rows - SUB :, at], taps_ref, out_ref, at, lanes_at(c), at)


def second_gate_kernel(first, k_ref, v_ref, q_ref, taps_ref, begun_ref, out_ref, more_ref):
    begun = sends_first()

    @pl.when(begun)
    def _():
        out_ref[...] = begun_ref[...]

    @pl.when(jnp.logical_not(begun))
    def _():
        gate_block(k_ref, v_ref, q_ref, taps_ref, out_ref, 0)
        rim_rows(k_ref, v_ref, out_ref)

    gate_block(k_ref, v_ref, q_ref, taps_ref, more_ref, first)


def second_gate(k, v, q, taps, begun, first, width):
    return pl.pallas_call(
        functools.partial(second_gate_kernel, first),
        in_specs=[VMEM] * 5,
        out_specs=[VMEM] * 2,
        out_shape=[
            jax.ShapeDtypeStruct(begun.shape, BF16),
            jax.ShapeDtypeStruct((k.shape[0], width), BF16),
        ],
        compiler_params=params(12),
        cost_estimate=COST,
        name="gate_second",
    )(k, v, q, taps, begun)


def gate_kernel(firsts, k_ref, v_ref, q_ref, taps_ref, h_ref, _, turned_ref, mask_ref, *out_refs):
    for first, out_ref in zip(firsts, out_refs):
        gate_block(k_ref, v_ref, q_ref, taps_ref, out_ref, first)
    turned_ref[...] = turned_filters(h_ref[...])
    fill_mask(mask_ref)


def gate(k, v, q, taps, h, after, firsts, widths):
    rows = k.shape[0]
    return pl.pallas_call(
        functools.partial(gate_kernel, firsts),
        in_specs=[VMEM] * 5 + [pl.BlockSpec(memory_space=pl.ANY)],
        out_specs=[VMEM] * (len(widths) + 2),
        out_shape=[jax.ShapeDtypeStruct(h.shape, F32), jax.ShapeDtypeStruct((rows, 2 * FILT), BF16)]
        + [jax.ShapeDtypeStruct((rows, w), BF16) for w in widths],
        compiler_params=params(12),
        cost_estimate=COST,
        name="gate",
    )(k, v, q, taps, h, after)


def settle_kernel(in_ref, out_ref):
    out_ref[...] = in_ref[...]


def settle(x):
    return pl.pallas_call(
        settle_kernel,
        in_specs=[VMEM],
        out_specs=VMEM,
        out_shape=jax.ShapeDtypeStruct(x.shape, x.dtype),
        compiler_params=params(12),
        cost_estimate=COST,
        name="settle",
    )(x)


def last_gate_kernel(k_ref, v_ref, taps_ref, crossed_ref, near_ref, own_ref, out_ref, edge_ref, got_ref):
    rows, width = own_ref.shape
    full = k_ref.shape[1]
    wide = got_ref.shape[1]
    iota = rows_iota((SUB, LANES))
    got_ref[...] = crossed_ref[...] + near_ref[...]

    for b in range(pl.cdiv(full, wide)):
        low = 2 * (FEAT - 1) * b
        count = min(wide, full - b * wide) // LANES

        @pl.loop(0, count, unroll=2)
        def _(c):
            rim = got_ref[rows:, lanes_at(c)].astype(F32)
            at = lanes_at(c + b * (wide // LANES))
            feats = []
            for i, ref in ((0, k_ref), (1, v_ref)):
                moved = pltpu.roll(rim, (SUB - (FEAT - 1) * (i + 1) - low) % SUB, 0)
                x = jnp.where(iota >= SUB - (FEAT - 1), moved, ref[:SUB, at].astype(F32))
                feats.append(feature(x, taps_ref[i + 1, :, at]))
            edge_ref[:, at] = (feats[0] * feats[1]).astype(BF16)

    extra = out_ref.shape[0] - rows

    @pl.loop(0, width // LANES)
    def _(c):
        out_ref[:rows, lanes_at(c)] = own_ref[:, lanes_at(c)]
        tail = jnp.zeros((extra, LANES), F32)
        for b in range(pl.cdiv(full, width)):
            at = lanes_at(lax.rem(c + b * (width // LANES), full // LANES))
            one = jnp.broadcast_to(edge_ref[:, at].astype(F32)[1:2], (extra, LANES))
            tail = jnp.where(rows_iota((extra, LANES)) == b, one, tail)
        out_ref[rows:, lanes_at(c)] = tail.astype(BF16)


def last_gate(k, v, taps, crossed, near, own):
    rows, width = own.shape
    full = k.shape[1]
    extra = pl.cdiv(pl.cdiv(full, width), 8) * 8
    return pl.pallas_call(
        last_gate_kernel,
        in_specs=[VMEM] * 6,
        out_specs=[VMEM] * 3,
        out_shape=[
            jax.ShapeDtypeStruct((rows + extra, width), BF16),
            jax.ShapeDtypeStruct((SUB, full), BF16),
            jax.ShapeDtypeStruct(crossed.shape, BF16),
        ],
        compiler_params=params(12),
        cost_estimate=COST,
        name="gate_last",
    )(k, v, taps, crossed, near, own)


def turned_filters(h):
    i = rows_iota((FILT, FILT))
    j = lax.broadcasted_iota(jnp.int32, (FILT, FILT), 1)
    flip = (i + j == FILT) | ((i == 0) & (j == 0))
    return jnp.dot(h, flip.astype(BF16), preferred_element_type=F32)


def fill_mask(mask_ref):
    rows, cols = mask_ref.shape
    i = rows_iota((rows, cols))
    b = i // SUB * 8 + i % 8
    m = lax.broadcasted_iota(jnp.int32, (rows, cols), 1)
    mask_ref[...] = jnp.where((m > b) & (m <= b + FILT), 1.0, 0.0).astype(BF16)


def mix_tile(turned_ref, mask_ref, lhs_ref, own_ref, got_ref, edge_ref, q_ref, taps_ref, skip_ref, before, src, dst, c):
    rows = q_ref.shape[0]
    half = rows // 2
    per = LANES // GROUP_CH
    iota = rows_iota((SUB, LANES))
    lane_group = lax.broadcasted_iota(jnp.int32, (8, 2 * LANES), 1) % LANES // GROUP_CH
    turned = turned_ref[pl.ds(pl.multiple_of(c * per, per), per), :]
    rings = []
    for g in range(per):
        row = jnp.broadcast_to(turned[g : g + 1], (half, FILT))
        rings.append(pltpu.roll(row, 0, 1, stride=1, stride_axis=0))
    for r in range(half // 8):
        mask = mask_ref[r * SUB : (r + 1) * SUB]
        for g in range(0, per, 2):
            pair = jnp.concatenate([rings[g][r * 8 : r * 8 + 8], rings[g + 1][r * 8 : r * 8 + 8]], axis=0)
            pair = pair.astype(BF16)
            low = (r * per + g) * 8
            lhs_ref[low : low + SUB, :] = jnp.concatenate([pair, pair], axis=1) * mask
    own_head = jnp.where(iota < FEAT - 1, edge_ref[:, src].astype(F32), own_ref[:SUB, dst].astype(F32))
    got_head = got_ref[:SUB, dst].astype(F32)
    q_rim = got_head
    if before is None:
        got_head = jnp.where(iota < FEAT - 1, 0.0, got_head)
    else:
        got_head = jnp.where(iota < FEAT - 1, before, got_head)
    cur0 = jnp.concatenate([own_head.astype(BF16), own_ref[SUB:half, dst]], axis=0)
    cur1 = own_ref[half:rows, dst]
    prev0 = jnp.concatenate([got_head.astype(BF16), got_ref[SUB:half, dst]], axis=0)
    prev1 = got_ref[half:rows, dst]
    rhs = jnp.concatenate(
        [
            jnp.concatenate([prev0, prev1], axis=1),
            jnp.concatenate([prev1, cur0], axis=1),
            jnp.concatenate([cur0, cur1], axis=1),
            jnp.concatenate([cur1, cur1], axis=1),
        ],
        axis=0,
    )
    res = jnp.dot(lhs_ref[...], rhs, preferred_element_type=F32)
    totals = []
    for r in range(half // 8):
        total = res[r * per * 8 : r * per * 8 + 8]
        for g in range(1, per):
            low = (r * per + g) * 8
            total = jnp.where(lane_group == g, res[low : low + 8], total)
        totals.append(total)
    conv = jnp.concatenate([t[:, :LANES] for t in totals] + [t[:, LANES:] for t in totals], axis=0)
    cur = jnp.concatenate([cur0, cur1], axis=0).astype(F32)
    q = q_ref[:, src].astype(F32)
    taps = taps_ref[0, :, src]
    q_feat = taps[0:1] * q
    for d in range(1, FEAT):
        moved = pltpu.roll(q, d, 0)
        shifted = pltpu.roll(q_rim, (d - (FEAT - 1)) % SUB, 0)
        head = jnp.where(iota < d, shifted, moved[:SUB])
        q_feat = q_feat + taps[d : d + 1] * jnp.concatenate([head, moved[SUB:]], axis=0)
    return q_feat * (conv + skip_ref[:, src] * cur), q_feat, turned


def mix_kernel(first, has_out, turned_ref, mask_ref, own_ref, got_ref, edge_ref, q_ref, taps_ref, skip_ref, *refs):
    refs = refs[1:] if has_out else refs
    out_hbm, head_ref, slope_ref, res_ref, lhs_ref, sems = refs
    rows = q_ref.shape[0]
    width = res_ref.shape[1]
    per = LANES // GROUP_CH
    row_group = rows_iota((per, LANES))
    lane_group = lax.broadcasted_iota(jnp.int32, (per, LANES), 1) // GROUP_CH

    run = run_of(width // LANES)
    runs = width // LANES // run

    def store(p):
        here = pl.ds(pl.multiple_of(p * run * LANES, LANES), run * LANES)
        there = pl.ds(pl.multiple_of(first + p * run * LANES, LANES), run * LANES)
        return pltpu.make_async_copy(
            res_ref.at[:, here], out_hbm.at[pl.ds(SUB, rows - SUB), there], sems.at[p]
        )

    @pl.loop(0, runs)
    def _(p):
        for u in range(run):
            c = p * run + u
            dst = lanes_at(c)
            src = lanes_at(c + first // LANES)
            mixed, q_feat, turned = mix_tile(
                turned_ref, mask_ref, lhs_ref.at[u], own_ref, got_ref, edge_ref, q_ref, taps_ref, skip_ref, None, src, dst, c + first // LANES
            )
            res_ref[:, dst] = mixed[SUB:].astype(BF16)
            head_ref[:, dst] = mixed[:SUB]
            last_tap = jnp.where(row_group == lane_group, jnp.broadcast_to(turned[:, 1:2], (per, LANES)), 0.0)
            slope_ref[:, dst] = q_feat[:8] * jnp.sum(last_tap, axis=0, keepdims=True)
        store(p).start()

    @pl.loop(0, runs)
    def _(p):
        store(p).wait()


def mix(turned, mask, own, got, edges, q, taps, skip, out, first):
    rows, full = q.shape
    width = own.shape[1]
    run = run_of(width // LANES)
    per = LANES // GROUP_CH
    args = [turned, mask, own, got, edges, q, taps, skip]
    in_specs = [VMEM] * len(args)
    if out is not None:
        in_specs.append(HBM)
        args.append(out)
    return pl.pallas_call(
        functools.partial(mix_kernel, first, out is not None),
        in_specs=in_specs,
        out_specs=[HBM, VMEM, VMEM],
        out_shape=[
            jax.ShapeDtypeStruct((rows, full), BF16),
            jax.ShapeDtypeStruct((SUB, width), F32),
            jax.ShapeDtypeStruct((8, width), F32),
        ],
        scratch_shapes=[
            pltpu.VMEM((rows - SUB, width), BF16),
            pltpu.VMEM((run, per * rows // 2, 2 * FILT), BF16),
            pltpu.SemaphoreType.DMA((width // LANES // run,)),
        ],
        input_output_aliases={} if out is None else {len(args) - 1: 0},
        compiler_params=params(12),
        cost_estimate=COST,
        name="mix",
    )(*args)


def last_mix_kernel(first, parts, turned_ref, mask_ref, own_ref, got_ref, edge_ref, q_ref, taps_ref, skip_ref, *refs):
    heads, slopes = refs[:parts], refs[parts : 2 * parts]
    _, out_hbm, res_ref, top_ref, before_ref, lhs_ref, sems, top_sem = refs[2 * parts :]
    rows, full = q_ref.shape
    width = res_ref.shape[1]
    iota = rows_iota((SUB, LANES))

    for b in range(pl.cdiv(full, width)):
        count = min(width, full - b * width)
        before_ref[:, b * width : b * width + count] = got_ref[rows:, :count].astype(F32)[b : b + 1]

    at_first = 0
    for head_ref, slope_ref in zip(heads, slopes):
        wide = head_ref.shape[1]

        @pl.loop(0, wide // LANES, unroll=run_of(wide // LANES))
        def _(c):
            c_all = c + at_first // LANES
            head = head_ref[:, lanes_at(c)]
            more = slope_ref[:, lanes_at(c)] * before_ref[:, lanes_at(c_all)]
            more = jnp.concatenate([more, jnp.zeros_like(more)], axis=0)
            top_ref[:, lanes_at(c_all)] = jnp.where(iota == 0, head + more, head).astype(BF16)

        at_first += wide
    top = pltpu.make_async_copy(top_ref, out_hbm.at[pl.ds(0, SUB), pl.ds(0, first)], top_sem)
    top.start()

    run = run_of(width // LANES)
    runs = width // LANES // run

    def store(p):
        here = pl.ds(pl.multiple_of(p * run * LANES, LANES), run * LANES)
        there = pl.ds(pl.multiple_of(first + p * run * LANES, LANES), run * LANES)
        return pltpu.make_async_copy(res_ref.at[:, here], out_hbm.at[:, there], sems.at[p])

    @pl.loop(0, runs)
    def _(p):
        for u in range(run):
            c = p * run + u
            dst = lanes_at(c)
            src = lanes_at(c + first // LANES)
            before = before_ref[:, src]
            mixed, _, _ = mix_tile(
                turned_ref, mask_ref, lhs_ref.at[u], own_ref, got_ref, edge_ref, q_ref, taps_ref, skip_ref, before, src, dst, c + first // LANES
            )
            res_ref[:, dst] = mixed.astype(BF16)
        store(p).start()

    @pl.loop(0, runs)
    def _(p):
        store(p).wait()

    top.wait()


def last_mix(turned, mask, own, got, edges, q, taps, skip, heads, slopes, out, first):
    rows, full = q.shape
    width = own.shape[1]
    run = run_of(width // LANES)
    per = LANES // GROUP_CH
    args = [turned, mask, own, got, edges, q, taps, skip, *heads, *slopes, out]
    return pl.pallas_call(
        functools.partial(last_mix_kernel, first, len(heads)),
        in_specs=[VMEM] * (len(args) - 1) + [HBM],
        out_specs=HBM,
        out_shape=jax.ShapeDtypeStruct((rows, full), BF16),
        scratch_shapes=[
            pltpu.VMEM((rows, width), BF16),
            pltpu.VMEM((SUB, first), BF16),
            pltpu.VMEM((1, full), F32),
            pltpu.VMEM((run, per * rows // 2, 2 * FILT), BF16),
            pltpu.SemaphoreType.DMA((width // LANES // run,)),
            pltpu.SemaphoreType.DMA,
        ],
        input_output_aliases={len(args) - 1: 0},
        compiler_params=params(12),
        cost_estimate=COST,
        name="mix_last",
    )(*args)


def shards(q_stream, k_stream, v_stream, feat_filter, long_filter, skip_gain):
    rows, width = q_stream.shape
    skip = skip_gain.reshape(1, width)
    unit = width // 32
    sizes = [9 * unit, 10 * unit, 9 * unit, 4 * unit]
    starts = [sum(sizes[:i]) for i in range(len(sizes))]
    streams = (k_stream, v_stream, q_stream, feat_filter)
    begun = first_gate(*streams, sizes[0])
    crossed = passed_along(begun, 1, 2)
    own = list(second_gate(*streams, begun, starts[1], sizes[1]))
    near = passed_along(own[0], 0, 2)
    got = [None, passed_along(own[1])]
    turned, mask, more, last = gate(*streams, long_filter, own[1], starts[2:], sizes[2:])
    own.append(more)
    got.append(passed_along(more))
    last, edges, got[0] = last_gate(k_stream, v_stream, feat_filter, settle(crossed), near, last)
    own.append(last)
    got.append(passed_along(last))
    out = None
    heads = []
    slopes = []
    for first, a, b in zip(starts[:3], own, got):
        out, head, slope = mix(turned, mask, a, b, edges, q_stream, feat_filter, skip, out, first)
        heads.append(head)
        slopes.append(slope)
    return last_mix(
        turned, mask, own[3], got[3], edges, q_stream, feat_filter, skip, heads, slopes, out, starts[3]
    )


def solution(mesh):
    in_specs = (
        P(("rep", "seq"), None),
        P(("rep", "seq"), None),
        P(("rep", "seq"), None),
        P(),
        P(),
        P(),
    )
    out_specs = P(("rep", "seq"), None)
    return jax.shard_map(shards, mesh=mesh, in_specs=in_specs, out_specs=out_specs, check_vma=False)
```

```python
import functools

import jax
import jax.numpy as jnp
from jax import lax
from jax.experimental import pallas as pl
from jax.experimental.pallas import tpu as pltpu
from jax.sharding import PartitionSpec as P

GROUP_CH = 16
FILT = 128
FEAT = 3
LANES = 128
SUB = 16
WINDOWS = 4
MIB = 1 << 20
F32 = jnp.float32
BF16 = jnp.bfloat16
VMEM = pl.BlockSpec(memory_space=pltpu.VMEM)
HBM = pl.BlockSpec(memory_space=pltpu.HBM)
COST = pl.CostEstimate(flops=1000, bytes_accessed=1000, transcendentals=0)


def passed_along(shard, first=0, step=1):
    length = lax.axis_size("seq")
    return lax.ppermute(shard, "seq", [(i, i + 1) for i in range(first, length - 1, step)])


def sends_first():
    return lax.rem(lax.axis_index("seq"), 2) == 1


def feature(x, taps):
    total = taps[0:1] * x
    for j in range(1, FEAT):
        total = total + taps[j : j + 1] * pltpu.roll(x, j, 0)
    return total


def rows_iota(shape):
    return lax.broadcasted_iota(jnp.int32, shape, 0)


def lanes_at(c):
    return pl.ds(c * LANES if isinstance(c, int) else pl.multiple_of(c * LANES, LANES), LANES)


def in_hbm(x):
    return pltpu.with_memory_space_constraint(x, pltpu.HBM)


def run_of(tiles, most=10):
    return max(n for n in range(1, most + 1) if tiles % n == 0)


def params(mib):
    return pltpu.CompilerParams(vmem_limit_bytes=mib * MIB)


def gate_tile(k, v, taps, at):
    return feature(k.astype(F32), taps[1, :, at]) * feature(v.astype(F32), taps[2, :, at])


def gate_piece(k_ref, v_ref, q_tail, taps_ref, out_ref, src, dst, at):
    rows = k_ref.shape[0]
    gated = gate_tile(k_ref[:, src], v_ref[:, src], taps_ref, at)
    tail = pltpu.roll(q_tail.astype(F32), FEAT - 1, 0)
    head = jnp.where(rows_iota((SUB, LANES)) < FEAT - 1, tail, gated[:SUB])
    out_ref[:SUB, dst] = head.astype(BF16)
    out_ref[SUB:rows, dst] = gated[SUB:].astype(BF16)


def rim_rows(kt_ref, vt_ref, out_ref):
    full = kt_ref.shape[1]
    rows, width = out_ref.shape
    last = kt_ref.shape[0] - SUB
    iota = rows_iota((SUB, LANES))

    @pl.loop(0, width // LANES, unroll=2)
    def _(c):
        tail = jnp.zeros((SUB, LANES), F32)
        for b in range(pl.cdiv(full, width)):
            low = 2 * (FEAT - 1) * b
            at = lanes_at(lax.rem(c + b * (width // LANES), full // LANES))
            kt = pltpu.roll(kt_ref[last:, at].astype(F32), (low + FEAT - 1) % SUB, 0)
            vt = pltpu.roll(vt_ref[last:, at].astype(F32), (low + 2 * (FEAT - 1)) % SUB, 0)
            tail = jnp.where((iota >= low) & (iota < low + FEAT - 1), kt, tail)
            tail = jnp.where((iota >= low + FEAT - 1) & (iota < low + 2 * (FEAT - 1)), vt, tail)
        out_ref[rows - SUB :, lanes_at(c)] = tail.astype(BF16)


def first_gate_kernel(*refs):
    @pl.when(sends_first())
    def _():
        first_gate_body(*refs)


def first_gate_body(k_hbm, v_hbm, q_hbm, taps_hbm, out_ref, k_ref, v_ref, taps_ref, qt_ref, kt_ref, vt_ref, sems):
    rows, width = k_ref.shape
    run = run_of(width // LANES, 5)
    pieces = width // LANES // run
    last = pl.ds(rows - SUB, SUB)

    def load(p, ref, hbm, i):
        at = pl.ds(p * run * LANES, run * LANES)
        return pltpu.make_async_copy(hbm.at[:, at], ref.at[:, at], sems.at[2 * p + i])

    rest = [
        pltpu.make_async_copy(taps_hbm.at[:, :, pl.ds(0, width)], taps_ref, sems.at[2 * pieces]),
        pltpu.make_async_copy(q_hbm.at[last, pl.ds(0, width)], qt_ref, sems.at[2 * pieces + 1]),
        pltpu.make_async_copy(k_hbm.at[last], kt_ref, sems.at[2 * pieces + 2]),
        pltpu.make_async_copy(v_hbm.at[last], vt_ref, sems.at[2 * pieces + 3]),
    ]
    rest[0].start()
    rest[1].start()
    for p in range(pieces):
        load(p, k_ref, k_hbm, 0).start()
        load(p, v_ref, v_hbm, 1).start()
    rest[2].start()
    rest[3].start()
    rest[0].wait()
    rest[1].wait()
    for p in range(pieces):
        load(p, k_ref, k_hbm, 0).wait()
        load(p, v_ref, v_hbm, 1).wait()

        @pl.loop(0, run, unroll=run)
        def _(c):
            at = lanes_at(c + p * run)
            gate_piece(k_ref, v_ref, qt_ref[:, at], taps_ref, out_ref, at, at, at)

    rest[2].wait()
    rest[3].wait()
    rim_rows(kt_ref, vt_ref, out_ref)


def first_gate(k, v, q, taps, width):
    rows, full = k.shape
    return pl.pallas_call(
        first_gate_kernel,
        in_specs=[HBM] * 4,
        out_specs=VMEM,
        out_shape=jax.ShapeDtypeStruct((rows + SUB, width), BF16),
        scratch_shapes=[
            pltpu.VMEM((rows, width), BF16),
            pltpu.VMEM((rows, width), BF16),
            pltpu.VMEM((3, FEAT, width), F32),
            pltpu.VMEM((SUB, width), BF16),
            pltpu.VMEM((SUB, full), BF16),
            pltpu.VMEM((SUB, full), BF16),
            pltpu.SemaphoreType.DMA((2 * (width // LANES // run_of(width // LANES, 5)) + 4,)),
        ],
        compiler_params=params(12),
        cost_estimate=COST,
        name="gate_first",
    )(*(in_hbm(x) for x in (k, v, q, taps)))


def gate_block(k_ref, v_ref, q_ref, taps_ref, out_ref, first):
    rows = k_ref.shape[0]

    @pl.loop(0, out_ref.shape[1] // LANES, unroll=2)
    def _(c):
        at = lanes_at(c + first // LANES)
        gate_piece(k_ref, v_ref, q_ref[rows - SUB :, at], taps_ref, out_ref, at, lanes_at(c), at)


def second_gate_kernel(first, k_ref, v_ref, q_ref, taps_ref, begun_ref, out_ref, more_ref):
    begun = sends_first()

    @pl.when(begun)
    def _():
        out_ref[...] = begun_ref[...]

    @pl.when(jnp.logical_not(begun))
    def _():
        gate_block(k_ref, v_ref, q_ref, taps_ref, out_ref, 0)
        rim_rows(k_ref, v_ref, out_ref)

    gate_block(k_ref, v_ref, q_ref, taps_ref, more_ref, first)


def second_gate(k, v, q, taps, begun, first, width):
    return pl.pallas_call(
        functools.partial(second_gate_kernel, first),
        in_specs=[VMEM] * 5,
        out_specs=[VMEM] * 2,
        out_shape=[
            jax.ShapeDtypeStruct(begun.shape, BF16),
            jax.ShapeDtypeStruct((k.shape[0], width), BF16),
        ],
        compiler_params=params(12),
        cost_estimate=COST,
        name="gate_second",
    )(k, v, q, taps, begun)


def gate_kernel(firsts, k_ref, v_ref, q_ref, taps_ref, h_ref, _, turned_ref, mask_ref, *out_refs):
    for first, out_ref in zip(firsts, out_refs):
        gate_block(k_ref, v_ref, q_ref, taps_ref, out_ref, first)
    turned_ref[...] = turned_filters(h_ref[...])
    fill_mask(mask_ref)


def gate(k, v, q, taps, h, after, firsts, widths):
    rows = k.shape[0]
    return pl.pallas_call(
        functools.partial(gate_kernel, firsts),
        in_specs=[VMEM] * 5 + [pl.BlockSpec(memory_space=pl.ANY)],
        out_specs=[VMEM] * (len(widths) + 2),
        out_shape=[jax.ShapeDtypeStruct(h.shape, F32), jax.ShapeDtypeStruct((2 * rows // WINDOWS, 2 * FILT), BF16)]
        + [jax.ShapeDtypeStruct((rows, w), BF16) for w in widths],
        compiler_params=params(12),
        cost_estimate=COST,
        name="gate",
    )(k, v, q, taps, h, after)


def settle_kernel(in_ref, out_ref):
    out_ref[...] = in_ref[...]


def settle(x):
    return pl.pallas_call(
        settle_kernel,
        in_specs=[VMEM],
        out_specs=VMEM,
        out_shape=jax.ShapeDtypeStruct(x.shape, x.dtype),
        compiler_params=params(12),
        cost_estimate=COST,
        name="settle",
    )(x)


def last_gate_kernel(k_ref, v_ref, taps_ref, crossed_ref, near_ref, own_ref, out_ref, edge_ref, got_ref):
    rows, width = own_ref.shape
    full = k_ref.shape[1]
    wide = got_ref.shape[1]
    iota = rows_iota((SUB, LANES))
    got_ref[...] = crossed_ref[...] + near_ref[...]

    for b in range(pl.cdiv(full, wide)):
        low = 2 * (FEAT - 1) * b
        count = min(wide, full - b * wide) // LANES

        @pl.loop(0, count, unroll=2)
        def _(c):
            rim = got_ref[rows:, lanes_at(c)].astype(F32)
            at = lanes_at(c + b * (wide // LANES))
            feats = []
            for i, ref in ((0, k_ref), (1, v_ref)):
                moved = pltpu.roll(rim, (SUB - (FEAT - 1) * (i + 1) - low) % SUB, 0)
                x = jnp.where(iota >= SUB - (FEAT - 1), moved, ref[:SUB, at].astype(F32))
                feats.append(feature(x, taps_ref[i + 1, :, at]))
            edge_ref[:, at] = (feats[0] * feats[1]).astype(BF16)

    extra = out_ref.shape[0] - rows

    @pl.loop(0, width // LANES)
    def _(c):
        out_ref[:rows, lanes_at(c)] = own_ref[:, lanes_at(c)]
        tail = jnp.zeros((extra, LANES), F32)
        for b in range(pl.cdiv(full, width)):
            at = lanes_at(lax.rem(c + b * (width // LANES), full // LANES))
            one = jnp.broadcast_to(edge_ref[:, at].astype(F32)[1:2], (extra, LANES))
            tail = jnp.where(rows_iota((extra, LANES)) == b, one, tail)
        out_ref[rows:, lanes_at(c)] = tail.astype(BF16)


def last_gate(k, v, taps, crossed, near, own):
    rows, width = own.shape
    full = k.shape[1]
    extra = pl.cdiv(pl.cdiv(full, width), 8) * 8
    return pl.pallas_call(
        last_gate_kernel,
        in_specs=[VMEM] * 6,
        out_specs=[VMEM] * 3,
        out_shape=[
            jax.ShapeDtypeStruct((rows + extra, width), BF16),
            jax.ShapeDtypeStruct((SUB, full), BF16),
            jax.ShapeDtypeStruct(crossed.shape, BF16),
        ],
        compiler_params=params(12),
        cost_estimate=COST,
        name="gate_last",
    )(k, v, taps, crossed, near, own)


def turned_filters(h):
    i = rows_iota((FILT, FILT))
    j = lax.broadcasted_iota(jnp.int32, (FILT, FILT), 1)
    flip = (i + j == FILT) | ((i == 0) & (j == 0))
    return jnp.dot(h, flip.astype(BF16), preferred_element_type=F32)


def fill_mask(mask_ref):
    rows, cols = mask_ref.shape
    i = rows_iota((rows, cols))
    b = i // SUB * 8 + i % 8
    m = lax.broadcasted_iota(jnp.int32, (rows, cols), 1)
    mask_ref[...] = jnp.where((m > b) & (m <= b + FILT), 1.0, 0.0).astype(BF16)


def mix_tile(turned_ref, mask_ref, lhs_ref, own_ref, got_ref, edge_ref, q_ref, taps_ref, skip_ref, before, src, dst, c):
    rows = q_ref.shape[0]
    span = rows // WINDOWS
    per = LANES // GROUP_CH
    half = per // 2
    iota = rows_iota((SUB, LANES))
    lane_group = lax.broadcasted_iota(jnp.int32, (8, 2 * LANES), 1) % (LANES // 2) // GROUP_CH
    turned = turned_ref[pl.ds(pl.multiple_of(c * per, per), per), :]
    rings = []
    for g in range(per):
        row = jnp.broadcast_to(turned[g : g + 1], (span, FILT))
        rings.append(pltpu.roll(row, 0, 1, stride=1, stride_axis=0))
    low = 0
    for h in range(2):
        for r in range(span // 8):
            mask = mask_ref[r * SUB : (r + 1) * SUB]
            for g in range(h * half, (h + 1) * half, 2):
                pair = jnp.concatenate([rings[g][r * 8 : r * 8 + 8], rings[g + 1][r * 8 : r * 8 + 8]], axis=0)
                pair = pair.astype(BF16)
                lhs_ref[low : low + SUB, :] = jnp.concatenate([pair, pair], axis=1) * mask
                low += SUB
    own_head = jnp.where(iota < FEAT - 1, edge_ref[:, src].astype(F32), own_ref[:SUB, dst].astype(F32))
    got_head = got_ref[:SUB, dst].astype(F32)
    q_rim = got_head
    if before is None:
        got_head = jnp.where(iota < FEAT - 1, 0.0, got_head)
    else:
        got_head = jnp.where(iota < FEAT - 1, before, got_head)
    both = [got_head.astype(BF16)] + [got_ref[r : r + SUB, dst] for r in range(SUB, rows, SUB)]
    both += [own_head.astype(BF16)] + [own_ref[r : r + SUB, dst] for r in range(SUB, rows, SUB)]
    ahead = span // SUB
    count = len(both) - ahead
    sides = (slice(0, LANES // 2), slice(LANES // 2, LANES))
    halves = [
        [jnp.concatenate([both[i][:, side], both[i + ahead][:, side]], axis=1) for i in range(count)]
        for side in sides
    ]
    res = []
    for h, blocks in enumerate(halves):
        cols = [
            jnp.concatenate([blocks[min(w * ahead + i, count - 1)] for i in range(2 * FILT // SUB)], axis=0)
            for w in range(0, WINDOWS, 2)
        ]
        lhs = lhs_ref[h * half * span : (h + 1) * half * span, :]
        res.append(jnp.dot(lhs, jnp.concatenate(cols, axis=1), preferred_element_type=F32))
    parts = [[] for _ in range(WINDOWS)]
    for r in range(span // 8):
        totals = []
        for x in res:
            total = x[r * half * 8 : r * half * 8 + 8]
            for g in range(1, half):
                at = (r * half + g) * 8
                total = jnp.where(lane_group == g, x[at : at + 8], total)
            totals.append(total)
        for w in range(0, WINDOWS, 2):
            a, b = (t[:, w // 2 * LANES : (w // 2 + 1) * LANES] for t in totals)
            for i, side in enumerate(sides):
                parts[w + i].append(jnp.concatenate([a[:, side], b[:, side]], axis=1))
    conv = jnp.concatenate([x for part in parts for x in part], axis=0)
    cur = jnp.concatenate(both[rows // SUB :], axis=0).astype(F32)
    q = q_ref[:, src].astype(F32)
    taps = taps_ref[0, :, src]
    q_feat = taps[0:1] * q
    for d in range(1, FEAT):
        moved = pltpu.roll(q, d, 0)
        shifted = pltpu.roll(q_rim, (d - (FEAT - 1)) % SUB, 0)
        head = jnp.where(iota < d, shifted, moved[:SUB])
        q_feat = q_feat + taps[d : d + 1] * jnp.concatenate([head, moved[SUB:]], axis=0)
    return q_feat * (conv + skip_ref[:, src] * cur), q_feat, turned


def mix_kernel(first, has_out, turned_ref, mask_ref, own_ref, got_ref, edge_ref, q_ref, taps_ref, skip_ref, *refs):
    refs = refs[1:] if has_out else refs
    out_hbm, head_ref, slope_ref, res_ref, lhs_ref, sems = refs
    rows = q_ref.shape[0]
    width = res_ref.shape[1]
    per = LANES // GROUP_CH
    row_group = rows_iota((per, LANES))
    lane_group = lax.broadcasted_iota(jnp.int32, (per, LANES), 1) // GROUP_CH

    run = run_of(width // LANES)
    runs = width // LANES // run

    def store(p):
        here = pl.ds(pl.multiple_of(p * run * LANES, LANES), run * LANES)
        there = pl.ds(pl.multiple_of(first + p * run * LANES, LANES), run * LANES)
        return pltpu.make_async_copy(
            res_ref.at[:, here], out_hbm.at[pl.ds(SUB, rows - SUB), there], sems.at[p]
        )

    @pl.loop(0, runs)
    def _(p):
        for u in range(run):
            c = p * run + u
            dst = lanes_at(c)
            src = lanes_at(c + first // LANES)
            mixed, q_feat, turned = mix_tile(
                turned_ref, mask_ref, lhs_ref.at[u], own_ref, got_ref, edge_ref, q_ref, taps_ref, skip_ref, None, src, dst, c + first // LANES
            )
            res_ref[:, dst] = mixed[SUB:].astype(BF16)
            head_ref[:, dst] = mixed[:SUB]
            last_tap = jnp.where(row_group == lane_group, jnp.broadcast_to(turned[:, 1:2], (per, LANES)), 0.0)
            slope_ref[:, dst] = q_feat[:8] * jnp.sum(last_tap, axis=0, keepdims=True)
        store(p).start()

    @pl.loop(0, runs)
    def _(p):
        store(p).wait()


def mix(turned, mask, own, got, edges, q, taps, skip, out, first):
    rows, full = q.shape
    width = own.shape[1]
    run = run_of(width // LANES)
    per = LANES // GROUP_CH
    args = [turned, mask, own, got, edges, q, taps, skip]
    in_specs = [VMEM] * len(args)
    if out is not None:
        in_specs.append(HBM)
        args.append(out)
    return pl.pallas_call(
        functools.partial(mix_kernel, first, out is not None),
        in_specs=in_specs,
        out_specs=[HBM, VMEM, VMEM],
        out_shape=[
            jax.ShapeDtypeStruct((rows, full), BF16),
            jax.ShapeDtypeStruct((SUB, width), F32),
            jax.ShapeDtypeStruct((8, width), F32),
        ],
        scratch_shapes=[
            pltpu.VMEM((rows - SUB, width), BF16),
            pltpu.VMEM((run, per * rows // WINDOWS, 2 * FILT), BF16),
            pltpu.SemaphoreType.DMA((width // LANES // run,)),
        ],
        input_output_aliases={} if out is None else {len(args) - 1: 0},
        compiler_params=params(12),
        cost_estimate=COST,
        name="mix",
    )(*args)


def last_mix_kernel(first, parts, turned_ref, mask_ref, own_ref, got_ref, edge_ref, q_ref, taps_ref, skip_ref, *refs):
    heads, slopes = refs[:parts], refs[parts : 2 * parts]
    _, out_hbm, res_ref, top_ref, before_ref, lhs_ref, sems, top_sem = refs[2 * parts :]
    rows, full = q_ref.shape
    width = res_ref.shape[1]
    iota = rows_iota((SUB, LANES))

    for b in range(pl.cdiv(full, width)):
        count = min(width, full - b * width)
        before_ref[:, b * width : b * width + count] = got_ref[rows:, :count].astype(F32)[b : b + 1]

    at_first = 0
    for head_ref, slope_ref in zip(heads, slopes):
        wide = head_ref.shape[1]

        @pl.loop(0, wide // LANES, unroll=run_of(wide // LANES))
        def _(c):
            c_all = c + at_first // LANES
            head = head_ref[:, lanes_at(c)]
            more = slope_ref[:, lanes_at(c)] * before_ref[:, lanes_at(c_all)]
            more = jnp.concatenate([more, jnp.zeros_like(more)], axis=0)
            top_ref[:, lanes_at(c_all)] = jnp.where(iota == 0, head + more, head).astype(BF16)

        at_first += wide
    top = pltpu.make_async_copy(top_ref, out_hbm.at[pl.ds(0, SUB), pl.ds(0, first)], top_sem)
    top.start()

    run = run_of(width // LANES)
    runs = width // LANES // run

    def store(p):
        here = pl.ds(pl.multiple_of(p * run * LANES, LANES), run * LANES)
        there = pl.ds(pl.multiple_of(first + p * run * LANES, LANES), run * LANES)
        return pltpu.make_async_copy(res_ref.at[:, here], out_hbm.at[:, there], sems.at[p])

    @pl.loop(0, runs)
    def _(p):
        for u in range(run):
            c = p * run + u
            dst = lanes_at(c)
            src = lanes_at(c + first // LANES)
            before = before_ref[:, src]
            mixed, _, _ = mix_tile(
                turned_ref, mask_ref, lhs_ref.at[u], own_ref, got_ref, edge_ref, q_ref, taps_ref, skip_ref, before, src, dst, c + first // LANES
            )
            res_ref[:, dst] = mixed.astype(BF16)
        store(p).start()

    @pl.loop(0, runs)
    def _(p):
        store(p).wait()

    top.wait()


def last_mix(turned, mask, own, got, edges, q, taps, skip, heads, slopes, out, first):
    rows, full = q.shape
    width = own.shape[1]
    run = run_of(width // LANES)
    per = LANES // GROUP_CH
    args = [turned, mask, own, got, edges, q, taps, skip, *heads, *slopes, out]
    return pl.pallas_call(
        functools.partial(last_mix_kernel, first, len(heads)),
        in_specs=[VMEM] * (len(args) - 1) + [HBM],
        out_specs=HBM,
        out_shape=jax.ShapeDtypeStruct((rows, full), BF16),
        scratch_shapes=[
            pltpu.VMEM((rows, width), BF16),
            pltpu.VMEM((SUB, first), BF16),
            pltpu.VMEM((1, full), F32),
            pltpu.VMEM((run, per * rows // WINDOWS, 2 * FILT), BF16),
            pltpu.SemaphoreType.DMA((width // LANES // run,)),
            pltpu.SemaphoreType.DMA,
        ],
        input_output_aliases={len(args) - 1: 0},
        compiler_params=params(12),
        cost_estimate=COST,
        name="mix_last",
    )(*args)


def shards(q_stream, k_stream, v_stream, feat_filter, long_filter, skip_gain):
    rows, width = q_stream.shape
    skip = skip_gain.reshape(1, width)
    unit = width // 32
    sizes = [9 * unit, 10 * unit, 9 * unit, 4 * unit]
    starts = [sum(sizes[:i]) for i in range(len(sizes))]
    streams = (k_stream, v_stream, q_stream, feat_filter)
    begun = first_gate(*streams, sizes[0])
    crossed = passed_along(begun, 1, 2)
    own = list(second_gate(*streams, begun, starts[1], sizes[1]))
    near = passed_along(own[0], 0, 2)
    got = [None, passed_along(own[1])]
    turned, mask, more, last = gate(*streams, long_filter, own[1], starts[2:], sizes[2:])
    own.append(more)
    got.append(passed_along(more))
    last, edges, got[0] = last_gate(k_stream, v_stream, feat_filter, settle(crossed), near, last)
    own.append(last)
    got.append(passed_along(last))
    out = None
    heads = []
    slopes = []
    for first, a, b in zip(starts[:3], own, got):
        out, head, slope = mix(turned, mask, a, b, edges, q_stream, feat_filter, skip, out, first)
        heads.append(head)
        slopes.append(slope)
    return last_mix(
        turned, mask, own[3], got[3], edges, q_stream, feat_filter, skip, heads, slopes, out, starts[3]
    )


def solution(mesh):
    in_specs = (
        P(("rep", "seq"), None),
        P(("rep", "seq"), None),
        P(("rep", "seq"), None),
        P(),
        P(),
        P(),
    )
    out_specs = P(("rep", "seq"), None)
    return jax.shard_map(shards, mesh=mesh, in_specs=in_specs, out_specs=out_specs, check_vma=False)
```

```python
import functools

import jax
import jax.numpy as jnp
from jax import lax
from jax.experimental import pallas as pl
from jax.experimental.pallas import tpu as pltpu
from jax.sharding import PartitionSpec as P

GROUP_CH = 16
FILT = 128
FEAT = 3
LANES = 128
SUB = 16
WINDOWS = 4
MIB = 1 << 20
F32 = jnp.float32
BF16 = jnp.bfloat16
VMEM = pl.BlockSpec(memory_space=pltpu.VMEM)
HBM = pl.BlockSpec(memory_space=pltpu.HBM)
COST = pl.CostEstimate(flops=1000, bytes_accessed=1000, transcendentals=0)


def passed_along(shard, first=0, step=1):
    length = lax.axis_size("seq")
    return lax.ppermute(shard, "seq", [(i, i + 1) for i in range(first, length - 1, step)])


def sends_first():
    return lax.rem(lax.axis_index("seq"), 2) == 1


def feature(x, taps):
    total = taps[0:1] * x
    for j in range(1, FEAT):
        total = total + taps[j : j + 1] * pltpu.roll(x, j, 0)
    return total


def rows_iota(shape):
    return lax.broadcasted_iota(jnp.int32, shape, 0)


def lanes_at(c):
    return pl.ds(c * LANES if isinstance(c, int) else pl.multiple_of(c * LANES, LANES), LANES)


def in_hbm(x):
    return pltpu.with_memory_space_constraint(x, pltpu.HBM)


def run_of(tiles, most=10):
    return max(n for n in range(1, most + 1) if tiles % n == 0)


def params(mib):
    return pltpu.CompilerParams(vmem_limit_bytes=mib * MIB)


def gate_tile(k, v, taps, at):
    return feature(k.astype(F32), taps[1, :, at]) * feature(v.astype(F32), taps[2, :, at])


def gate_piece(k_ref, v_ref, q_tail, taps_ref, out_ref, src, dst, at):
    rows = k_ref.shape[0]
    gated = gate_tile(k_ref[:, src], v_ref[:, src], taps_ref, at)
    tail = pltpu.roll(q_tail.astype(F32), FEAT - 1, 0)
    head = jnp.where(rows_iota((SUB, LANES)) < FEAT - 1, tail, gated[:SUB])
    out_ref[:SUB, dst] = head.astype(BF16)
    out_ref[SUB:rows, dst] = gated[SUB:].astype(BF16)


def rim_rows(kt_ref, vt_ref, out_ref):
    full = kt_ref.shape[1]
    rows, width = out_ref.shape
    last = kt_ref.shape[0] - SUB
    iota = rows_iota((SUB, LANES))

    @pl.loop(0, width // LANES, unroll=2)
    def _(c):
        tail = jnp.zeros((SUB, LANES), F32)
        for b in range(pl.cdiv(full, width)):
            low = 2 * (FEAT - 1) * b
            at = lanes_at(lax.rem(c + b * (width // LANES), full // LANES))
            kt = pltpu.roll(kt_ref[last:, at].astype(F32), (low + FEAT - 1) % SUB, 0)
            vt = pltpu.roll(vt_ref[last:, at].astype(F32), (low + 2 * (FEAT - 1)) % SUB, 0)
            tail = jnp.where((iota >= low) & (iota < low + FEAT - 1), kt, tail)
            tail = jnp.where((iota >= low + FEAT - 1) & (iota < low + 2 * (FEAT - 1)), vt, tail)
        out_ref[rows - SUB :, lanes_at(c)] = tail.astype(BF16)


def first_gate_kernel(*refs):
    @pl.when(sends_first())
    def _():
        first_gate_body(*refs)


def first_gate_body(k_hbm, v_hbm, q_hbm, taps_hbm, out_ref, k_ref, v_ref, taps_ref, qt_ref, kt_ref, vt_ref, sems):
    rows, width = k_ref.shape
    run = run_of(width // LANES, 5)
    pieces = width // LANES // run
    last = pl.ds(rows - SUB, SUB)

    def load(p, ref, hbm, i):
        at = pl.ds(p * run * LANES, run * LANES)
        return pltpu.make_async_copy(hbm.at[:, at], ref.at[:, at], sems.at[2 * p + i])

    rest = [
        pltpu.make_async_copy(taps_hbm.at[:, :, pl.ds(0, width)], taps_ref, sems.at[2 * pieces]),
        pltpu.make_async_copy(q_hbm.at[last, pl.ds(0, width)], qt_ref, sems.at[2 * pieces + 1]),
        pltpu.make_async_copy(k_hbm.at[last], kt_ref, sems.at[2 * pieces + 2]),
        pltpu.make_async_copy(v_hbm.at[last], vt_ref, sems.at[2 * pieces + 3]),
    ]
    rest[0].start()
    rest[1].start()
    for p in range(pieces):
        load(p, k_ref, k_hbm, 0).start()
        load(p, v_ref, v_hbm, 1).start()
    rest[2].start()
    rest[3].start()
    rest[0].wait()
    rest[1].wait()
    for p in range(pieces):
        load(p, k_ref, k_hbm, 0).wait()
        load(p, v_ref, v_hbm, 1).wait()

        @pl.loop(0, run, unroll=run)
        def _(c):
            at = lanes_at(c + p * run)
            gate_piece(k_ref, v_ref, qt_ref[:, at], taps_ref, out_ref, at, at, at)

    rest[2].wait()
    rest[3].wait()
    rim_rows(kt_ref, vt_ref, out_ref)


def first_gate(k, v, q, taps, width):
    rows, full = k.shape
    return pl.pallas_call(
        first_gate_kernel,
        in_specs=[HBM] * 4,
        out_specs=VMEM,
        out_shape=jax.ShapeDtypeStruct((rows + SUB, width), BF16),
        scratch_shapes=[
            pltpu.VMEM((rows, width), BF16),
            pltpu.VMEM((rows, width), BF16),
            pltpu.VMEM((3, FEAT, width), F32),
            pltpu.VMEM((SUB, width), BF16),
            pltpu.VMEM((SUB, full), BF16),
            pltpu.VMEM((SUB, full), BF16),
            pltpu.SemaphoreType.DMA((2 * (width // LANES // run_of(width // LANES, 5)) + 4,)),
        ],
        compiler_params=params(12),
        cost_estimate=COST,
        name="gate_first",
    )(*(in_hbm(x) for x in (k, v, q, taps)))


def gate_block(k_ref, v_ref, q_ref, taps_ref, out_ref, first):
    rows = k_ref.shape[0]

    @pl.loop(0, out_ref.shape[1] // LANES, unroll=2)
    def _(c):
        at = lanes_at(c + first // LANES)
        gate_piece(k_ref, v_ref, q_ref[rows - SUB :, at], taps_ref, out_ref, at, lanes_at(c), at)


def second_gate_kernel(first, k_ref, v_ref, q_ref, taps_ref, begun_ref, out_ref, more_ref):
    begun = sends_first()

    @pl.when(begun)
    def _():
        out_ref[...] = begun_ref[...]

    @pl.when(jnp.logical_not(begun))
    def _():
        gate_block(k_ref, v_ref, q_ref, taps_ref, out_ref, 0)
        rim_rows(k_ref, v_ref, out_ref)

    gate_block(k_ref, v_ref, q_ref, taps_ref, more_ref, first)


def second_gate(k, v, q, taps, begun, first, width):
    return pl.pallas_call(
        functools.partial(second_gate_kernel, first),
        in_specs=[VMEM] * 5,
        out_specs=[VMEM] * 2,
        out_shape=[
            jax.ShapeDtypeStruct(begun.shape, BF16),
            jax.ShapeDtypeStruct((k.shape[0], width), BF16),
        ],
        compiler_params=params(12),
        cost_estimate=COST,
        name="gate_second",
    )(k, v, q, taps, begun)


def gate_kernel(firsts, k_ref, v_ref, q_ref, taps_ref, h_ref, _, turned_ref, mask_ref, *out_refs):
    for first, out_ref in zip(firsts, out_refs):
        gate_block(k_ref, v_ref, q_ref, taps_ref, out_ref, first)
    turned_ref[...] = turned_filters(h_ref[...])
    fill_mask(mask_ref)


def gate(k, v, q, taps, h, after, firsts, widths):
    rows = k.shape[0]
    return pl.pallas_call(
        functools.partial(gate_kernel, firsts),
        in_specs=[VMEM] * 5 + [pl.BlockSpec(memory_space=pl.ANY)],
        out_specs=[VMEM] * (len(widths) + 2),
        out_shape=[jax.ShapeDtypeStruct(h.shape, F32), jax.ShapeDtypeStruct((2 * rows // WINDOWS, 2 * FILT), BF16)]
        + [jax.ShapeDtypeStruct((rows, w), BF16) for w in widths],
        compiler_params=params(12),
        cost_estimate=COST,
        name="gate",
    )(k, v, q, taps, h, after)


def settle_kernel(in_ref, out_ref):
    out_ref[...] = in_ref[...]


def settle(x):
    return pl.pallas_call(
        settle_kernel,
        in_specs=[VMEM],
        out_specs=VMEM,
        out_shape=jax.ShapeDtypeStruct(x.shape, x.dtype),
        compiler_params=params(12),
        cost_estimate=COST,
        name="settle",
    )(x)


def last_gate_kernel(k_ref, v_ref, taps_ref, crossed_ref, near_ref, own_ref, out_ref, edge_ref, got_ref):
    rows, width = own_ref.shape
    full = k_ref.shape[1]
    wide = got_ref.shape[1]
    iota = rows_iota((SUB, LANES))
    got_ref[...] = crossed_ref[...] + near_ref[...]

    for b in range(pl.cdiv(full, wide)):
        low = 2 * (FEAT - 1) * b
        count = min(wide, full - b * wide) // LANES

        @pl.loop(0, count, unroll=2)
        def _(c):
            rim = got_ref[rows:, lanes_at(c)].astype(F32)
            at = lanes_at(c + b * (wide // LANES))
            feats = []
            for i, ref in ((0, k_ref), (1, v_ref)):
                moved = pltpu.roll(rim, (SUB - (FEAT - 1) * (i + 1) - low) % SUB, 0)
                x = jnp.where(iota >= SUB - (FEAT - 1), moved, ref[:SUB, at].astype(F32))
                feats.append(feature(x, taps_ref[i + 1, :, at]))
            edge_ref[:, at] = (feats[0] * feats[1]).astype(BF16)

    extra = out_ref.shape[0] - rows

    @pl.loop(0, width // LANES)
    def _(c):
        out_ref[:rows, lanes_at(c)] = own_ref[:, lanes_at(c)]
        tail = jnp.zeros((extra, LANES), F32)
        for b in range(pl.cdiv(full, width)):
            at = lanes_at(lax.rem(c + b * (width // LANES), full // LANES))
            one = jnp.broadcast_to(edge_ref[:, at].astype(F32)[1:2], (extra, LANES))
            tail = jnp.where(rows_iota((extra, LANES)) == b, one, tail)
        out_ref[rows:, lanes_at(c)] = tail.astype(BF16)


def last_gate(k, v, taps, crossed, near, own):
    rows, width = own.shape
    full = k.shape[1]
    extra = pl.cdiv(pl.cdiv(full, width), 8) * 8
    return pl.pallas_call(
        last_gate_kernel,
        in_specs=[VMEM] * 6,
        out_specs=[VMEM] * 3,
        out_shape=[
            jax.ShapeDtypeStruct((rows + extra, width), BF16),
            jax.ShapeDtypeStruct((SUB, full), BF16),
            jax.ShapeDtypeStruct(crossed.shape, BF16),
        ],
        compiler_params=params(12),
        cost_estimate=COST,
        name="gate_last",
    )(k, v, taps, crossed, near, own)


def turned_filters(h):
    i = rows_iota((FILT, FILT))
    j = lax.broadcasted_iota(jnp.int32, (FILT, FILT), 1)
    flip = (i + j == FILT) | ((i == 0) & (j == 0))
    return jnp.dot(h, flip.astype(BF16), preferred_element_type=F32)


def fill_mask(mask_ref):
    rows, cols = mask_ref.shape
    i = rows_iota((rows, cols))
    b = i // SUB * 8 + i % 8
    m = lax.broadcasted_iota(jnp.int32, (rows, cols), 1)
    mask_ref[...] = jnp.where((m > b) & (m <= b + FILT), 1.0, 0.0).astype(BF16)


def toeplitz_rows(turned, mask_ref, lhs_ref):
    span = mask_ref.shape[0] // 2
    per = LANES // GROUP_CH
    half = per // 2
    rings = []
    for g in range(per):
        row = jnp.broadcast_to(turned[g : g + 1], (span, FILT))
        rings.append(pltpu.roll(row, 0, 1, stride=1, stride_axis=0))
    low = 0
    for h in range(2):
        for r in range(span // 8):
            mask = mask_ref[r * SUB : (r + 1) * SUB]
            for g in range(h * half, (h + 1) * half, 2):
                pair = jnp.concatenate([rings[g][r * 8 : r * 8 + 8], rings[g + 1][r * 8 : r * 8 + 8]], axis=0)
                pair = pair.astype(BF16)
                lhs_ref[low : low + SUB, :] = jnp.concatenate([pair, pair], axis=1) * mask
                low += SUB


def own_feature(q, taps):
    iota = rows_iota((SUB, LANES))
    total = taps[0:1] * q
    for d in range(1, FEAT):
        moved = pltpu.roll(q, d, 0)
        head = jnp.where(iota < d, 0.0, moved[:SUB])
        total = total + taps[d : d + 1] * jnp.concatenate([head, moved[SUB:]], axis=0)
    return total


def prepare_kernel(firsts, turned_ref, mask_ref, q_ref, taps_ref, *out_refs):
    per = LANES // GROUP_CH
    for i, first in enumerate(firsts):
        lhs_ref, feat_ref = out_refs[2 * i : 2 * i + 2]
        tiles = lhs_ref.shape[0]

        @pl.loop(0, tiles, unroll=run_of(tiles, 4))
        def _(c):
            c_all = c + first // LANES
            src = lanes_at(c_all)
            toeplitz_rows(turned_ref[pl.ds(pl.multiple_of(c_all * per, per), per), :], mask_ref, lhs_ref.at[c])
            feat_ref[:, lanes_at(c)] = own_feature(q_ref[:, src].astype(F32), taps_ref[0, :, src])


def prepare(turned, mask, q, taps, firsts, widths):
    rows = q.shape[0]
    lhs = LANES // GROUP_CH * rows // WINDOWS
    return pl.pallas_call(
        functools.partial(prepare_kernel, firsts),
        in_specs=[VMEM] * 4,
        out_specs=[VMEM] * (2 * len(widths)),
        out_shape=[
            shape
            for w in widths
            for shape in (
                jax.ShapeDtypeStruct((w // LANES, lhs, 2 * FILT), BF16),
                jax.ShapeDtypeStruct((rows, w), F32),
            )
        ],
        compiler_params=params(12),
        cost_estimate=COST,
        name="prepare",
    )(turned, mask, q, taps)


def mix_tile(turned_ref, mask_ref, lhs_ref, feat_ref, own_ref, got_ref, edge_ref, q_ref, taps_ref, skip_ref, before, src, dst, c):
    rows = q_ref.shape[0]
    span = rows // WINDOWS
    per = LANES // GROUP_CH
    half = per // 2
    iota = rows_iota((SUB, LANES))
    lane_group = lax.broadcasted_iota(jnp.int32, (8, 2 * LANES), 1) % (LANES // 2) // GROUP_CH
    turned = turned_ref[pl.ds(c * per if isinstance(c, int) else pl.multiple_of(c * per, per), per), :]
    taps = taps_ref[0, :, src]
    if feat_ref is None:
        toeplitz_rows(turned, mask_ref, lhs_ref)
        q_feat = own_feature(q_ref[:, src].astype(F32), taps)
    else:
        q_feat = feat_ref[:, dst]
    own_head = jnp.where(iota < FEAT - 1, edge_ref[:, src].astype(F32), own_ref[:SUB, dst].astype(F32))
    got_head = got_ref[:SUB, dst].astype(F32)
    q_rim = got_head
    if before is None:
        got_head = jnp.where(iota < FEAT - 1, 0.0, got_head)
    else:
        got_head = jnp.where(iota < FEAT - 1, before, got_head)
    both = [got_head.astype(BF16)] + [got_ref[r : r + SUB, dst] for r in range(SUB, rows, SUB)]
    both += [own_head.astype(BF16)] + [own_ref[r : r + SUB, dst] for r in range(SUB, rows, SUB)]
    ahead = span // SUB
    count = len(both) - ahead
    sides = (slice(0, LANES // 2), slice(LANES // 2, LANES))
    halves = [
        [jnp.concatenate([both[i][:, side], both[i + ahead][:, side]], axis=1) for i in range(count)]
        for side in sides
    ]
    res = []
    for h, blocks in enumerate(halves):
        cols = [
            jnp.concatenate([blocks[min(w * ahead + i, count - 1)] for i in range(2 * FILT // SUB)], axis=0)
            for w in range(0, WINDOWS, 2)
        ]
        lhs = lhs_ref[h * half * span : (h + 1) * half * span, :]
        res.append(jnp.dot(lhs, jnp.concatenate(cols, axis=1), preferred_element_type=F32))
    parts = [[] for _ in range(WINDOWS)]
    for r in range(span // 8):
        totals = []
        for x in res:
            total = x[r * half * 8 : r * half * 8 + 8]
            for g in range(1, half):
                at = (r * half + g) * 8
                total = jnp.where(lane_group == g, x[at : at + 8], total)
            totals.append(total)
        for w in range(0, WINDOWS, 2):
            a, b = (t[:, w // 2 * LANES : (w // 2 + 1) * LANES] for t in totals)
            for i, side in enumerate(sides):
                parts[w + i].append(jnp.concatenate([a[:, side], b[:, side]], axis=1))
    conv = jnp.concatenate([x for part in parts for x in part], axis=0)
    cur = jnp.concatenate(both[rows // SUB :], axis=0).astype(F32)
    head = q_feat[:SUB]
    for d in range(1, FEAT):
        shifted = pltpu.roll(q_rim, (d - (FEAT - 1)) % SUB, 0)
        head = head + taps[d : d + 1] * jnp.where(iota < d, shifted, 0.0)
    q_feat = jnp.concatenate([head, q_feat[SUB:]], axis=0)
    return q_feat * (conv + skip_ref[:, src] * cur), q_feat, turned


def mix_kernel(first, has_out, has_ready, has_after, turned_ref, mask_ref, own_ref, got_ref, edge_ref, q_ref, taps_ref, skip_ref, *refs):
    refs = refs[has_out + has_after :]
    feat_ref = None
    if has_ready:
        lhs_ref, feat_ref, *refs = refs
    out_hbm, head_ref, slope_ref, res_ref, *lhs, sems = refs
    lhs_ref = lhs_ref if has_ready else lhs[0]
    rows = q_ref.shape[0]
    width = res_ref.shape[1]
    per = LANES // GROUP_CH
    row_group = rows_iota((per, LANES))
    lane_group = lax.broadcasted_iota(jnp.int32, (per, LANES), 1) // GROUP_CH

    run = run_of(width // LANES)
    runs = width // LANES // run

    def store(p):
        here = pl.ds(pl.multiple_of(p * run * LANES, LANES), run * LANES)
        there = pl.ds(pl.multiple_of(first + p * run * LANES, LANES), run * LANES)
        return pltpu.make_async_copy(
            res_ref.at[:, here], out_hbm.at[pl.ds(SUB, rows - SUB), there], sems.at[p]
        )

    @pl.loop(0, runs)
    def _(p):
        for u in range(run):
            c = p * run + u
            dst = lanes_at(c)
            src = lanes_at(c + first // LANES)
            mixed, q_feat, turned = mix_tile(
                turned_ref,
                mask_ref,
                lhs_ref.at[c if has_ready else u],
                feat_ref,
                own_ref,
                got_ref,
                edge_ref,
                q_ref,
                taps_ref,
                skip_ref,
                None,
                src,
                dst,
                c + first // LANES,
            )
            res_ref[:, dst] = mixed[SUB:].astype(BF16)
            head_ref[:, dst] = mixed[:SUB]
            last_tap = jnp.where(row_group == lane_group, jnp.broadcast_to(turned[:, 1:2], (per, LANES)), 0.0)
            slope = q_feat[:8] * jnp.sum(last_tap, axis=0, keepdims=True)
            slope_ref[:, dst] = jnp.where(rows_iota((8, LANES)) == 0, slope, 0.0)
        store(p).start()

    @pl.loop(0, runs)
    def _(p):
        store(p).wait()


def mix(turned, mask, own, got, edges, q, taps, skip, out, first, ready=(), after=None):
    rows, full = q.shape
    width = own.shape[1]
    run = run_of(width // LANES)
    per = LANES // GROUP_CH
    args = [turned, mask, own, got, edges, q, taps, skip]
    in_specs = [VMEM] * len(args)
    aliases = {}
    if out is not None:
        aliases = {len(args): 0}
        in_specs.append(HBM)
        args.append(out)
    if after is not None:
        in_specs.append(pl.BlockSpec(memory_space=pl.ANY))
        args.append(after)
    in_specs += [VMEM] * len(ready)
    args += ready
    scratch = [] if ready else [pltpu.VMEM((run, per * rows // WINDOWS, 2 * FILT), BF16)]
    return pl.pallas_call(
        functools.partial(mix_kernel, first, out is not None, len(ready) > 0, after is not None),
        in_specs=in_specs,
        out_specs=[HBM, VMEM, VMEM],
        out_shape=[
            jax.ShapeDtypeStruct((rows, full), BF16),
            jax.ShapeDtypeStruct((SUB, width), F32),
            jax.ShapeDtypeStruct((8, width), F32),
        ],
        scratch_shapes=[
            pltpu.VMEM((rows - SUB, width), BF16),
            *scratch,
            pltpu.SemaphoreType.DMA((width // LANES // run,)),
        ],
        input_output_aliases=aliases,
        compiler_params=params(12),
        cost_estimate=COST,
        name="mix",
    )(*args)


def last_mix_kernel(first, parts, turned_ref, mask_ref, own_ref, got_ref, edge_ref, q_ref, taps_ref, skip_ref, *refs):
    heads, slopes = refs[:parts], refs[parts : 2 * parts]
    lhs_ref, feat_ref, _, out_hbm, res_ref, top_ref, sems = refs[2 * parts :]
    rows = q_ref.shape[0]
    tiles = res_ref.shape[1] // LANES
    mine = first // LANES
    before = [got_ref[rows:, lanes_at(c)].astype(F32) for c in range(tiles)]

    def before_at(c_all):
        return before[c_all % tiles][c_all // tiles : c_all // tiles + 1]

    c_all = 0
    for head_ref, slope_ref in zip(heads, slopes):
        for c in range(head_ref.shape[1] // LANES):
            at = lanes_at(c)
            head = head_ref[:, at]
            changed = head[:8] + slope_ref[:, at] * before_at(c_all)
            top_ref[:, lanes_at(c_all)] = jnp.concatenate([changed, head[8:]], axis=0).astype(BF16)
            c_all += 1
    top = pltpu.make_async_copy(top_ref, out_hbm.at[pl.ds(0, SUB), pl.ds(0, first)], sems.at[0])
    top.start()
    for c in range(tiles):
        dst = lanes_at(c)
        mixed, _, _ = mix_tile(
            turned_ref,
            mask_ref,
            lhs_ref.at[c],
            feat_ref,
            own_ref,
            got_ref,
            edge_ref,
            q_ref,
            taps_ref,
            skip_ref,
            before_at(c + mine),
            lanes_at(c + mine),
            dst,
            c + mine,
        )
        res_ref[:, dst] = mixed.astype(BF16)
    copy = pltpu.make_async_copy(res_ref, out_hbm.at[:, pl.ds(first, tiles * LANES)], sems.at[1])
    copy.start()
    top.wait()
    copy.wait()


def last_mix(turned, mask, own, got, edges, q, taps, skip, heads, slopes, ready, out, first):
    rows, full = q.shape
    width = own.shape[1]
    args = [turned, mask, own, got, edges, q, taps, skip, *heads, *slopes, *ready, out]
    return pl.pallas_call(
        functools.partial(last_mix_kernel, first, len(heads)),
        in_specs=[VMEM] * (len(args) - 1) + [HBM],
        out_specs=HBM,
        out_shape=jax.ShapeDtypeStruct((rows, full), BF16),
        scratch_shapes=[
            pltpu.VMEM((rows, width), BF16),
            pltpu.VMEM((SUB, first), BF16),
            pltpu.SemaphoreType.DMA((2,)),
        ],
        input_output_aliases={len(args) - 1: 0},
        compiler_params=params(12),
        cost_estimate=COST,
        name="mix_last",
    )(*args)


def shards(q_stream, k_stream, v_stream, feat_filter, long_filter, skip_gain):
    rows, width = q_stream.shape
    skip = skip_gain.reshape(1, width)
    unit = width // 32
    sizes = [9 * unit, 10 * unit, 9 * unit, 4 * unit]
    starts = [sum(sizes[:i]) for i in range(len(sizes))]
    streams = (k_stream, v_stream, q_stream, feat_filter)
    begun = first_gate(*streams, sizes[0])
    crossed = passed_along(begun, 1, 2)
    own = list(second_gate(*streams, begun, starts[1], sizes[1]))
    near = passed_along(own[0], 0, 2)
    got = [None, passed_along(own[1])]
    turned, mask, more, last = gate(*streams, long_filter, own[1], starts[2:], sizes[2:])
    own.append(more)
    got.append(passed_along(more))
    last, edges, got[0] = last_gate(k_stream, v_stream, feat_filter, settle(crossed), near, last)
    own.append(last)
    got.append(passed_along(last))
    ready = prepare(turned, mask, q_stream, feat_filter, starts[2:], sizes[2:])
    rest = (edges, q_stream, feat_filter, skip)
    out = None
    heads = []
    slopes = []
    more = ({}, {"after": ready[3]}, {"ready": ready[:2]})
    for first, a, b, m in zip(starts[:3], own, got, more):
        out, head, slope = mix(turned, mask, a, b, *rest, out, first, **m)
        heads.append(head)
        slopes.append(slope)
    return last_mix(turned, mask, own[3], got[3], *rest, heads, slopes, ready[2:], out, starts[3])


def solution(mesh):
    in_specs = (
        P(("rep", "seq"), None),
        P(("rep", "seq"), None),
        P(("rep", "seq"), None),
        P(),
        P(),
        P(),
    )
    out_specs = P(("rep", "seq"), None)
    return jax.shard_map(shards, mesh=mesh, in_specs=in_specs, out_specs=out_specs, check_vma=False)
```

```python
import functools

import jax
import jax.numpy as jnp
from jax import lax
from jax.experimental import pallas as pl
from jax.experimental.pallas import tpu as pltpu
from jax.sharding import PartitionSpec as P

GROUP_CH = 16
FILT = 128
FEAT = 3
LANES = 128
SUB = 16
WINDOWS = 4
MIB = 1 << 20
F32 = jnp.float32
BF16 = jnp.bfloat16
VMEM = pl.BlockSpec(memory_space=pltpu.VMEM)
HBM = pl.BlockSpec(memory_space=pltpu.HBM)
COST = pl.CostEstimate(flops=1000, bytes_accessed=1000, transcendentals=0)


def passed_along(shard, first=0, step=1):
    length = lax.axis_size("seq")
    return lax.ppermute(shard, "seq", [(i, i + 1) for i in range(first, length - 1, step)])


def sends_first():
    return lax.rem(lax.axis_index("seq"), 2) == 1


def feature(x, taps):
    total = taps[0:1] * x
    for j in range(1, FEAT):
        total = total + taps[j : j + 1] * pltpu.roll(x, j, 0)
    return total


def rows_iota(shape):
    return lax.broadcasted_iota(jnp.int32, shape, 0)


def lanes_at(c):
    return pl.ds(c * LANES if isinstance(c, int) else pl.multiple_of(c * LANES, LANES), LANES)


def in_hbm(x):
    return pltpu.with_memory_space_constraint(x, pltpu.HBM)


def run_of(tiles, most=12):
    return max(n for n in range(1, most + 1) if tiles % n == 0)


def params(mib):
    return pltpu.CompilerParams(vmem_limit_bytes=mib * MIB)


def gate_tile(k, v, taps, at):
    return feature(k.astype(F32), taps[1, :, at]) * feature(v.astype(F32), taps[2, :, at])


def gate_piece(k_ref, v_ref, q_tail, taps_ref, out_ref, src, dst, at):
    rows = k_ref.shape[0]
    gated = gate_tile(k_ref[:, src], v_ref[:, src], taps_ref, at)
    tail = pltpu.roll(q_tail.astype(F32), FEAT - 1, 0)
    head = jnp.where(rows_iota((SUB, LANES)) < FEAT - 1, tail, gated[:SUB])
    out_ref[:SUB, dst] = head.astype(BF16)
    out_ref[SUB:rows, dst] = gated[SUB:].astype(BF16)


def rim_rows(kt_ref, vt_ref, out_ref):
    full = kt_ref.shape[1]
    rows, width = out_ref.shape
    last = kt_ref.shape[0] - SUB
    iota = rows_iota((SUB, LANES))

    @pl.loop(0, width // LANES, unroll=2)
    def _(c):
        tail = jnp.zeros((SUB, LANES), F32)
        for b in range(pl.cdiv(full, width)):
            low = 2 * (FEAT - 1) * b
            at = lanes_at(lax.rem(c + b * (width // LANES), full // LANES))
            kt = pltpu.roll(kt_ref[last:, at].astype(F32), (low + FEAT - 1) % SUB, 0)
            vt = pltpu.roll(vt_ref[last:, at].astype(F32), (low + 2 * (FEAT - 1)) % SUB, 0)
            tail = jnp.where((iota >= low) & (iota < low + FEAT - 1), kt, tail)
            tail = jnp.where((iota >= low + FEAT - 1) & (iota < low + 2 * (FEAT - 1)), vt, tail)
        out_ref[rows - SUB :, lanes_at(c)] = tail.astype(BF16)


def first_gate_kernel(*refs):
    @pl.when(sends_first())
    def _():
        first_gate_body(*refs)


def first_gate_body(k_hbm, v_hbm, q_hbm, taps_hbm, out_ref, k_ref, v_ref, taps_ref, qt_ref, kt_ref, vt_ref, sems):
    rows, width = k_ref.shape
    run = run_of(width // LANES, 5)
    pieces = width // LANES // run
    last = pl.ds(rows - SUB, SUB)

    def load(p, ref, hbm, i):
        at = pl.ds(p * run * LANES, run * LANES)
        return pltpu.make_async_copy(hbm.at[:, at], ref.at[:, at], sems.at[2 * p + i])

    rest = [
        pltpu.make_async_copy(taps_hbm.at[:, :, pl.ds(0, width)], taps_ref, sems.at[2 * pieces]),
        pltpu.make_async_copy(q_hbm.at[last, pl.ds(0, width)], qt_ref, sems.at[2 * pieces + 1]),
        pltpu.make_async_copy(k_hbm.at[last], kt_ref, sems.at[2 * pieces + 2]),
        pltpu.make_async_copy(v_hbm.at[last], vt_ref, sems.at[2 * pieces + 3]),
    ]
    rest[0].start()
    rest[1].start()
    for p in range(pieces):
        load(p, k_ref, k_hbm, 0).start()
        load(p, v_ref, v_hbm, 1).start()
    rest[2].start()
    rest[3].start()
    rest[0].wait()
    rest[1].wait()
    for p in range(pieces):
        load(p, k_ref, k_hbm, 0).wait()
        load(p, v_ref, v_hbm, 1).wait()

        @pl.loop(0, run, unroll=run)
        def _(c):
            at = lanes_at(c + p * run)
            gate_piece(k_ref, v_ref, qt_ref[:, at], taps_ref, out_ref, at, at, at)

    rest[2].wait()
    rest[3].wait()
    rim_rows(kt_ref, vt_ref, out_ref)


def first_gate(k, v, q, taps, width):
    rows, full = k.shape
    return pl.pallas_call(
        first_gate_kernel,
        in_specs=[HBM] * 4,
        out_specs=VMEM,
        out_shape=jax.ShapeDtypeStruct((rows + SUB, width), BF16),
        scratch_shapes=[
            pltpu.VMEM((rows, width), BF16),
            pltpu.VMEM((rows, width), BF16),
            pltpu.VMEM((3, FEAT, width), F32),
            pltpu.VMEM((SUB, width), BF16),
            pltpu.VMEM((SUB, full), BF16),
            pltpu.VMEM((SUB, full), BF16),
            pltpu.SemaphoreType.DMA((2 * (width // LANES // run_of(width // LANES, 5)) + 4,)),
        ],
        compiler_params=params(12),
        cost_estimate=COST,
        name="gate_first",
    )(*(in_hbm(x) for x in (k, v, q, taps)))


def gate_block(k_ref, v_ref, q_ref, taps_ref, out_ref, first):
    rows = k_ref.shape[0]

    @pl.loop(0, out_ref.shape[1] // LANES, unroll=2)
    def _(c):
        at = lanes_at(c + first // LANES)
        gate_piece(k_ref, v_ref, q_ref[rows - SUB :, at], taps_ref, out_ref, at, lanes_at(c), at)


def second_gate_kernel(first, k_ref, v_ref, q_ref, taps_ref, begun_ref, out_ref, more_ref):
    begun = sends_first()

    @pl.when(begun)
    def _():
        out_ref[...] = begun_ref[...]

    @pl.when(jnp.logical_not(begun))
    def _():
        gate_block(k_ref, v_ref, q_ref, taps_ref, out_ref, 0)
        rim_rows(k_ref, v_ref, out_ref)

    gate_block(k_ref, v_ref, q_ref, taps_ref, more_ref, first)


def second_gate(k, v, q, taps, begun, first, width):
    return pl.pallas_call(
        functools.partial(second_gate_kernel, first),
        in_specs=[VMEM] * 5,
        out_specs=[VMEM] * 2,
        out_shape=[
            jax.ShapeDtypeStruct(begun.shape, BF16),
            jax.ShapeDtypeStruct((k.shape[0], width), BF16),
        ],
        compiler_params=params(12),
        cost_estimate=COST,
        name="gate_second",
    )(k, v, q, taps, begun)


def gate_kernel(firsts, k_ref, v_ref, q_ref, taps_ref, h_ref, _, turned_ref, mask_ref, *out_refs):
    for first, out_ref in zip(firsts, out_refs):
        gate_block(k_ref, v_ref, q_ref, taps_ref, out_ref, first)
    turned_ref[...] = turned_filters(h_ref[...])
    fill_mask(mask_ref)


def gate(k, v, q, taps, h, after, firsts, widths):
    rows = k.shape[0]
    return pl.pallas_call(
        functools.partial(gate_kernel, firsts),
        in_specs=[VMEM] * 5 + [pl.BlockSpec(memory_space=pl.ANY)],
        out_specs=[VMEM] * (len(widths) + 2),
        out_shape=[jax.ShapeDtypeStruct(h.shape, F32), jax.ShapeDtypeStruct((2 * rows // WINDOWS, 2 * FILT), BF16)]
        + [jax.ShapeDtypeStruct((rows, w), BF16) for w in widths],
        compiler_params=params(12),
        cost_estimate=COST,
        name="gate",
    )(k, v, q, taps, h, after)


def settle_kernel(in_ref, out_ref):
    out_ref[...] = in_ref[...]


def settle(x):
    return pl.pallas_call(
        settle_kernel,
        in_specs=[VMEM],
        out_specs=VMEM,
        out_shape=jax.ShapeDtypeStruct(x.shape, x.dtype),
        compiler_params=params(12),
        cost_estimate=COST,
        name="settle",
    )(x)


def last_gate_kernel(k_ref, v_ref, taps_ref, crossed_ref, near_ref, own_ref, out_ref, edge_ref, got_ref):
    rows, width = own_ref.shape
    full = k_ref.shape[1]
    wide = got_ref.shape[1]
    iota = rows_iota((SUB, LANES))
    got_ref[...] = crossed_ref[...] + near_ref[...]

    for b in range(pl.cdiv(full, wide)):
        low = 2 * (FEAT - 1) * b
        count = min(wide, full - b * wide) // LANES

        @pl.loop(0, count, unroll=2)
        def _(c):
            rim = got_ref[rows:, lanes_at(c)].astype(F32)
            at = lanes_at(c + b * (wide // LANES))
            feats = []
            for i, ref in ((0, k_ref), (1, v_ref)):
                moved = pltpu.roll(rim, (SUB - (FEAT - 1) * (i + 1) - low) % SUB, 0)
                x = jnp.where(iota >= SUB - (FEAT - 1), moved, ref[:SUB, at].astype(F32))
                feats.append(feature(x, taps_ref[i + 1, :, at]))
            edge_ref[:, at] = (feats[0] * feats[1]).astype(BF16)

    extra = out_ref.shape[0] - rows

    @pl.loop(0, width // LANES)
    def _(c):
        out_ref[:rows, lanes_at(c)] = own_ref[:, lanes_at(c)]
        tail = jnp.zeros((extra, LANES), F32)
        for b in range(pl.cdiv(full, width)):
            at = lanes_at(lax.rem(c + b * (width // LANES), full // LANES))
            one = jnp.broadcast_to(edge_ref[:, at].astype(F32)[1:2], (extra, LANES))
            tail = jnp.where(rows_iota((extra, LANES)) == b, one, tail)
        out_ref[rows:, lanes_at(c)] = tail.astype(BF16)


def last_gate(k, v, taps, crossed, near, own):
    rows, width = own.shape
    full = k.shape[1]
    extra = pl.cdiv(pl.cdiv(full, width), 8) * 8
    return pl.pallas_call(
        last_gate_kernel,
        in_specs=[VMEM] * 6,
        out_specs=[VMEM] * 3,
        out_shape=[
            jax.ShapeDtypeStruct((rows + extra, width), BF16),
            jax.ShapeDtypeStruct((SUB, full), BF16),
            jax.ShapeDtypeStruct(crossed.shape, BF16),
        ],
        compiler_params=params(12),
        cost_estimate=COST,
        name="gate_last",
    )(k, v, taps, crossed, near, own)


def turned_filters(h):
    i = rows_iota((FILT, FILT))
    j = lax.broadcasted_iota(jnp.int32, (FILT, FILT), 1)
    flip = (i + j == FILT) | ((i == 0) & (j == 0))
    return jnp.dot(h, flip.astype(BF16), preferred_element_type=F32)


def fill_mask(mask_ref):
    rows, cols = mask_ref.shape
    i = rows_iota((rows, cols))
    b = i // SUB * 8 + i % 8
    m = lax.broadcasted_iota(jnp.int32, (rows, cols), 1)
    mask_ref[...] = jnp.where((m > b) & (m <= b + FILT), 1.0, 0.0).astype(BF16)


def toeplitz_rows(turned, mask_ref, lhs_ref):
    span = mask_ref.shape[0] // 2
    per = LANES // GROUP_CH
    half = per // 2
    rings = []
    for g in range(per):
        row = jnp.broadcast_to(turned[g : g + 1], (span, FILT))
        rings.append(pltpu.roll(row, 0, 1, stride=1, stride_axis=0))
    low = 0
    for h in range(2):
        for r in range(span // 8):
            mask = mask_ref[r * SUB : (r + 1) * SUB]
            for g in range(h * half, (h + 1) * half, 2):
                pair = jnp.concatenate([rings[g][r * 8 : r * 8 + 8], rings[g + 1][r * 8 : r * 8 + 8]], axis=0)
                pair = pair.astype(BF16)
                lhs_ref[low : low + SUB, :] = jnp.concatenate([pair, pair], axis=1) * mask
                low += SUB


def own_feature(q, taps):
    iota = rows_iota((SUB, LANES))
    total = taps[0:1] * q
    for d in range(1, FEAT):
        moved = pltpu.roll(q, d, 0)
        head = jnp.where(iota < d, 0.0, moved[:SUB])
        total = total + taps[d : d + 1] * jnp.concatenate([head, moved[SUB:]], axis=0)
    return total


def prepare_kernel(firsts, turned_ref, mask_ref, q_ref, taps_ref, *out_refs):
    per = LANES // GROUP_CH
    for i, first in enumerate(firsts):
        lhs_ref, feat_ref = out_refs[2 * i : 2 * i + 2]
        tiles = lhs_ref.shape[0]

        @pl.loop(0, tiles, unroll=run_of(tiles, 4))
        def _(c):
            c_all = c + first // LANES
            src = lanes_at(c_all)
            toeplitz_rows(turned_ref[pl.ds(pl.multiple_of(c_all * per, per), per), :], mask_ref, lhs_ref.at[c])
            feat_ref[:, lanes_at(c)] = own_feature(q_ref[:, src].astype(F32), taps_ref[0, :, src])


def prepare(turned, mask, q, taps, firsts, widths):
    rows = q.shape[0]
    lhs = LANES // GROUP_CH * rows // WINDOWS
    return pl.pallas_call(
        functools.partial(prepare_kernel, firsts),
        in_specs=[VMEM] * 4,
        out_specs=[VMEM] * (2 * len(widths)),
        out_shape=[
            shape
            for w in widths
            for shape in (
                jax.ShapeDtypeStruct((w // LANES, lhs, 2 * FILT), BF16),
                jax.ShapeDtypeStruct((rows, w), F32),
            )
        ],
        compiler_params=params(12),
        cost_estimate=COST,
        name="prepare",
    )(turned, mask, q, taps)


def mix_tile(turned_ref, mask_ref, lhs_ref, feat_ref, own_ref, got_ref, edge_ref, q_ref, taps_ref, skip_ref, before, src, dst, c):
    rows = q_ref.shape[0]
    span = rows // WINDOWS
    per = LANES // GROUP_CH
    half = per // 2
    iota = rows_iota((SUB, LANES))
    lane_group = lax.broadcasted_iota(jnp.int32, (8, 2 * LANES), 1) % (LANES // 2) // GROUP_CH
    turned = turned_ref[pl.ds(c * per if isinstance(c, int) else pl.multiple_of(c * per, per), per), :]
    taps = taps_ref[0, :, src]
    if feat_ref is None:
        toeplitz_rows(turned, mask_ref, lhs_ref)
        q_feat = own_feature(q_ref[:, src].astype(F32), taps)
    else:
        q_feat = feat_ref[:, dst]
    own_head = jnp.where(iota < FEAT - 1, edge_ref[:, src].astype(F32), own_ref[:SUB, dst].astype(F32))
    got_head = got_ref[:SUB, dst].astype(F32)
    q_rim = got_head
    if before is None:
        got_head = jnp.where(iota < FEAT - 1, 0.0, got_head)
    else:
        got_head = jnp.where(iota < FEAT - 1, before, got_head)
    both = [got_head.astype(BF16)] + [got_ref[r : r + SUB, dst] for r in range(SUB, rows, SUB)]
    both += [own_head.astype(BF16)] + [own_ref[r : r + SUB, dst] for r in range(SUB, rows, SUB)]
    ahead = span // SUB
    count = len(both) - ahead
    sides = (slice(0, LANES // 2), slice(LANES // 2, LANES))
    halves = [
        [jnp.concatenate([both[i][:, side], both[i + ahead][:, side]], axis=1) for i in range(count)]
        for side in sides
    ]
    res = []
    for h, blocks in enumerate(halves):
        cols = [
            jnp.concatenate([blocks[min(w * ahead + i, count - 1)] for i in range(2 * FILT // SUB)], axis=0)
            for w in range(0, WINDOWS, 2)
        ]
        lhs = lhs_ref[h * half * span : (h + 1) * half * span, :]
        res.append(jnp.dot(lhs, jnp.concatenate(cols, axis=1), preferred_element_type=F32))
    parts = [[] for _ in range(WINDOWS)]
    for r in range(span // 8):
        totals = []
        for x in res:
            total = x[r * half * 8 : r * half * 8 + 8]
            for g in range(1, half):
                at = (r * half + g) * 8
                total = jnp.where(lane_group == g, x[at : at + 8], total)
            totals.append(total)
        for w in range(0, WINDOWS, 2):
            a, b = (t[:, w // 2 * LANES : (w // 2 + 1) * LANES] for t in totals)
            for i, side in enumerate(sides):
                parts[w + i].append(jnp.concatenate([a[:, side], b[:, side]], axis=1))
    conv = jnp.concatenate([x for part in parts for x in part], axis=0)
    cur = jnp.concatenate(both[rows // SUB :], axis=0).astype(F32)
    head = q_feat[:SUB]
    for d in range(1, FEAT):
        shifted = pltpu.roll(q_rim, (d - (FEAT - 1)) % SUB, 0)
        head = head + taps[d : d + 1] * jnp.where(iota < d, shifted, 0.0)
    q_feat = jnp.concatenate([head, q_feat[SUB:]], axis=0)
    return q_feat * (conv + skip_ref[:, src] * cur), q_feat, turned


def mix_kernel(first, has_out, has_ready, has_after, turned_ref, mask_ref, own_ref, got_ref, edge_ref, q_ref, taps_ref, skip_ref, *refs):
    refs = refs[has_out + has_after :]
    feat_ref = None
    if has_ready:
        lhs_ref, feat_ref, *refs = refs
    out_hbm, head_ref, slope_ref, res_ref, *lhs, sems = refs
    lhs_ref = lhs_ref if has_ready else lhs[0]
    rows = q_ref.shape[0]
    width = res_ref.shape[1]
    per = LANES // GROUP_CH
    row_group = rows_iota((per, LANES))
    lane_group = lax.broadcasted_iota(jnp.int32, (per, LANES), 1) // GROUP_CH

    run = run_of(width // LANES)
    runs = width // LANES // run

    def store(p):
        here = pl.ds(pl.multiple_of(p * run * LANES, LANES), run * LANES)
        there = pl.ds(pl.multiple_of(first + p * run * LANES, LANES), run * LANES)
        return pltpu.make_async_copy(
            res_ref.at[:, here], out_hbm.at[pl.ds(SUB, rows - SUB), there], sems.at[p]
        )

    @pl.loop(0, runs)
    def _(p):
        for u in range(run):
            c = p * run + u
            dst = lanes_at(c)
            src = lanes_at(c + first // LANES)
            mixed, q_feat, turned = mix_tile(
                turned_ref,
                mask_ref,
                lhs_ref.at[c if has_ready else u],
                feat_ref,
                own_ref,
                got_ref,
                edge_ref,
                q_ref,
                taps_ref,
                skip_ref,
                None,
                src,
                dst,
                c + first // LANES,
            )
            res_ref[:, dst] = mixed[SUB:].astype(BF16)
            head_ref[:, dst] = mixed[:SUB]
            last_tap = jnp.where(row_group == lane_group, jnp.broadcast_to(turned[:, 1:2], (per, LANES)), 0.0)
            slope = q_feat[:8] * jnp.sum(last_tap, axis=0, keepdims=True)
            slope_ref[:, dst] = jnp.where(rows_iota((8, LANES)) == 0, slope, 0.0)
        store(p).start()

    @pl.loop(0, runs)
    def _(p):
        store(p).wait()


def mix(turned, mask, own, got, edges, q, taps, skip, out, first, ready=(), after=None):
    rows, full = q.shape
    width = own.shape[1]
    run = run_of(width // LANES)
    per = LANES // GROUP_CH
    args = [turned, mask, own, got, edges, q, taps, skip]
    in_specs = [VMEM] * len(args)
    aliases = {}
    if out is not None:
        aliases = {len(args): 0}
        in_specs.append(HBM)
        args.append(out)
    if after is not None:
        in_specs.append(pl.BlockSpec(memory_space=pl.ANY))
        args.append(after)
    in_specs += [VMEM] * len(ready)
    args += ready
    scratch = [] if ready else [pltpu.VMEM((run, per * rows // WINDOWS, 2 * FILT), BF16)]
    return pl.pallas_call(
        functools.partial(mix_kernel, first, out is not None, len(ready) > 0, after is not None),
        in_specs=in_specs,
        out_specs=[HBM, VMEM, VMEM],
        out_shape=[
            jax.ShapeDtypeStruct((rows, full), BF16),
            jax.ShapeDtypeStruct((SUB, width), F32),
            jax.ShapeDtypeStruct((8, width), F32),
        ],
        scratch_shapes=[
            pltpu.VMEM((rows - SUB, width), BF16),
            *scratch,
            pltpu.SemaphoreType.DMA((width // LANES // run,)),
        ],
        input_output_aliases=aliases,
        compiler_params=params(12),
        cost_estimate=COST,
        name="mix",
    )(*args)


def last_mix_kernel(first, parts, turned_ref, mask_ref, own_ref, got_ref, edge_ref, q_ref, taps_ref, skip_ref, *refs):
    heads, slopes = refs[:parts], refs[parts : 2 * parts]
    lhs_ref, feat_ref, _, out_hbm, res_ref, top_ref, sems = refs[2 * parts :]
    rows = q_ref.shape[0]
    tiles = res_ref.shape[1] // LANES
    mine = first // LANES
    before = [got_ref[rows:, lanes_at(c)].astype(F32) for c in range(tiles)]

    def before_at(c_all):
        return before[c_all % tiles][c_all // tiles : c_all // tiles + 1]

    c_all = 0
    for head_ref, slope_ref in zip(heads, slopes):
        for c in range(head_ref.shape[1] // LANES):
            at = lanes_at(c)
            head = head_ref[:, at]
            changed = head[:8] + slope_ref[:, at] * before_at(c_all)
            top_ref[:, lanes_at(c_all)] = jnp.concatenate([changed, head[8:]], axis=0).astype(BF16)
            c_all += 1
    top = pltpu.make_async_copy(top_ref, out_hbm.at[pl.ds(0, SUB), pl.ds(0, first)], sems.at[0])
    top.start()
    for c in range(tiles):
        dst = lanes_at(c)
        mixed, _, _ = mix_tile(
            turned_ref,
            mask_ref,
            lhs_ref.at[c],
            feat_ref,
            own_ref,
            got_ref,
            edge_ref,
            q_ref,
            taps_ref,
            skip_ref,
            before_at(c + mine),
            lanes_at(c + mine),
            dst,
            c + mine,
        )
        res_ref[:, dst] = mixed.astype(BF16)
    copy = pltpu.make_async_copy(res_ref, out_hbm.at[:, pl.ds(first, tiles * LANES)], sems.at[1])
    copy.start()
    top.wait()
    copy.wait()


def last_mix(turned, mask, own, got, edges, q, taps, skip, heads, slopes, ready, out, first):
    rows, full = q.shape
    width = own.shape[1]
    args = [turned, mask, own, got, edges, q, taps, skip, *heads, *slopes, *ready, out]
    return pl.pallas_call(
        functools.partial(last_mix_kernel, first, len(heads)),
        in_specs=[VMEM] * (len(args) - 1) + [HBM],
        out_specs=HBM,
        out_shape=jax.ShapeDtypeStruct((rows, full), BF16),
        scratch_shapes=[
            pltpu.VMEM((rows, width), BF16),
            pltpu.VMEM((SUB, first), BF16),
            pltpu.SemaphoreType.DMA((2,)),
        ],
        input_output_aliases={len(args) - 1: 0},
        compiler_params=params(12),
        cost_estimate=COST,
        name="mix_last",
    )(*args)


def shards(q_stream, k_stream, v_stream, feat_filter, long_filter, skip_gain):
    rows, width = q_stream.shape
    skip = skip_gain.reshape(1, width)
    unit = width // 32
    sizes = [10 * unit, 11 * unit, 8 * unit, 3 * unit]
    starts = [sum(sizes[:i]) for i in range(len(sizes))]
    streams = (k_stream, v_stream, q_stream, feat_filter)
    begun = first_gate(*streams, sizes[0])
    crossed = passed_along(begun, 1, 2)
    own = list(second_gate(*streams, begun, starts[1], sizes[1]))
    near = passed_along(own[0], 0, 2)
    got = [None, passed_along(own[1])]
    turned, mask, more, last = gate(*streams, long_filter, own[1], starts[2:], sizes[2:])
    own.append(more)
    got.append(passed_along(more))
    last, edges, got[0] = last_gate(k_stream, v_stream, feat_filter, settle(crossed), near, last)
    own.append(last)
    got.append(passed_along(last))
    ready = prepare(turned, mask, q_stream, feat_filter, starts[2:], sizes[2:])
    rest = (edges, q_stream, feat_filter, skip)
    out = None
    heads = []
    slopes = []
    more = ({}, {"after": ready[3]}, {"ready": ready[:2]})
    for first, a, b, m in zip(starts[:3], own, got, more):
        out, head, slope = mix(turned, mask, a, b, *rest, out, first, **m)
        heads.append(head)
        slopes.append(slope)
    return last_mix(turned, mask, own[3], got[3], *rest, heads, slopes, ready[2:], out, starts[3])


def solution(mesh):
    in_specs = (
        P(("rep", "seq"), None),
        P(("rep", "seq"), None),
        P(("rep", "seq"), None),
        P(),
        P(),
        P(),
    )
    out_specs = P(("rep", "seq"), None)
    return jax.shard_map(shards, mesh=mesh, in_specs=in_specs, out_specs=out_specs, check_vma=False)
```

```python
import functools

import jax
import jax.numpy as jnp
from jax import lax
from jax.experimental import pallas as pl
from jax.experimental.pallas import tpu as pltpu
from jax.sharding import PartitionSpec as P

GROUP_CH = 16
FILT = 128
FEAT = 3
LANES = 128
SUB = 16
WINDOWS = 4
MIB = 1 << 20
F32 = jnp.float32
BF16 = jnp.bfloat16
VMEM = pl.BlockSpec(memory_space=pltpu.VMEM)
HBM = pl.BlockSpec(memory_space=pltpu.HBM)
COST = pl.CostEstimate(flops=1000, bytes_accessed=1000, transcendentals=0)


def passed_along(shard, first=0, step=1):
    length = lax.axis_size("seq")
    return lax.ppermute(shard, "seq", [(i, i + 1) for i in range(first, length - 1, step)])


def sends_first():
    return lax.rem(lax.axis_index("seq"), 2) == 1


def feature(x, taps):
    total = taps[0:1] * x
    for j in range(1, FEAT):
        total = total + taps[j : j + 1] * pltpu.roll(x, j, 0)
    return total


def rows_iota(shape):
    return lax.broadcasted_iota(jnp.int32, shape, 0)


def lanes_at(c):
    return pl.ds(c * LANES if isinstance(c, int) else pl.multiple_of(c * LANES, LANES), LANES)


def in_hbm(x):
    return pltpu.with_memory_space_constraint(x, pltpu.HBM)


def run_of(tiles, most=10):
    return max(n for n in range(1, most + 1) if tiles % n == 0)


def params(mib):
    return pltpu.CompilerParams(vmem_limit_bytes=mib * MIB)


def gate_tile(k, v, taps, at):
    return feature(k.astype(F32), taps[1, :, at]) * feature(v.astype(F32), taps[2, :, at])


def gate_piece(k_ref, v_ref, q_tail, taps_ref, out_ref, src, dst, at):
    rows = k_ref.shape[0]
    gated = gate_tile(k_ref[:, src], v_ref[:, src], taps_ref, at)
    tail = pltpu.roll(q_tail.astype(F32), FEAT - 1, 0)
    head = jnp.where(rows_iota((SUB, LANES)) < FEAT - 1, tail, gated[:SUB])
    out_ref[:SUB, dst] = head.astype(BF16)
    out_ref[SUB:rows, dst] = gated[SUB:].astype(BF16)


def rim_rows(kt_ref, vt_ref, out_ref):
    full = kt_ref.shape[1]
    rows, width = out_ref.shape
    last = kt_ref.shape[0] - SUB
    iota = rows_iota((SUB, LANES))

    @pl.loop(0, width // LANES, unroll=2)
    def _(c):
        tail = jnp.zeros((SUB, LANES), F32)
        for b in range(pl.cdiv(full, width)):
            low = 2 * (FEAT - 1) * b
            at = lanes_at(lax.rem(c + b * (width // LANES), full // LANES))
            kt = pltpu.roll(kt_ref[last:, at].astype(F32), (low + FEAT - 1) % SUB, 0)
            vt = pltpu.roll(vt_ref[last:, at].astype(F32), (low + 2 * (FEAT - 1)) % SUB, 0)
            tail = jnp.where((iota >= low) & (iota < low + FEAT - 1), kt, tail)
            tail = jnp.where((iota >= low + FEAT - 1) & (iota < low + 2 * (FEAT - 1)), vt, tail)
        out_ref[rows - SUB :, lanes_at(c)] = tail.astype(BF16)


def first_gate_kernel(*refs):
    @pl.when(sends_first())
    def _():
        first_gate_body(*refs)


def first_gate_body(k_hbm, v_hbm, q_hbm, taps_hbm, out_ref, k_ref, v_ref, taps_ref, qt_ref, kt_ref, vt_ref, sems):
    rows, width = k_ref.shape
    run = run_of(width // LANES, 5)
    pieces = width // LANES // run
    last = pl.ds(rows - SUB, SUB)

    def load(p, ref, hbm, i):
        at = pl.ds(p * run * LANES, run * LANES)
        return pltpu.make_async_copy(hbm.at[:, at], ref.at[:, at], sems.at[2 * p + i])

    rest = [
        pltpu.make_async_copy(taps_hbm.at[:, :, pl.ds(0, width)], taps_ref, sems.at[2 * pieces]),
        pltpu.make_async_copy(q_hbm.at[last, pl.ds(0, width)], qt_ref, sems.at[2 * pieces + 1]),
        pltpu.make_async_copy(k_hbm.at[last], kt_ref, sems.at[2 * pieces + 2]),
        pltpu.make_async_copy(v_hbm.at[last], vt_ref, sems.at[2 * pieces + 3]),
    ]
    rest[0].start()
    rest[1].start()
    for p in range(pieces):
        load(p, k_ref, k_hbm, 0).start()
        load(p, v_ref, v_hbm, 1).start()
    rest[2].start()
    rest[3].start()
    rest[0].wait()
    rest[1].wait()
    for p in range(pieces):
        load(p, k_ref, k_hbm, 0).wait()
        load(p, v_ref, v_hbm, 1).wait()

        @pl.loop(0, run, unroll=run)
        def _(c):
            at = lanes_at(c + p * run)
            gate_piece(k_ref, v_ref, qt_ref[:, at], taps_ref, out_ref, at, at, at)

    rest[2].wait()
    rest[3].wait()
    rim_rows(kt_ref, vt_ref, out_ref)


def first_gate(k, v, q, taps, width):
    rows, full = k.shape
    return pl.pallas_call(
        first_gate_kernel,
        in_specs=[HBM] * 4,
        out_specs=VMEM,
        out_shape=jax.ShapeDtypeStruct((rows + SUB, width), BF16),
        scratch_shapes=[
            pltpu.VMEM((rows, width), BF16),
            pltpu.VMEM((rows, width), BF16),
            pltpu.VMEM((3, FEAT, width), F32),
            pltpu.VMEM((SUB, width), BF16),
            pltpu.VMEM((SUB, full), BF16),
            pltpu.VMEM((SUB, full), BF16),
            pltpu.SemaphoreType.DMA((2 * (width // LANES // run_of(width // LANES, 5)) + 4,)),
        ],
        compiler_params=params(12),
        cost_estimate=COST,
        name="gate_first",
    )(*(in_hbm(x) for x in (k, v, q, taps)))


def gate_block(k_ref, v_ref, q_ref, taps_ref, out_ref, first):
    rows = k_ref.shape[0]

    @pl.loop(0, out_ref.shape[1] // LANES, unroll=2)
    def _(c):
        at = lanes_at(c + first // LANES)
        gate_piece(k_ref, v_ref, q_ref[rows - SUB :, at], taps_ref, out_ref, at, lanes_at(c), at)


def second_gate_kernel(first, k_ref, v_ref, q_ref, taps_ref, begun_ref, out_ref, more_ref):
    begun = sends_first()

    @pl.when(begun)
    def _():
        out_ref[...] = begun_ref[...]

    @pl.when(jnp.logical_not(begun))
    def _():
        gate_block(k_ref, v_ref, q_ref, taps_ref, out_ref, 0)
        rim_rows(k_ref, v_ref, out_ref)

    gate_block(k_ref, v_ref, q_ref, taps_ref, more_ref, first)


def second_gate(k, v, q, taps, begun, first, width):
    return pl.pallas_call(
        functools.partial(second_gate_kernel, first),
        in_specs=[VMEM] * 5,
        out_specs=[VMEM] * 2,
        out_shape=[
            jax.ShapeDtypeStruct(begun.shape, BF16),
            jax.ShapeDtypeStruct((k.shape[0], width), BF16),
        ],
        compiler_params=params(12),
        cost_estimate=COST,
        name="gate_second",
    )(k, v, q, taps, begun)


def gate_kernel(firsts, k_ref, v_ref, q_ref, taps_ref, h_ref, _, turned_ref, mask_ref, *out_refs):
    for first, out_ref in zip(firsts, out_refs):
        gate_block(k_ref, v_ref, q_ref, taps_ref, out_ref, first)
    turned_ref[...] = turned_filters(h_ref[...])
    fill_mask(mask_ref)


def gate(k, v, q, taps, h, after, firsts, widths):
    rows = k.shape[0]
    return pl.pallas_call(
        functools.partial(gate_kernel, firsts),
        in_specs=[VMEM] * 5 + [pl.BlockSpec(memory_space=pl.ANY)],
        out_specs=[VMEM] * (len(widths) + 2),
        out_shape=[jax.ShapeDtypeStruct(h.shape, F32), jax.ShapeDtypeStruct((2 * rows // WINDOWS, 2 * FILT), BF16)]
        + [jax.ShapeDtypeStruct((rows, w), BF16) for w in widths],
        compiler_params=params(12),
        cost_estimate=COST,
        name="gate",
    )(k, v, q, taps, h, after)


def settle_kernel(in_ref, out_ref):
    out_ref[...] = in_ref[...]


def settle(x):
    return pl.pallas_call(
        settle_kernel,
        in_specs=[VMEM],
        out_specs=VMEM,
        out_shape=jax.ShapeDtypeStruct(x.shape, x.dtype),
        compiler_params=params(12),
        cost_estimate=COST,
        name="settle",
    )(x)


def last_gate_kernel(k_ref, v_ref, taps_ref, crossed_ref, near_ref, own_ref, out_ref, edge_ref, got_ref):
    rows, width = own_ref.shape
    full = k_ref.shape[1]
    wide = got_ref.shape[1]
    iota = rows_iota((SUB, LANES))
    got_ref[...] = crossed_ref[...] + near_ref[...]

    for b in range(pl.cdiv(full, wide)):
        low = 2 * (FEAT - 1) * b
        count = min(wide, full - b * wide) // LANES

        @pl.loop(0, count, unroll=2)
        def _(c):
            rim = got_ref[rows:, lanes_at(c)].astype(F32)
            at = lanes_at(c + b * (wide // LANES))
            feats = []
            for i, ref in ((0, k_ref), (1, v_ref)):
                moved = pltpu.roll(rim, (SUB - (FEAT - 1) * (i + 1) - low) % SUB, 0)
                x = jnp.where(iota >= SUB - (FEAT - 1), moved, ref[:SUB, at].astype(F32))
                feats.append(feature(x, taps_ref[i + 1, :, at]))
            edge_ref[:, at] = (feats[0] * feats[1]).astype(BF16)

    extra = out_ref.shape[0] - rows

    @pl.loop(0, width // LANES)
    def _(c):
        out_ref[:rows, lanes_at(c)] = own_ref[:, lanes_at(c)]
        tail = jnp.zeros((extra, LANES), F32)
        for b in range(pl.cdiv(full, width)):
            at = lanes_at(lax.rem(c + b * (width // LANES), full // LANES))
            one = jnp.broadcast_to(edge_ref[:, at].astype(F32)[1:2], (extra, LANES))
            tail = jnp.where(rows_iota((extra, LANES)) == b, one, tail)
        out_ref[rows:, lanes_at(c)] = tail.astype(BF16)


def last_gate(k, v, taps, crossed, near, own):
    rows, width = own.shape
    full = k.shape[1]
    extra = pl.cdiv(pl.cdiv(full, width), 8) * 8
    return pl.pallas_call(
        last_gate_kernel,
        in_specs=[VMEM] * 6,
        out_specs=[VMEM] * 3,
        out_shape=[
            jax.ShapeDtypeStruct((rows + extra, width), BF16),
            jax.ShapeDtypeStruct((SUB, full), BF16),
            jax.ShapeDtypeStruct(crossed.shape, BF16),
        ],
        compiler_params=params(12),
        cost_estimate=COST,
        name="gate_last",
    )(k, v, taps, crossed, near, own)


def turned_filters(h):
    i = rows_iota((FILT, FILT))
    j = lax.broadcasted_iota(jnp.int32, (FILT, FILT), 1)
    flip = (i + j == FILT) | ((i == 0) & (j == 0))
    return jnp.dot(h, flip.astype(BF16), preferred_element_type=F32)


def fill_mask(mask_ref):
    rows, cols = mask_ref.shape
    i = rows_iota((rows, cols))
    b = i // SUB * 8 + i % 8
    m = lax.broadcasted_iota(jnp.int32, (rows, cols), 1)
    mask_ref[...] = jnp.where((m > b) & (m <= b + FILT), 1.0, 0.0).astype(BF16)


def toeplitz_rows(turned, mask_ref, lhs_ref):
    span = mask_ref.shape[0] // 2
    per = LANES // GROUP_CH
    half = per // 2
    rings = []
    for g in range(per):
        row = jnp.broadcast_to(turned[g : g + 1], (span, FILT))
        rings.append(pltpu.roll(row, 0, 1, stride=1, stride_axis=0))
    low = 0
    for h in range(2):
        for r in range(span // 8):
            mask = mask_ref[r * SUB : (r + 1) * SUB]
            for g in range(h * half, (h + 1) * half, 2):
                pair = jnp.concatenate([rings[g][r * 8 : r * 8 + 8], rings[g + 1][r * 8 : r * 8 + 8]], axis=0)
                pair = pair.astype(BF16)
                lhs_ref[low : low + SUB, :] = jnp.concatenate([pair, pair], axis=1) * mask
                low += SUB


def own_feature(q, taps):
    iota = rows_iota((SUB, LANES))
    total = taps[0:1] * q
    for d in range(1, FEAT):
        moved = pltpu.roll(q, d, 0)
        head = jnp.where(iota < d, 0.0, moved[:SUB])
        total = total + taps[d : d + 1] * jnp.concatenate([head, moved[SUB:]], axis=0)
    return total


def window_conv(lhs_ref, both, depth):
    rows = len(both) // 2 * SUB
    span = rows // WINDOWS
    half = LANES // GROUP_CH // 2
    lane_group = lax.broadcasted_iota(jnp.int32, (8, 2 * LANES), 1) % (LANES // 2) // GROUP_CH
    ahead = span // SUB
    count = len(both) - ahead
    sides = (slice(0, LANES // 2), slice(LANES // 2, LANES))
    halves = [
        [jnp.concatenate([both[i][:, side], both[i + ahead][:, side]], axis=1) for i in range(count)]
        for side in sides
    ]
    res = []
    for h, blocks in enumerate(halves):
        cols = [
            jnp.concatenate([blocks[min(w * ahead + i, count - 1)] for i in range(depth // SUB)], axis=0)
            for w in range(0, WINDOWS, 2)
        ]
        lhs = lhs_ref[h * half * span : (h + 1) * half * span, :depth]
        res.append(jnp.dot(lhs, jnp.concatenate(cols, axis=1), preferred_element_type=F32))
    parts = [[] for _ in range(WINDOWS)]
    for r in range(span // 8):
        totals = []
        for x in res:
            total = x[r * half * 8 : r * half * 8 + 8]
            for g in range(1, half):
                at = (r * half + g) * 8
                total = jnp.where(lane_group == g, x[at : at + 8], total)
            totals.append(total)
        for w in range(0, WINDOWS, 2):
            a, b = (t[:, w // 2 * LANES : (w // 2 + 1) * LANES] for t in totals)
            for i, side in enumerate(sides):
                parts[w + i].append(jnp.concatenate([a[:, side], b[:, side]], axis=1))
    return jnp.concatenate([x for part in parts for x in part], axis=0)


def prepare_kernel(firsts, turned_ref, mask_ref, q_ref, taps_ref, own_ref, edge_ref, skip_ref, *out_refs):
    part_ref = out_refs[-1]
    rows = q_ref.shape[0]
    iota = rows_iota((SUB, LANES))
    per = LANES // GROUP_CH
    for i, first in enumerate(firsts):
        lhs_ref, feat_ref = out_refs[2 * i : 2 * i + 2]
        tiles = lhs_ref.shape[0]

        @pl.loop(0, tiles, unroll=run_of(tiles, 4))
        def _(c):
            c_all = c + first // LANES
            src = lanes_at(c_all)
            toeplitz_rows(turned_ref[pl.ds(pl.multiple_of(c_all * per, per), per), :], mask_ref, lhs_ref.at[c])
            feat_ref[:, lanes_at(c)] = own_feature(q_ref[:, src].astype(F32), taps_ref[0, :, src])
            if i == len(firsts) - 1:
                at = lanes_at(c)
                head = jnp.where(iota < FEAT - 1, edge_ref[:, src].astype(F32), own_ref[:SUB, at].astype(F32))
                own = [head.astype(BF16)] + [own_ref[r : r + SUB, at] for r in range(SUB, rows, SUB)]
                none = [jnp.zeros((SUB, LANES), BF16)] * (rows // SUB)
                cur = jnp.concatenate(own, axis=0).astype(F32)
                part_ref[:, at] = window_conv(lhs_ref.at[c], none + own, 2 * FILT) + skip_ref[:, src] * cur


def prepare(turned, mask, q, taps, own, edges, skip, firsts, widths):
    rows = q.shape[0]
    lhs = LANES // GROUP_CH * rows // WINDOWS
    return pl.pallas_call(
        functools.partial(prepare_kernel, firsts),
        in_specs=[VMEM] * 7,
        out_specs=[VMEM] * (2 * len(widths) + 1),
        out_shape=[
            shape
            for w in widths
            for shape in (
                jax.ShapeDtypeStruct((w // LANES, lhs, 2 * FILT), BF16),
                jax.ShapeDtypeStruct((rows, w), F32),
            )
        ]
        + [jax.ShapeDtypeStruct((rows, widths[-1]), F32)],
        compiler_params=params(12),
        cost_estimate=COST,
        name="prepare",
    )(turned, mask, q, taps, own, edges, skip)


def mix_tile(turned_ref, mask_ref, lhs_ref, feat_ref, own_ref, got_ref, edge_ref, q_ref, taps_ref, skip_ref, before, src, dst, c, part_ref=None):
    rows = q_ref.shape[0]
    per = LANES // GROUP_CH
    iota = rows_iota((SUB, LANES))
    turned = turned_ref[pl.ds(c * per if isinstance(c, int) else pl.multiple_of(c * per, per), per), :]
    taps = taps_ref[0, :, src]
    if feat_ref is None:
        toeplitz_rows(turned, mask_ref, lhs_ref)
        q_feat = own_feature(q_ref[:, src].astype(F32), taps)
    else:
        q_feat = feat_ref[:, dst]
    own_head = jnp.where(iota < FEAT - 1, edge_ref[:, src].astype(F32), own_ref[:SUB, dst].astype(F32))
    got_head = got_ref[:SUB, dst].astype(F32)
    q_rim = got_head
    if before is None:
        got_head = jnp.where(iota < FEAT - 1, 0.0, got_head)
    else:
        got_head = jnp.where(iota < FEAT - 1, before, got_head)
    both = [got_head.astype(BF16)] + [got_ref[r : r + SUB, dst] for r in range(SUB, rows, SUB)]
    both += [own_head.astype(BF16)] + [own_ref[r : r + SUB, dst] for r in range(SUB, rows, SUB)]
    if part_ref is None:
        cur = jnp.concatenate(both[rows // SUB :], axis=0).astype(F32)
        summed = window_conv(lhs_ref, both, 2 * FILT) + skip_ref[:, src] * cur
    else:
        none = [jnp.zeros((SUB, LANES), BF16)] * (rows // SUB)
        summed = window_conv(lhs_ref, both[: rows // SUB] + none, FILT) + part_ref[:, dst]
    head = q_feat[:SUB]
    for d in range(1, FEAT):
        shifted = pltpu.roll(q_rim, (d - (FEAT - 1)) % SUB, 0)
        head = head + taps[d : d + 1] * jnp.where(iota < d, shifted, 0.0)
    q_feat = jnp.concatenate([head, q_feat[SUB:]], axis=0)
    return q_feat * summed, q_feat, turned


def mix_kernel(first, has_out, has_ready, has_after, turned_ref, mask_ref, own_ref, got_ref, edge_ref, q_ref, taps_ref, skip_ref, *refs):
    refs = refs[has_out + has_after :]
    feat_ref = None
    if has_ready:
        lhs_ref, feat_ref, *refs = refs
    out_hbm, head_ref, slope_ref, res_ref, *lhs, sems = refs
    lhs_ref = lhs_ref if has_ready else lhs[0]
    rows = q_ref.shape[0]
    width = res_ref.shape[1]
    per = LANES // GROUP_CH
    row_group = rows_iota((per, LANES))
    lane_group = lax.broadcasted_iota(jnp.int32, (per, LANES), 1) // GROUP_CH

    run = run_of(width // LANES)
    runs = width // LANES // run

    def store(p):
        here = pl.ds(pl.multiple_of(p * run * LANES, LANES), run * LANES)
        there = pl.ds(pl.multiple_of(first + p * run * LANES, LANES), run * LANES)
        return pltpu.make_async_copy(
            res_ref.at[:, here], out_hbm.at[pl.ds(SUB, rows - SUB), there], sems.at[p]
        )

    @pl.loop(0, runs)
    def _(p):
        for u in range(run):
            c = p * run + u
            dst = lanes_at(c)
            src = lanes_at(c + first // LANES)
            mixed, q_feat, turned = mix_tile(
                turned_ref,
                mask_ref,
                lhs_ref.at[c if has_ready else u],
                feat_ref,
                own_ref,
                got_ref,
                edge_ref,
                q_ref,
                taps_ref,
                skip_ref,
                None,
                src,
                dst,
                c + first // LANES,
            )
            res_ref[:, dst] = mixed[SUB:].astype(BF16)
            head_ref[:, dst] = mixed[:SUB]
            last_tap = jnp.where(row_group == lane_group, jnp.broadcast_to(turned[:, 1:2], (per, LANES)), 0.0)
            slope = q_feat[:8] * jnp.sum(last_tap, axis=0, keepdims=True)
            slope_ref[:, dst] = jnp.where(rows_iota((8, LANES)) == 0, slope, 0.0)
        store(p).start()

    @pl.loop(0, runs)
    def _(p):
        store(p).wait()


def mix(turned, mask, own, got, edges, q, taps, skip, out, first, ready=(), after=None):
    rows, full = q.shape
    width = own.shape[1]
    run = run_of(width // LANES)
    per = LANES // GROUP_CH
    args = [turned, mask, own, got, edges, q, taps, skip]
    in_specs = [VMEM] * len(args)
    aliases = {}
    if out is not None:
        aliases = {len(args): 0}
        in_specs.append(HBM)
        args.append(out)
    if after is not None:
        in_specs.append(pl.BlockSpec(memory_space=pl.ANY))
        args.append(after)
    in_specs += [VMEM] * len(ready)
    args += ready
    scratch = [] if ready else [pltpu.VMEM((run, per * rows // WINDOWS, 2 * FILT), BF16)]
    return pl.pallas_call(
        functools.partial(mix_kernel, first, out is not None, len(ready) > 0, after is not None),
        in_specs=in_specs,
        out_specs=[HBM, VMEM, VMEM],
        out_shape=[
            jax.ShapeDtypeStruct((rows, full), BF16),
            jax.ShapeDtypeStruct((SUB, width), F32),
            jax.ShapeDtypeStruct((8, width), F32),
        ],
        scratch_shapes=[
            pltpu.VMEM((rows - SUB, width), BF16),
            *scratch,
            pltpu.SemaphoreType.DMA((width // LANES // run,)),
        ],
        input_output_aliases=aliases,
        compiler_params=params(12),
        cost_estimate=COST,
        name="mix",
    )(*args)


def last_mix_kernel(first, parts, turned_ref, mask_ref, own_ref, got_ref, edge_ref, q_ref, taps_ref, skip_ref, *refs):
    heads, slopes = refs[:parts], refs[parts : 2 * parts]
    lhs_ref, feat_ref, part_ref, _, out_hbm, res_ref, top_ref, sems = refs[2 * parts :]
    rows = q_ref.shape[0]
    tiles = res_ref.shape[1] // LANES
    mine = first // LANES
    before = [got_ref[rows:, lanes_at(c)].astype(F32) for c in range(tiles)]

    def before_at(c_all):
        return before[c_all % tiles][c_all // tiles : c_all // tiles + 1]

    c_all = 0
    for head_ref, slope_ref in zip(heads, slopes):
        for c in range(head_ref.shape[1] // LANES):
            at = lanes_at(c)
            head = head_ref[:, at]
            changed = head[:8] + slope_ref[:, at] * before_at(c_all)
            top_ref[:, lanes_at(c_all)] = jnp.concatenate([changed, head[8:]], axis=0).astype(BF16)
            c_all += 1
    top = pltpu.make_async_copy(top_ref, out_hbm.at[pl.ds(0, SUB), pl.ds(0, first)], sems.at[0])
    top.start()
    for c in range(tiles):
        dst = lanes_at(c)
        mixed, _, _ = mix_tile(
            turned_ref,
            mask_ref,
            lhs_ref.at[c],
            feat_ref,
            own_ref,
            got_ref,
            edge_ref,
            q_ref,
            taps_ref,
            skip_ref,
            before_at(c + mine),
            lanes_at(c + mine),
            dst,
            c + mine,
            part_ref,
        )
        res_ref[:, dst] = mixed.astype(BF16)
    copy = pltpu.make_async_copy(res_ref, out_hbm.at[:, pl.ds(first, tiles * LANES)], sems.at[1])
    copy.start()
    top.wait()
    copy.wait()


def last_mix(turned, mask, own, got, edges, q, taps, skip, heads, slopes, ready, out, first):
    rows, full = q.shape
    width = own.shape[1]
    args = [turned, mask, own, got, edges, q, taps, skip, *heads, *slopes, *ready, out]
    return pl.pallas_call(
        functools.partial(last_mix_kernel, first, len(heads)),
        in_specs=[VMEM] * (len(args) - 1) + [HBM],
        out_specs=HBM,
        out_shape=jax.ShapeDtypeStruct((rows, full), BF16),
        scratch_shapes=[
            pltpu.VMEM((rows, width), BF16),
            pltpu.VMEM((SUB, first), BF16),
            pltpu.SemaphoreType.DMA((2,)),
        ],
        input_output_aliases={len(args) - 1: 0},
        compiler_params=params(12),
        cost_estimate=COST,
        name="mix_last",
    )(*args)


def shards(q_stream, k_stream, v_stream, feat_filter, long_filter, skip_gain):
    rows, width = q_stream.shape
    skip = skip_gain.reshape(1, width)
    unit = width // 32
    sizes = [9 * unit, 10 * unit, 9 * unit, 4 * unit]
    starts = [sum(sizes[:i]) for i in range(len(sizes))]
    streams = (k_stream, v_stream, q_stream, feat_filter)
    begun = first_gate(*streams, sizes[0])
    crossed = passed_along(begun, 1, 2)
    own = list(second_gate(*streams, begun, starts[1], sizes[1]))
    near = passed_along(own[0], 0, 2)
    got = [None, passed_along(own[1])]
    turned, mask, more, last = gate(*streams, long_filter, own[1], starts[2:], sizes[2:])
    own.append(more)
    got.append(passed_along(more))
    last, edges, got[0] = last_gate(k_stream, v_stream, feat_filter, settle(crossed), near, last)
    own.append(last)
    got.append(passed_along(last))
    ready = prepare(turned, mask, q_stream, feat_filter, own[3], edges, skip, starts[2:], sizes[2:])
    rest = (edges, q_stream, feat_filter, skip)
    out = None
    heads = []
    slopes = []
    more = ({}, {"after": ready[3]}, {"ready": ready[:2]})
    for first, a, b, m in zip(starts[:3], own, got, more):
        out, head, slope = mix(turned, mask, a, b, *rest, out, first, **m)
        heads.append(head)
        slopes.append(slope)
    return last_mix(turned, mask, own[3], got[3], *rest, heads, slopes, ready[2:], out, starts[3])


def solution(mesh):
    in_specs = (
        P(("rep", "seq"), None),
        P(("rep", "seq"), None),
        P(("rep", "seq"), None),
        P(),
        P(),
        P(),
    )
    out_specs = P(("rep", "seq"), None)
    return jax.shard_map(shards, mesh=mesh, in_specs=in_specs, out_specs=out_specs, check_vma=False)
```

```python
import functools

import jax
import jax.numpy as jnp
from jax import lax
from jax.experimental import pallas as pl
from jax.experimental.pallas import tpu as pltpu
from jax.sharding import PartitionSpec as P

GROUP_CH = 16
FILT = 128
FEAT = 3
LANES = 128
SUB = 16
WINDOWS = 4
MIB = 1 << 20
F32 = jnp.float32
BF16 = jnp.bfloat16
VMEM = pl.BlockSpec(memory_space=pltpu.VMEM)
HBM = pl.BlockSpec(memory_space=pltpu.HBM)
COST = pl.CostEstimate(flops=1000, bytes_accessed=1000, transcendentals=0)


def passed_along(shard, first=0, step=1):
    length = lax.axis_size("seq")
    return lax.ppermute(shard, "seq", [(i, i + 1) for i in range(first, length - 1, step)])


def sends_first():
    return lax.rem(lax.axis_index("seq"), 2) == 1


def feature(x, taps):
    total = taps[0:1] * x
    for j in range(1, FEAT):
        total = total + taps[j : j + 1] * pltpu.roll(x, j, 0)
    return total


def rows_iota(shape):
    return lax.broadcasted_iota(jnp.int32, shape, 0)


def lanes_at(c):
    return pl.ds(c * LANES if isinstance(c, int) else pl.multiple_of(c * LANES, LANES), LANES)


def in_hbm(x):
    return pltpu.with_memory_space_constraint(x, pltpu.HBM)


def run_of(tiles, most=10):
    return max(n for n in range(1, most + 1) if tiles % n == 0)


def params(mib):
    return pltpu.CompilerParams(vmem_limit_bytes=mib * MIB)


def gate_tile(k, v, taps, at):
    return feature(k.astype(F32), taps[1, :, at]) * feature(v.astype(F32), taps[2, :, at])


def gate_piece(k_ref, v_ref, q_tail, taps_ref, out_ref, src, dst, at):
    rows = k_ref.shape[0]
    gated = gate_tile(k_ref[:, src], v_ref[:, src], taps_ref, at)
    tail = pltpu.roll(q_tail.astype(F32), FEAT - 1, 0)
    head = jnp.where(rows_iota((SUB, LANES)) < FEAT - 1, tail, gated[:SUB])
    out_ref[:SUB, dst] = head.astype(BF16)
    out_ref[SUB:rows, dst] = gated[SUB:].astype(BF16)


def rim_rows(kt_ref, vt_ref, out_ref):
    full = kt_ref.shape[1]
    rows, width = out_ref.shape
    last = kt_ref.shape[0] - SUB
    iota = rows_iota((SUB, LANES))

    @pl.loop(0, width // LANES, unroll=2)
    def _(c):
        tail = jnp.zeros((SUB, LANES), F32)
        for b in range(pl.cdiv(full, width)):
            low = 2 * (FEAT - 1) * b
            at = lanes_at(lax.rem(c + b * (width // LANES), full // LANES))
            kt = pltpu.roll(kt_ref[last:, at].astype(F32), (low + FEAT - 1) % SUB, 0)
            vt = pltpu.roll(vt_ref[last:, at].astype(F32), (low + 2 * (FEAT - 1)) % SUB, 0)
            tail = jnp.where((iota >= low) & (iota < low + FEAT - 1), kt, tail)
            tail = jnp.where((iota >= low + FEAT - 1) & (iota < low + 2 * (FEAT - 1)), vt, tail)
        out_ref[rows - SUB :, lanes_at(c)] = tail.astype(BF16)


def first_gate_kernel(*refs):
    @pl.when(sends_first())
    def _():
        first_gate_body(*refs)


def first_gate_body(k_hbm, v_hbm, q_hbm, taps_hbm, out_ref, k_ref, v_ref, taps_ref, qt_ref, kt_ref, vt_ref, sems):
    rows, width = k_ref.shape
    run = run_of(width // LANES, 5)
    pieces = width // LANES // run
    last = pl.ds(rows - SUB, SUB)

    def load(p, ref, hbm, i):
        at = pl.ds(p * run * LANES, run * LANES)
        return pltpu.make_async_copy(hbm.at[:, at], ref.at[:, at], sems.at[2 * p + i])

    rest = [
        pltpu.make_async_copy(taps_hbm.at[:, :, pl.ds(0, width)], taps_ref, sems.at[2 * pieces]),
        pltpu.make_async_copy(q_hbm.at[last, pl.ds(0, width)], qt_ref, sems.at[2 * pieces + 1]),
        pltpu.make_async_copy(k_hbm.at[last], kt_ref, sems.at[2 * pieces + 2]),
        pltpu.make_async_copy(v_hbm.at[last], vt_ref, sems.at[2 * pieces + 3]),
    ]
    rest[0].start()
    rest[1].start()
    for p in range(pieces):
        load(p, k_ref, k_hbm, 0).start()
        load(p, v_ref, v_hbm, 1).start()
    rest[2].start()
    rest[3].start()
    rest[0].wait()
    rest[1].wait()
    for p in range(pieces):
        load(p, k_ref, k_hbm, 0).wait()
        load(p, v_ref, v_hbm, 1).wait()

        @pl.loop(0, run, unroll=run)
        def _(c):
            at = lanes_at(c + p * run)
            gate_piece(k_ref, v_ref, qt_ref[:, at], taps_ref, out_ref, at, at, at)

    rest[2].wait()
    rest[3].wait()
    rim_rows(kt_ref, vt_ref, out_ref)


def first_gate(k, v, q, taps, width):
    rows, full = k.shape
    return pl.pallas_call(
        first_gate_kernel,
        in_specs=[HBM] * 4,
        out_specs=VMEM,
        out_shape=jax.ShapeDtypeStruct((rows + SUB, width), BF16),
        scratch_shapes=[
            pltpu.VMEM((rows, width), BF16),
            pltpu.VMEM((rows, width), BF16),
            pltpu.VMEM((3, FEAT, width), F32),
            pltpu.VMEM((SUB, width), BF16),
            pltpu.VMEM((SUB, full), BF16),
            pltpu.VMEM((SUB, full), BF16),
            pltpu.SemaphoreType.DMA((2 * (width // LANES // run_of(width // LANES, 5)) + 4,)),
        ],
        compiler_params=params(12),
        cost_estimate=COST,
        name="gate_first",
    )(*(in_hbm(x) for x in (k, v, q, taps)))


def gate_block(k_ref, v_ref, q_ref, taps_ref, out_ref, first):
    rows = k_ref.shape[0]

    @pl.loop(0, out_ref.shape[1] // LANES, unroll=2)
    def _(c):
        at = lanes_at(c + first // LANES)
        gate_piece(k_ref, v_ref, q_ref[rows - SUB :, at], taps_ref, out_ref, at, lanes_at(c), at)


def second_gate_kernel(first, k_ref, v_ref, q_ref, taps_ref, begun_ref, out_ref, more_ref):
    begun = sends_first()

    @pl.when(begun)
    def _():
        out_ref[...] = begun_ref[...]

    @pl.when(jnp.logical_not(begun))
    def _():
        gate_block(k_ref, v_ref, q_ref, taps_ref, out_ref, 0)
        rim_rows(k_ref, v_ref, out_ref)

    gate_block(k_ref, v_ref, q_ref, taps_ref, more_ref, first)


def second_gate(k, v, q, taps, begun, first, width):
    return pl.pallas_call(
        functools.partial(second_gate_kernel, first),
        in_specs=[VMEM] * 5,
        out_specs=[VMEM] * 2,
        out_shape=[
            jax.ShapeDtypeStruct(begun.shape, BF16),
            jax.ShapeDtypeStruct((k.shape[0], width), BF16),
        ],
        compiler_params=params(12),
        cost_estimate=COST,
        name="gate_second",
    )(k, v, q, taps, begun)


def gate_kernel(firsts, k_ref, v_ref, q_ref, taps_ref, h_ref, _, turned_ref, mask_ref, *out_refs):
    for first, out_ref in zip(firsts, out_refs):
        gate_block(k_ref, v_ref, q_ref, taps_ref, out_ref, first)
    turned_ref[...] = turned_filters(h_ref[...])
    fill_mask(mask_ref)


def gate(k, v, q, taps, h, after, firsts, widths):
    rows = k.shape[0]
    return pl.pallas_call(
        functools.partial(gate_kernel, firsts),
        in_specs=[VMEM] * 5 + [pl.BlockSpec(memory_space=pl.ANY)],
        out_specs=[VMEM] * (len(widths) + 2),
        out_shape=[jax.ShapeDtypeStruct(h.shape, F32), jax.ShapeDtypeStruct((2 * rows // WINDOWS, 2 * FILT), BF16)]
        + [jax.ShapeDtypeStruct((rows, w), BF16) for w in widths],
        compiler_params=params(12),
        cost_estimate=COST,
        name="gate",
    )(k, v, q, taps, h, after)


def settle_kernel(in_ref, out_ref):
    out_ref[...] = in_ref[...]


def settle(x):
    return pl.pallas_call(
        settle_kernel,
        in_specs=[VMEM],
        out_specs=VMEM,
        out_shape=jax.ShapeDtypeStruct(x.shape, x.dtype),
        compiler_params=params(12),
        cost_estimate=COST,
        name="settle",
    )(x)


def last_gate_kernel(k_ref, v_ref, taps_ref, crossed_ref, near_ref, own_ref, out_ref, edge_ref, got_ref):
    rows, width = own_ref.shape
    full = k_ref.shape[1]
    wide = got_ref.shape[1]
    iota = rows_iota((SUB, LANES))
    got_ref[...] = crossed_ref[...] + near_ref[...]

    for b in range(pl.cdiv(full, wide)):
        low = 2 * (FEAT - 1) * b
        count = min(wide, full - b * wide) // LANES

        @pl.loop(0, count, unroll=2)
        def _(c):
            rim = got_ref[rows:, lanes_at(c)].astype(F32)
            at = lanes_at(c + b * (wide // LANES))
            feats = []
            for i, ref in ((0, k_ref), (1, v_ref)):
                moved = pltpu.roll(rim, (SUB - (FEAT - 1) * (i + 1) - low) % SUB, 0)
                x = jnp.where(iota >= SUB - (FEAT - 1), moved, ref[:SUB, at].astype(F32))
                feats.append(feature(x, taps_ref[i + 1, :, at]))
            edge_ref[:, at] = (feats[0] * feats[1]).astype(BF16)

    extra = out_ref.shape[0] - rows

    @pl.loop(0, width // LANES)
    def _(c):
        out_ref[:rows, lanes_at(c)] = own_ref[:, lanes_at(c)]
        tail = jnp.zeros((extra, LANES), F32)
        for b in range(pl.cdiv(full, width)):
            at = lanes_at(lax.rem(c + b * (width // LANES), full // LANES))
            one = jnp.broadcast_to(edge_ref[:, at].astype(F32)[1:2], (extra, LANES))
            tail = jnp.where(rows_iota((extra, LANES)) == b, one, tail)
        out_ref[rows:, lanes_at(c)] = tail.astype(BF16)


def last_gate(k, v, taps, crossed, near, own):
    rows, width = own.shape
    full = k.shape[1]
    extra = pl.cdiv(pl.cdiv(full, width), 8) * 8
    return pl.pallas_call(
        last_gate_kernel,
        in_specs=[VMEM] * 6,
        out_specs=[VMEM] * 3,
        out_shape=[
            jax.ShapeDtypeStruct((rows + extra, width), BF16),
            jax.ShapeDtypeStruct((SUB, full), BF16),
            jax.ShapeDtypeStruct(crossed.shape, BF16),
        ],
        compiler_params=params(12),
        cost_estimate=COST,
        name="gate_last",
    )(k, v, taps, crossed, near, own)


def turned_filters(h):
    i = rows_iota((FILT, FILT))
    j = lax.broadcasted_iota(jnp.int32, (FILT, FILT), 1)
    flip = (i + j == FILT) | ((i == 0) & (j == 0))
    return jnp.dot(h, flip.astype(BF16), preferred_element_type=F32)


def fill_mask(mask_ref):
    rows, cols = mask_ref.shape
    i = rows_iota((rows, cols))
    b = i // SUB * 8 + i % 8
    m = lax.broadcasted_iota(jnp.int32, (rows, cols), 1)
    mask_ref[...] = jnp.where((m > b) & (m <= b + FILT), 1.0, 0.0).astype(BF16)


def toeplitz_rows(turned, mask_ref, lhs_ref):
    span = mask_ref.shape[0] // 2
    per = LANES // GROUP_CH
    half = per // 2
    rings = []
    for g in range(per):
        row = jnp.broadcast_to(turned[g : g + 1], (span, FILT))
        rings.append(pltpu.roll(row, 0, 1, stride=1, stride_axis=0))
    low = 0
    for h in range(2):
        for r in range(span // 8):
            mask = mask_ref[r * SUB : (r + 1) * SUB]
            for g in range(h * half, (h + 1) * half, 2):
                pair = jnp.concatenate([rings[g][r * 8 : r * 8 + 8], rings[g + 1][r * 8 : r * 8 + 8]], axis=0)
                pair = pair.astype(BF16)
                lhs_ref[low : low + SUB, :] = jnp.concatenate([pair, pair], axis=1) * mask
                low += SUB


def own_feature(q, taps):
    iota = rows_iota((SUB, LANES))
    total = taps[0:1] * q
    for d in range(1, FEAT):
        moved = pltpu.roll(q, d, 0)
        head = jnp.where(iota < d, 0.0, moved[:SUB])
        total = total + taps[d : d + 1] * jnp.concatenate([head, moved[SUB:]], axis=0)
    return total


def window_conv(lhs_ref, both, depth):
    rows = len(both) // 2 * SUB
    span = rows // WINDOWS
    half = LANES // GROUP_CH // 2
    lane_group = lax.broadcasted_iota(jnp.int32, (8, 2 * LANES), 1) % (LANES // 2) // GROUP_CH
    ahead = span // SUB
    count = len(both) - ahead
    sides = (slice(0, LANES // 2), slice(LANES // 2, LANES))
    halves = [
        [jnp.concatenate([both[i][:, side], both[i + ahead][:, side]], axis=1) for i in range(count)]
        for side in sides
    ]
    res = []
    for h, blocks in enumerate(halves):
        cols = [
            jnp.concatenate([blocks[min(w * ahead + i, count - 1)] for i in range(depth // SUB)], axis=0)
            for w in range(0, WINDOWS, 2)
        ]
        lhs = lhs_ref[h * half * span : (h + 1) * half * span, :depth]
        res.append(jnp.dot(lhs, jnp.concatenate(cols, axis=1), preferred_element_type=F32))
    parts = [[] for _ in range(WINDOWS)]
    for r in range(span // 8):
        totals = []
        for x in res:
            total = x[r * half * 8 : r * half * 8 + 8]
            for g in range(1, half):
                at = (r * half + g) * 8
                total = jnp.where(lane_group == g, x[at : at + 8], total)
            totals.append(total)
        for w in range(0, WINDOWS, 2):
            a, b = (t[:, w // 2 * LANES : (w // 2 + 1) * LANES] for t in totals)
            for i, side in enumerate(sides):
                parts[w + i].append(jnp.concatenate([a[:, side], b[:, side]], axis=1))
    return jnp.concatenate([x for part in parts for x in part], axis=0)


def prepare_kernel(firsts, turned_ref, mask_ref, q_ref, taps_ref, own_ref, edge_ref, skip_ref, *out_refs):
    part_ref = out_refs[-1]
    rows = q_ref.shape[0]
    iota = rows_iota((SUB, LANES))
    per = LANES // GROUP_CH
    for i, first in enumerate(firsts):
        lhs_ref, feat_ref = out_refs[2 * i : 2 * i + 2]
        tiles = lhs_ref.shape[0]

        @pl.loop(0, tiles, unroll=run_of(tiles, 4))
        def _(c):
            c_all = c + first // LANES
            src = lanes_at(c_all)
            toeplitz_rows(turned_ref[pl.ds(pl.multiple_of(c_all * per, per), per), :], mask_ref, lhs_ref.at[c])
            feat_ref[:, lanes_at(c)] = own_feature(q_ref[:, src].astype(F32), taps_ref[0, :, src])
            if i == len(firsts) - 1:
                at = lanes_at(c)
                head = jnp.where(iota < FEAT - 1, edge_ref[:, src].astype(F32), own_ref[:SUB, at].astype(F32))
                own = [head.astype(BF16)] + [own_ref[r : r + SUB, at] for r in range(SUB, rows, SUB)]
                none = [jnp.zeros((SUB, LANES), BF16)] * (rows // SUB)
                cur = jnp.concatenate(own, axis=0).astype(F32)
                part_ref[:, at] = window_conv(lhs_ref.at[c], none + own, 2 * FILT) + skip_ref[:, src] * cur


def prepare(turned, mask, q, taps, own, edges, skip, firsts, widths):
    rows = q.shape[0]
    lhs = LANES // GROUP_CH * rows // WINDOWS
    return pl.pallas_call(
        functools.partial(prepare_kernel, firsts),
        in_specs=[VMEM] * 7,
        out_specs=[VMEM] * (2 * len(widths) + 1),
        out_shape=[
            shape
            for w in widths
            for shape in (
                jax.ShapeDtypeStruct((w // LANES, lhs, 2 * FILT), BF16),
                jax.ShapeDtypeStruct((rows, w), F32),
            )
        ]
        + [jax.ShapeDtypeStruct((rows, widths[-1]), F32)],
        compiler_params=params(12),
        cost_estimate=COST,
        name="prepare",
    )(turned, mask, q, taps, own, edges, skip)


def mix_tile(turned_ref, mask_ref, lhs_ref, feat_ref, own_ref, got_ref, edge_ref, q_ref, taps_ref, skip_ref, before, src, dst, c, part_ref=None):
    rows = q_ref.shape[0]
    per = LANES // GROUP_CH
    iota = rows_iota((SUB, LANES))
    turned = turned_ref[pl.ds(c * per if isinstance(c, int) else pl.multiple_of(c * per, per), per), :]
    taps = taps_ref[0, :, src]
    if feat_ref is None:
        toeplitz_rows(turned, mask_ref, lhs_ref)
        q_feat = own_feature(q_ref[:, src].astype(F32), taps)
    else:
        q_feat = feat_ref[:, dst]
    own_head = jnp.where(iota < FEAT - 1, edge_ref[:, src].astype(F32), own_ref[:SUB, dst].astype(F32))
    got_head = got_ref[:SUB, dst].astype(F32)
    q_rim = got_head
    if before is None:
        got_head = jnp.where(iota < FEAT - 1, 0.0, got_head)
    else:
        got_head = jnp.where(iota < FEAT - 1, before, got_head)
    both = [got_head.astype(BF16)] + [got_ref[r : r + SUB, dst] for r in range(SUB, rows, SUB)]
    both += [own_head.astype(BF16)] + [own_ref[r : r + SUB, dst] for r in range(SUB, rows, SUB)]
    if part_ref is None:
        cur = jnp.concatenate(both[rows // SUB :], axis=0).astype(F32)
        summed = window_conv(lhs_ref, both, 2 * FILT) + skip_ref[:, src] * cur
    else:
        none = [jnp.zeros((SUB, LANES), BF16)] * (rows // SUB)
        summed = window_conv(lhs_ref, both[: rows // SUB] + none, FILT) + part_ref[:, dst]
    head = q_feat[:SUB]
    for d in range(1, FEAT):
        shifted = pltpu.roll(q_rim, (d - (FEAT - 1)) % SUB, 0)
        head = head + taps[d : d + 1] * jnp.where(iota < d, shifted, 0.0)
    q_feat = jnp.concatenate([head, q_feat[SUB:]], axis=0)
    return q_feat * summed, q_feat, turned


def mix_kernel(first, has_out, has_ready, has_after, turned_ref, mask_ref, own_ref, got_ref, edge_ref, q_ref, taps_ref, skip_ref, *refs):
    refs = refs[has_out + has_after :]
    feat_ref = None
    if has_ready:
        lhs_ref, feat_ref, *refs = refs
    out_hbm, head_ref, slope_ref, res_ref, *lhs, sems = refs
    lhs_ref = lhs_ref if has_ready else lhs[0]
    rows = q_ref.shape[0]
    width = res_ref.shape[1]
    per = LANES // GROUP_CH
    row_group = rows_iota((per, LANES))
    lane_group = lax.broadcasted_iota(jnp.int32, (per, LANES), 1) // GROUP_CH

    run = run_of(width // LANES)
    runs = width // LANES // run

    def store(p):
        here = pl.ds(pl.multiple_of(p * run * LANES, LANES), run * LANES)
        there = pl.ds(pl.multiple_of(first + p * run * LANES, LANES), run * LANES)
        return pltpu.make_async_copy(
            res_ref.at[:, here], out_hbm.at[pl.ds(SUB, rows - SUB), there], sems.at[p]
        )

    @pl.loop(0, runs)
    def _(p):
        for u in range(run):
            c = p * run + u
            dst = lanes_at(c)
            src = lanes_at(c + first // LANES)
            mixed, q_feat, turned = mix_tile(
                turned_ref,
                mask_ref,
                lhs_ref.at[c if has_ready else u],
                feat_ref,
                own_ref,
                got_ref,
                edge_ref,
                q_ref,
                taps_ref,
                skip_ref,
                None,
                src,
                dst,
                c + first // LANES,
            )
            res_ref[:, dst] = mixed[SUB:].astype(BF16)
            head_ref[:, dst] = mixed[:SUB]
            last_tap = jnp.where(row_group == lane_group, jnp.broadcast_to(turned[:, 1:2], (per, LANES)), 0.0)
            slope = q_feat[:8] * jnp.sum(last_tap, axis=0, keepdims=True)
            slope_ref[:, dst] = jnp.where(rows_iota((8, LANES)) == 0, slope, 0.0)
        store(p).start()

    @pl.loop(0, runs)
    def _(p):
        store(p).wait()


def mix(turned, mask, own, got, edges, q, taps, skip, out, first, ready=(), after=None):
    rows, full = q.shape
    width = own.shape[1]
    run = run_of(width // LANES)
    per = LANES // GROUP_CH
    args = [turned, mask, own, got, edges, q, taps, skip]
    in_specs = [VMEM] * len(args)
    aliases = {}
    if out is not None:
        aliases = {len(args): 0}
        in_specs.append(HBM)
        args.append(out)
    if after is not None:
        in_specs.append(pl.BlockSpec(memory_space=pl.ANY))
        args.append(after)
    in_specs += [VMEM] * len(ready)
    args += ready
    scratch = [] if ready else [pltpu.VMEM((run, per * rows // WINDOWS, 2 * FILT), BF16)]
    return pl.pallas_call(
        functools.partial(mix_kernel, first, out is not None, len(ready) > 0, after is not None),
        in_specs=in_specs,
        out_specs=[HBM, VMEM, VMEM],
        out_shape=[
            jax.ShapeDtypeStruct((rows, full), BF16),
            jax.ShapeDtypeStruct((SUB, width), F32),
            jax.ShapeDtypeStruct((8, width), F32),
        ],
        scratch_shapes=[
            pltpu.VMEM((rows - SUB, width), BF16),
            *scratch,
            pltpu.SemaphoreType.DMA((width // LANES // run,)),
        ],
        input_output_aliases=aliases,
        compiler_params=params(12),
        cost_estimate=COST,
        name="mix",
    )(*args)


def last_mix_kernel(first, parts, turned_ref, mask_ref, own_ref, got_ref, edge_ref, q_ref, taps_ref, skip_ref, *refs):
    heads, slopes = refs[:parts], refs[parts : 2 * parts]
    lhs_ref, feat_ref, part_ref, _, out_hbm, res_ref, top_ref, sems = refs[2 * parts :]
    rows = q_ref.shape[0]
    tiles = res_ref.shape[1] // LANES
    mine = first // LANES
    before = [got_ref[rows:, lanes_at(c)].astype(F32) for c in range(tiles)]

    def before_at(c_all):
        return before[c_all % tiles][c_all // tiles : c_all // tiles + 1]

    c_all = 0
    for head_ref, slope_ref in zip(heads, slopes):
        for c in range(head_ref.shape[1] // LANES):
            at = lanes_at(c)
            head = head_ref[:, at]
            changed = head[:8] + slope_ref[:, at] * before_at(c_all)
            top_ref[:, lanes_at(c_all)] = jnp.concatenate([changed, head[8:]], axis=0).astype(BF16)
            c_all += 1
    top = pltpu.make_async_copy(top_ref, out_hbm.at[pl.ds(0, SUB), pl.ds(0, first)], sems.at[0])
    top.start()
    for c in range(tiles):
        dst = lanes_at(c)
        mixed, _, _ = mix_tile(
            turned_ref,
            mask_ref,
            lhs_ref.at[c],
            feat_ref,
            own_ref,
            got_ref,
            edge_ref,
            q_ref,
            taps_ref,
            skip_ref,
            before_at(c + mine),
            lanes_at(c + mine),
            dst,
            c + mine,
            part_ref,
        )
        res_ref[:, dst] = mixed.astype(BF16)
    copy = pltpu.make_async_copy(res_ref, out_hbm.at[:, pl.ds(first, tiles * LANES)], sems.at[1])
    copy.start()
    top.wait()
    copy.wait()


def last_mix(turned, mask, own, got, edges, q, taps, skip, heads, slopes, ready, out, first):
    rows, full = q.shape
    width = own.shape[1]
    args = [turned, mask, own, got, edges, q, taps, skip, *heads, *slopes, *ready, out]
    return pl.pallas_call(
        functools.partial(last_mix_kernel, first, len(heads)),
        in_specs=[VMEM] * (len(args) - 1) + [HBM],
        out_specs=HBM,
        out_shape=jax.ShapeDtypeStruct((rows, full), BF16),
        scratch_shapes=[
            pltpu.VMEM((rows, width), BF16),
            pltpu.VMEM((SUB, first), BF16),
            pltpu.SemaphoreType.DMA((2,)),
        ],
        input_output_aliases={len(args) - 1: 0},
        compiler_params=params(12),
        cost_estimate=COST,
        name="mix_last",
    )(*args)


def shards(q_stream, k_stream, v_stream, feat_filter, long_filter, skip_gain):
    rows, width = q_stream.shape
    skip = skip_gain.reshape(1, width)
    unit = width // 32
    sizes = [9 * unit, 10 * unit, 10 * unit, 3 * unit]
    starts = [sum(sizes[:i]) for i in range(len(sizes))]
    streams = (k_stream, v_stream, q_stream, feat_filter)
    begun = first_gate(*streams, sizes[0])
    crossed = passed_along(begun, 1, 2)
    own = list(second_gate(*streams, begun, starts[1], sizes[1]))
    near = passed_along(own[0], 0, 2)
    got = [None, passed_along(own[1])]
    turned, mask, more, last = gate(*streams, long_filter, own[1], starts[2:], sizes[2:])
    own.append(more)
    got.append(passed_along(more))
    last, edges, got[0] = last_gate(k_stream, v_stream, feat_filter, settle(crossed), near, last)
    own.append(last)
    got.append(passed_along(last))
    ready = prepare(turned, mask, q_stream, feat_filter, own[3], edges, skip, starts[2:], sizes[2:])
    rest = (edges, q_stream, feat_filter, skip)
    out = None
    heads = []
    slopes = []
    more = ({}, {"after": ready[3]}, {"ready": ready[:2]})
    for first, a, b, m in zip(starts[:3], own, got, more):
        out, head, slope = mix(turned, mask, a, b, *rest, out, first, **m)
        heads.append(head)
        slopes.append(slope)
    return last_mix(turned, mask, own[3], got[3], *rest, heads, slopes, ready[2:], out, starts[3])


def solution(mesh):
    in_specs = (
        P(("rep", "seq"), None),
        P(("rep", "seq"), None),
        P(("rep", "seq"), None),
        P(),
        P(),
        P(),
    )
    out_specs = P(("rep", "seq"), None)
    return jax.shard_map(shards, mesh=mesh, in_specs=in_specs, out_specs=out_specs, check_vma=False)
```
